32 devices in a mesh: dp: 2 (over y), seq: 16 (over z, x, core).
Axes of the slice: x: 2, y: 2, z: 4, core: 2. Of those that a mesh axis runs over, the one named last changes fastest.
Arguments:
- normed: bfloat16 [2, 3072, 2560], P('dp', 'seq'), may hold values from -6 to 6
- values: bfloat16 [2, 3072, 2560], P('dp', 'seq'), may hold values from -6 to 6
- cotangent: bfloat16 [2, 3072, 2560], P('dp', 'seq'), may hold values from -0.59765625 to 0.59765625
- w_bc: bfloat16 [2560, 256], replicated, may hold values from -0.009765625 to 0.009765625
- rate_index: int32 [2, 40, 3072], P('dp', None, 'seq'), may hold values from 0 to 15, as said below
- starts: int32 [2, 3072], P('dp', 'seq'), may hold values 0 or 1
Outputs:
- grad_values: bfloat16 [2, 3072, 2560], P('dp', 'seq')
- grad_wbc: float32 [2560, 256], P(('dp', 'seq'))
The draws below stay inside these ranges and needn't reach their ends.
Inputs may be any that keep to these rules, and one draw needn't show every extreme that they name: `rate_index`: indices into the table of 16 decays.
All inputs are finite; a program needn't handle non-finite values. No bound on the sum of `starts` on one device may be relied on, other than what follows from the above.
Results may differ from the reference program's by a relative error of at most 0.0057.
Values sent between devices are 32-bit elements; how exact they have to be, the bound alone decides.
No kernel may reach another device: no remote copies, remote signals or barrier semaphores. Data moves between devices by JAX's collectives and lax.ppermute only.
A program may use at most 64 MiB of HBM per device.

```python
import jax
import jax.numpy as jnp
from jax import lax

D = 2560
H = 40
P_SIZE = 64
N = 128
RATES = 16
TOK_DEV = 192
TOKENS = 3072
PACKS = 2


def draw_rate_index(key, part):
    key_base, key_step = jax.random.split(key)
    start_level = jax.random.randint(key_base, (PACKS, H, 1), 0, RATES - 2)
    region_step = jax.random.randint(key_step, (PACKS, H, TOKENS // TOK_DEV), 0, 3)
    indices = jnp.repeat(region_step, TOK_DEV, axis=2) + start_level
    indices = jnp.minimum(indices, RATES - 1)
    first_level = jnp.where(jnp.arange(H) % 2 == 0, RATES - 1, 0)
    indices = indices.at[:, :, 0].set(jnp.broadcast_to(first_level[None, :], (PACKS, H)))
    return indices.astype(jnp.int32)


def plant(entries, stream_key, low, high):
    longest = entries.shape.index(max(entries.shape))
    spots = []
    for shift in (0, 1):
        where = [jax.random.randint(jax.random.fold_in(stream_key, axis), (), 0, length) for axis, length in enumerate(entries.shape)]
        where[longest] = (where[longest] + shift) % entries.shape[longest]
        spots.append(tuple(where))
    return entries.at[spots[0]].set(low).at[spots[1]].set(high)


def raised(array, own_key, source, target, blocks, factor):
    def block_of(axis_at):
        return (jnp.arange(array.shape[axis_at]) // (array.shape[axis_at] // blocks)).reshape((-1,) + (1,) * (array.ndim - 1 - axis_at))

    first = jax.random.permutation(own_key, blocks)[block_of(target)]
    other_side = (block_of(target) + blocks // 2) % blocks
    return jnp.where((block_of(source) == first) | (block_of(source) == other_side), factor * array, array)


def shard_levels(stream_key, extent, cuts, least, high):
    def one(position, blocks):
        draws = jax.random.uniform(jax.random.fold_in(jax.random.fold_in(stream_key, 6), position), (blocks,), jnp.float32, least / len(cuts), high / len(cuts))
        return jnp.repeat(jnp.exp(draws), extent[position] // blocks).reshape((-1,) + (1,) * (len(extent) - position - 1))

    loudness = one(*cuts[0])
    for cut in cuts[1:]:
        loudness = loudness * one(*cut)
    return loudness


def gaussian(rng, extent, deviation, reach, pieces=(), dtype=jnp.bfloat16):
    entries = jax.random.normal(rng, extent, jnp.float32) * deviation
    if len(pieces) > 0:
        entries = shard_levels(rng, extent, pieces, -0.22, 0.18) * entries
    return jnp.clip(entries, min=-reach, max=reach).astype(dtype)


def bell_draw_with(own_key, extent, scale, bound, cuts, heavy, dtype=jnp.bfloat16):
    entries = scale * jax.random.normal(own_key, extent, jnp.float32)
    if cuts:
        entries = entries * shard_levels(own_key, extent, cuts, -0.22, 0.18)
    return jnp.clip(raised(entries, jax.random.fold_in(own_key, 3), *heavy), -bound, bound).astype(dtype)


def setup_inputs(seed: int = 0) -> dict:
    seeds = jax.random.split(jax.random.key(seed), 7)
    normed = bell_draw_with(seeds[0], (PACKS, TOKENS, D), 1.0, 6.0, ((0, 2), (1, 16)), (1, 2, 16, 2.0))
    values = gaussian(seeds[1], (PACKS, TOKENS, H * P_SIZE), 1.0, 6.0, ((0, 2), (1, 16)))
    cotangent = gaussian(seeds[2], (PACKS, TOKENS, H * P_SIZE), 0.1, 0.59765625, ((0, 2), (1, 16)))
    w_bc = gaussian(seeds[3], (D, 2 * N), (D * N) ** -0.5, 0.009765625)
    rate_index = draw_rate_index(jax.random.fold_in(seeds[6], 71), 0)
    starts = plant((jax.random.randint(seeds[5], (PACKS, TOKENS), 0, 512) < 1).astype(jnp.int32), jax.random.fold_in(seeds[5], 1), 0, 1)
    return dict(normed=normed, values=values, cotangent=cotangent, w_bc=w_bc, rate_index=rate_index, starts=starts)


highest = lax.Precision.HIGHEST
block_len = 64


def rate_logs():
    ranks = jnp.arange(RATES).astype(jnp.float32)
    return -0.0001 * jnp.power(jnp.float32(500.0), ranks / (RATES - 1))


def decay_parts(logrates, flags):
    length = flags.shape[0]
    sums = jnp.cumsum(logrates, axis=1)
    segment = jnp.cumsum(flags.astype(jnp.int32))
    order = jnp.arange(length)
    inside = (segment[:, None] == segment[None, :]) & (order[:, None] >= order[None, :])
    spread = sums[:, :, None] - sums[:, None, :]
    lower_mat = jnp.where(inside[None], jnp.exp(jnp.where(inside[None], spread, 0.0)), 0.0)
    cumulative = jnp.where((segment == 0)[None, :], jnp.exp(sums), 0.0)
    end_weight = lower_mat[:, length - 1, :]
    return lower_mat, cumulative, end_weight


def span_grads(vals, bmat, cmat, cotan, lower_mat, cumulative, end_weight, before, after):
    scores = jnp.dot(cmat, bmat.T, precision=highest)
    mixed = lower_mat * scores[None]
    grad_vals = jnp.einsum('hts,thp->shp', mixed, cotan, precision=highest)
    grad_vals = grad_vals + end_weight.T[:, :, None] * jnp.einsum('sn,hnp->shp', bmat, after, precision=highest)
    paired = lower_mat * jnp.einsum('thp,shp->hts', cotan, vals, precision=highest)
    grad_b = jnp.einsum('hts,tn->sn', paired, cmat, precision=highest)
    grad_b = grad_b + jnp.einsum('hs,shp,hnp->sn', end_weight, vals, after, precision=highest)
    grad_c = jnp.einsum('hts,sn->tn', paired, bmat, precision=highest)
    grad_c = grad_c + jnp.einsum('ht,thp,hnp->tn', cumulative, cotan, before, precision=highest)
    return grad_vals, grad_b, grad_c


def one_pack(items, w_bc):
    normed, values, cotangent, rate_index, starts = items
    tokens = normed.shape[0]
    proj = jnp.dot(normed, w_bc, preferred_element_type=jnp.float32).astype(jnp.bfloat16)
    bmat = proj[:, :N].astype(jnp.float32)
    cmat = proj[:, N:].astype(jnp.float32)
    logrates = rate_logs()[rate_index]
    blocks = tokens // block_len
    vals = values.astype(jnp.float32).reshape(blocks, block_len, H, P_SIZE)
    cots = cotangent.astype(jnp.float32).reshape(blocks, block_len, H, P_SIZE)
    bparts = bmat.reshape(blocks, block_len, N)
    cparts = cmat.reshape(blocks, block_len, N)
    logparts = logrates.reshape(H, blocks, block_len).transpose(1, 0, 2)
    flagparts = starts.reshape(blocks, block_len)
    zero_state = jnp.zeros((H, N, P_SIZE), jnp.float32)

    def forward(carry, piece):
        val, bpart, logpart, flagpart = piece
        lower_mat, cumulative, end_weight = decay_parts(logpart, flagpart)
        ends = jnp.einsum('hk,kn,khp->hnp', end_weight, bpart, val, precision=highest)
        return cumulative[:, -1][:, None, None] * carry + ends, carry

    unused, befores = lax.scan(forward, zero_state, (vals, bparts, logparts, flagparts))

    def backward(carry, piece):
        val, bpart, cpart, cot, logpart, flagpart, before = piece
        lower_mat, cumulative, end_weight = decay_parts(logpart, flagpart)
        grads = span_grads(val, bpart, cpart, cot, lower_mat, cumulative, end_weight, before, carry)
        feeds = jnp.einsum('hk,kn,khp->hnp', cumulative, cpart, cot, precision=highest)
        return feeds + cumulative[:, -1][:, None, None] * carry, grads

    unused_two, (grad_vals, grad_b, grad_c) = lax.scan(backward, zero_state, (vals, bparts, cparts, cots, logparts, flagparts, befores), reverse=True)
    grad_values = grad_vals.reshape(tokens, H * P_SIZE).astype(jnp.bfloat16)
    grad_bc = jnp.concatenate([grad_b.reshape(tokens, N), grad_c.reshape(tokens, N)], axis=1).astype(jnp.bfloat16)
    weight_term = jnp.dot(normed.T, grad_bc, preferred_element_type=jnp.float32)
    return grad_values, weight_term


def reference(normed, values, cotangent, w_bc, rate_index, starts):
    grad_values, terms = lax.map(lambda items: one_pack(items, w_bc), (normed, values, cotangent, rate_index, starts))
    grad_wbc = jnp.sum(terms, axis=0) / (PACKS * TOKENS)
    return grad_values, grad_wbc
```

```python
import math

import jax
import jax.numpy as jnp
from jax import lax
from jax.experimental import pallas as pl
from jax.experimental.pallas import tpu as pltpu
from jax.sharding import PartitionSpec as P

RATES = 16
CHUNKS = 2
LANES = 128
MIB = 1024 * 1024

f32 = jnp.float32
bf16 = jnp.bfloat16
highest = lax.Precision.HIGHEST


def log_rate(index):
    return -0.0001 * jnp.exp(index.astype(f32) * (math.log(500.0) / (RATES - 1)))


def dot(lhs, rhs, over=(1, 0), precision=None):
    dims = (((over[0],), (over[1],)), ((), ()))
    return lax.dot_general(lhs, rhs, dims, precision=precision, preferred_element_type=f32)


def padded(rows):
    return -(-rows // 8) * 8


def spread(small, heads, width):
    lane = lax.broadcasted_iota(jnp.int32, (heads, width), 1) // (width // heads)
    row = lax.broadcasted_iota(jnp.int32, (heads, width), 0)
    pattern = jnp.where(lane == row, 1.0, 0.0).astype(bf16)
    high = small.astype(bf16)
    low = (small - high.astype(f32)).astype(bf16)
    return dot(high, pattern) + dot(low, pattern)


def orders(length):
    return (lax.broadcasted_iota(jnp.int32, (length, length), 0), lax.broadcasted_iota(jnp.int32, (length, length), 1))


def decay_sums(logs):
    order, other = orders(logs.shape[1])
    lower = jnp.where(other <= order, 1.0, 0.0).astype(f32)
    return dot(lower, logs, (1, 1), highest)


def segments(flags):
    order, other = orders(flags.shape[1])
    column = jnp.sum(jnp.where(other <= order, flags, 0.0), axis=1, keepdims=True)
    return column, jnp.sum(flags, axis=1, keepdims=True)


def pieces_of(array, count):
    rows = array.shape[0] // count
    return [slice(i * rows, (i + 1) * rows) for i in range(count)]


def first_body(
    place, normed_far, w_far, vals_far, cots_far, rate_far, starts_far, message, keep_f, keep_g, decays, u_out, v_out, bc_out,
    groups, normed, w_bc, vals, cots, rate, starts, small, first, second, third, fourth,
):
    heads = rate.shape[0]
    width = vals.shape[1]
    state = w_bc.shape[1] // 2
    early = [pltpu.make_async_copy(rate_far.at[0], rate, small.at[0]), pltpu.make_async_copy(starts_far, starts, small.at[1])]
    waves = []
    for source, target, sems in (
        (normed_far.at[0], normed, first), (w_far, w_bc, second), (cots_far.at[0], cots, third), (vals_far.at[0], vals, fourth),
    ):
        waves.append([
            pltpu.make_async_copy(source.at[rows], target.at[rows], sems.at[i])
            for i, rows in enumerate(pieces_of(target, sems.shape[0]))
        ])
    for copies in [early] + waves:
        for copy in copies:
            copy.start()
    for copy in early:
        copy.wait()
    logs = log_rate(rate[...])
    flags = starts[...].astype(f32)
    sums = decay_sums(logs)
    segment, last_segment = segments(flags)
    total = jnp.where(last_segment == 0.0, jnp.exp(jnp.sum(logs, axis=1, keepdims=True)), 0.0)
    total = jnp.broadcast_to(total, (heads, LANES))
    eighth = heads // 8
    for group in range(8):
        groups[group, :eighth, :] = total[group * eighth:(group + 1) * eighth]
    up = jnp.where(segment == 0.0, jnp.exp(sums), 0.0)
    down = jnp.where(segment == last_segment, jnp.exp(sums[-1:, :] - sums), 0.0)
    up_wide = spread(up, heads, width)
    down_wide = spread(down, heads, width)
    for copy in waves[0] + waves[1]:
        copy.wait()
    bc = dot(normed[...], w_bc[...]).astype(bf16)
    bc_out[...] = bc
    for copy in waves[2]:
        copy.wait()
    u_out[...] = (up_wide * cots[...].astype(f32)).astype(bf16)
    for copy in waves[3]:
        copy.wait()
    v_out[...] = (down_wide * vals[...].astype(f32)).astype(bf16)
    bmat, cmat = bc[:, :state], bc[:, state:]
    slot = groups.shape[1]
    half, part = width // 2, width // 8
    quad = quad_of(place)
    for near_set in (1, 0):
        which = lax.rem(place[0] + near_set, 2)
        columns = pl.ds(pl.multiple_of(which * half, half), half)
        forward = dot(v_out[:, columns], bmat, (0, 0))
        backward = dot(u_out[:, columns], cmat, (0, 0))
        for group in range(4):
            flip = jnp.bitwise_xor(quad, group)
            rows = slice(group * part, (group + 1) * part)
            to = pl.ds(pl.multiple_of(flip * part, part), part)
            behind = pl.ds(pl.multiple_of(half + flip * part, part), part)
            factors = groups[which * 4 + group]
            if near_set == 0:
                keep_f[to, :] = forward[rows]
                keep_g[to, :] = backward[rows]
                decays[pl.ds(pl.multiple_of(flip * slot, slot), slot), :] = factors
            else:
                message[to, :] = forward[rows]
                message[behind, :] = backward[rows]
                message[pl.ds(pl.multiple_of(2 * half + flip * slot, slot), slot), :] = factors


def local_body(place, vals, cots, rate, starts, bc_ref, grad_out, scale_out, dbc_out):
    heads, length = rate.shape
    width = vals.shape[1]
    state = bc_ref.shape[1] // 2
    flags = starts[...].astype(f32)
    sums = decay_sums(log_rate(rate[...]))
    segment, last_segment = segments(flags)
    order, other = orders(length)
    later = jnp.where(other <= order, flags, 0.0)
    reach = dot(later.astype(bf16), jnp.where(order > other, 1.0, 0.0).astype(bf16))
    inside = jnp.logical_and(order >= other, reach == 0.0)
    scale = spread(jnp.exp(sums[-1:, :] - sums), heads, width)
    lifted = (spread(jnp.exp(sums - sums[-1:, :]), heads, width) * cots[...].astype(f32)).astype(bf16)
    weighted = (scale * vals[...].astype(f32)).astype(bf16)
    bmat, cmat = bc_ref[:, :state], bc_ref[:, state:]
    paired = jnp.where(inside, dot(lifted, weighted, (1, 1)), 0.0).astype(bf16)
    scores = jnp.where(inside, dot(cmat, bmat, (1, 1)), 0.0).astype(bf16)
    grad_out[...] = scale * dot(scores, lifted, (0, 0))
    scale_out[...] = jnp.where(segment == last_segment, scale, 0.0)
    dbc_out[:, :state] = dot(paired, cmat, (0, 0))
    dbc_out[:, state:] = dot(paired, bmat)


def pick(flag, first, second):
    return jnp.where(flag, first, second)


def quad_of(place):
    return lax.rem(place[2], 2) * 2 + place[1]


def chip_body(start, size, head, place, keep_f, keep_g, decays, recv, *outs):
    rows = size * head
    base = keep_f.shape[0]
    slot = decays.shape[0] // 4
    second = place[0] == 1
    for flip, out in enumerate(outs):
        for k in range(size):
            at = flip * (base // 4) + (start + k) * head
            spot = flip * slot + start + k
            mine = decays[spot:spot + 1, :]
            theirs = recv[2 * base + spot:2 * base + spot + 1, :]
            kf, rf = keep_f[at:at + head, :], recv[at:at + head, :]
            kg, rg = keep_g[at:at + head, :], recv[base + at:base + at + head, :]
            to = slice(k * head, (k + 1) * head)
            out[to, :] = pick(second, 1.0, theirs) * kf + pick(second, mine, 1.0) * rf
            to = slice(rows + k * head, rows + (k + 1) * head)
            out[to, :] = pick(second, theirs, 1.0) * kg + pick(second, 1.0, mine) * rg
            out[2 * rows + k:2 * rows + k + 1, :] = mine * theirs


def parts(ref, size, head, k):
    rows = size * head
    return ref[k * head:(k + 1) * head, :], ref[rows + k * head:rows + (k + 1) * head, :], ref[2 * rows + k:2 * rows + k + 1, :]


def joined(mine, theirs, second):
    forward = pick(second, 1.0, theirs[2]) * mine[0] + pick(second, mine[2], 1.0) * theirs[0]
    backward = pick(second, theirs[2], 1.0) * mine[1] + pick(second, 1.0, mine[2]) * theirs[1]
    return forward, backward, mine[2] * theirs[2]


def entering(mine, theirs, second, before, behind):
    my_before = pick(second, theirs[2], 1.0) * before + pick(second, 1.0, 0.0) * theirs[0]
    their_before = pick(second, 1.0, mine[2]) * before + pick(second, 0.0, 1.0) * mine[0]
    my_behind = pick(second, 1.0, theirs[2]) * behind + pick(second, 0.0, 1.0) * theirs[1]
    their_behind = pick(second, mine[2], 1.0) * behind + pick(second, 1.0, 0.0) * mine[1]
    return (my_before, my_behind), (their_before, their_behind)


def level_bit(place, bit):
    return lax.rem(place[2] // (1 << bit), 2) == 1


def store_total(out, total, size, head, k, upper):
    rows = size * head
    if upper is None:
        out[k * head:(k + 1) * head, :] = total[0]
        out[rows + k * head:rows + (k + 1) * head, :] = total[1]
        out[2 * rows + k:2 * rows + k + 1, :] = total[2]
    else:
        out[k * head:(k + 1) * head, :] = pick(upper, total[1], total[0])


def quad_body(size, head, last, place, own, one, two, three, out):
    second, later = place[1] == 1, level_bit(place, 0)
    upper = None if last is None else level_bit(place, last)
    for k in range(size):
        here, beside, along, across = (parts(ref, size, head, k) for ref in (own, one, two, three))
        total = joined(joined(here, beside, second), joined(along, across, second), later)
        store_total(out, total, size, head, k, upper)


def join_body(size, head, bit, last, place, total, recv, out):
    upper = None if last is None else level_bit(place, last)
    for k in range(size):
        mine, theirs = parts(total, size, head, k), parts(recv, size, head, k)
        store_total(out, joined(mine, theirs, level_bit(place, bit)), size, head, k, upper)


def enter_body(chunks, head, bits, place, *refs):
    outs = refs[-4:]
    second, later, total = place[1] == 1, level_bit(place, 0), outs[0].shape[0] // 2
    each = 4 + bits - 1
    for number, (start, size) in enumerate(chunks):
        own, one, two, three, *levels, final = refs[number * each:(number + 1) * each]
        for k in range(size):
            before, behind, left, right = 0.0, 0.0, 1.0, 1.0
            for bit, recv in enumerate(levels):
                high = level_bit(place, bit + 1)
                forward, backward, decay = parts(recv, size, head, k)
                before = before + pick(high, left, 0.0) * forward
                behind = behind + pick(high, 0.0, right) * backward
                left = pick(high, left * decay, left)
                right = pick(high, right, right * decay)
            high = level_bit(place, bits - 1)
            last = final[k * head:(k + 1) * head, :]
            before = before + pick(high, left, 0.0) * last
            behind = behind + pick(high, 0.0, right) * last
            here, beside, along, across = (parts(ref, size, head, k) for ref in (own, one, two, three))
            row, other = entering(joined(here, beside, second), joined(along, across, second), later, before, behind)
            states = entering(here, beside, second, *row) + entering(along, across, second, *other)
            at = (start + k) * head
            for out, (state_before, state_behind) in zip(outs, states):
                out[at:at + head, :] = state_before
                out[total + at:total + at + head, :] = state_behind


def core_body(start, size, head, place, *refs):
    states, keep_f, keep_g, decays, recv, send, own = refs[:4], *refs[4:]
    rows = size * head
    base = keep_f.shape[0]
    slot = decays.shape[0] // 4
    second = place[0] == 1
    for flip, ref in enumerate(states):
        for k in range(size):
            at = flip * (base // 4) + (start + k) * head
            spot = flip * slot + start + k
            here = decays[spot:spot + 1, :]
            there = recv[2 * base + spot:2 * base + spot + 1, :]
            state = ref[k * head:(k + 1) * head, :]
            to = slice(flip * rows + k * head, flip * rows + (k + 1) * head)
            send[to, :] = pick(second, 1.0, here) * state + pick(second, 0.0, 1.0) * keep_f[at:at + head, :]
            own[to, :] = (pick(second, there, 1.0) * state + pick(second, 1.0, 0.0) * recv[at:at + head, :]).astype(bf16)
            state = ref[rows + k * head:rows + (k + 1) * head, :]
            to = slice((4 + flip) * rows + k * head, (4 + flip) * rows + (k + 1) * head)
            send[to, :] = pick(second, here, 1.0) * state + pick(second, 1.0, 0.0) * keep_g[at:at + head, :]
            own[to, :] = (pick(second, 1.0, there) * state + pick(second, 0.0, 1.0) * recv[base + at:base + at + head, :]).astype(bf16)


def cross_body(chunks, head, place, u_ref, v_ref, local_ref, *refs):
    count = len(chunks)
    mine, theirs = refs[:count], refs[count:2 * count]
    out, after, before = refs[2 * count:]
    group = after.shape[0] // 8
    state = after.shape[1]
    quad = quad_of(place)
    for near_set, pieces in ((0, mine), (1, theirs)):
        for (start, size), piece in zip(chunks, pieces):
            rows = size * head
            for flip in range(4):
                which = lax.rem(place[0] + near_set, 2) * 4 + jnp.bitwise_xor(quad, flip)
                to = pl.ds(pl.multiple_of(which * group + start * head, head), rows)
                before[to, :] = piece[flip * rows:(flip + 1) * rows, :].astype(bf16)
                after[to, :] = piece[(4 + flip) * rows:(5 + flip) * rows, :].astype(bf16)
    out[:, :state] = (local_ref[:, :state] + dot(v_ref[...], after[...])).astype(bf16).astype(f32)
    out[:, state:] = (local_ref[:, state:] + dot(u_ref[...], before[...])).astype(bf16).astype(f32)


def values_body(place, grad_ref, scale_ref, bc_ref, after, grad_out, done):
    done[...] = jnp.zeros_like(done)
    bmat = bc_ref[:, : after.shape[1]]
    grad_out[...] = (grad_ref[...] + scale_ref[...] * dot(bmat, after[...], (1, 1))).astype(bf16)


def block_row(quarter, position, levels, rows):
    quad, rest = position // (levels // 2), position % (levels // 2)
    level = 0
    for bit in range(levels.bit_length() - 2):
        level = level * 2 + rest % 2
        rest //= 2
    index = (quarter // 2) * (4 * levels) + (level * 2 + quad // 2) * 4 + quad % 2 * 2 + lax.rem(quarter, 2)
    return pl.multiple_of(index * rows, rows)


def turn_body(levels, rows, place, normed, own, beside, beyond, turned):
    turned[...] = normed[...].T.astype(f32)
    count = 2 * levels
    quarter = place[3] * 2 + place[0]
    half = count // 2 * rows
    for flip in range(4):
        out, base = ((own, 0), (beside, 0), (beyond, 0), (beyond, 3 * half))[flip]
        for position in range(count):
            start = block_row(jnp.bitwise_xor(quarter, flip), position, levels, rows)
            block = turned[pl.ds(start, rows), :]
            at = position * rows
            if flip == 0:
                out[at:at + rows, :] = block.astype(bf16)
            else:
                out[base + at:base + at + rows, :] = block[:, :LANES]
                tail = base + 2 * half + at % half
                lanes = slice(0, LANES // 2) if position < count // 2 else slice(LANES // 2, LANES)
                out[tail:tail + rows, lanes] = block[:, LANES:]


def stack_body(place, beside, beyond, out):
    rows = beside.shape[0]
    out[:rows, :] = beside[...]
    out[rows:, :] = beyond[rows:, :]


def unpack_body(place, own, beside, beyond, out):
    length = own.shape[1]
    total = own.shape[0]
    half = total // 2
    wide = 3 * half
    out[:, :length] = own[...]
    for index, (ref, base) in enumerate(((beside, 0), (beyond, 0), (beside, wide)), 1):
        left = index * length
        out[:, left:left + LANES] = ref[base:base + total, :].astype(bf16)
        out[:half, left + LANES:left + length] = ref[base + total:base + wide, :LANES // 2].astype(bf16)
        out[half:, left + LANES:left + length] = ref[base + total:base + wide, LANES // 2:].astype(bf16)


def weight_body(place, turned, own, one, two, three, *refs):
    outs, product = refs[:4], refs[4]
    length = own.shape[0]
    total = None
    for index, ref in enumerate((own, one, two, three)):
        term = dot(turned[:, index * length:(index + 1) * length], ref[...].astype(bf16))
        total = term if total is None else total + term
    product[...] = total
    rows = outs[0].shape[0]
    for flip, out in enumerate(outs):
        block = jnp.bitwise_xor(quad_of(place), flip)
        out[...] = product[pl.ds(pl.multiple_of(block * rows, rows), rows), :]


def halve_body(bit, place, *refs):
    terms, send, keep = refs[:-2], refs[-2], refs[-1]
    rows = keep.shape[0]
    here = lax.rem(place[2] // (1 << bit), 2)
    for which, out in ((1 - here, send), (here, keep)):
        at = pl.ds(pl.multiple_of(which * rows, rows), rows)
        total = terms[0][at, :]
        for term in terms[1:]:
            total = total + term[at, :]
        out[...] = total


def local(normed, values, cotangent, w_bc, rate_index, starts):
    hidden, vals, cots = normed[0], values[0], cotangent[0]
    rate = rate_index[0]
    length, width = vals.shape
    depth = hidden.shape[1]
    heads = rate.shape[0]
    head = width // heads
    state = w_bc.shape[1] // 2
    shards = lax.axis_size("seq")
    packs = lax.axis_size("dp")
    levels = shards // 4
    bits = levels.bit_length() - 1
    eighth = heads // 8
    slot = padded(eighth)
    base = width // 2

    def shape(rows, columns, dtype=f32):
        return jax.ShapeDtypeStruct((rows, columns), dtype)

    token = []

    def kernel(body, outs, *args, scratch=(), vmem=4, far=False, behind=()):
        count = len(args)
        after = list(token) + list(behind)
        single = not isinstance(outs, tuple)

        def run(*refs):
            spot = lax.axis_index("seq")
            place = (spot & 1, (spot >> 1) & 1, spot >> 2, lax.axis_index("dp") & 1)
            body(place, *refs[:count], *refs[count + len(after):])

        here = pl.BlockSpec(memory_space=pltpu.VMEM)
        there = pl.BlockSpec(memory_space=pltpu.HBM) if far else here
        if far:
            args = [pltpu.with_memory_space_constraint(array, pltpu.HBM) for array in args]
        result = pl.pallas_call(
            run,
            in_specs=[there] * count + [pl.BlockSpec(memory_space=pl.ANY)] * len(after),
            out_specs=here if single else (here,) * len(outs),
            out_shape=outs,
            scratch_shapes=list(scratch),
            compiler_params=pltpu.CompilerParams(vmem_limit_bytes=vmem * MIB),
            cost_estimate=pl.CostEstimate(flops=1000, bytes_accessed=1000, transcendentals=0),
        )(*args, *after)
        token[:] = [result if single else min(result, key=lambda array: array.size)]
        return result

    def bind(body, *constants):
        return lambda *refs: body(*constants, *refs)

    def swap(array, mask):
        return lax.ppermute(array, "seq", [(s, s ^ mask) for s in range(shards)])

    def swap_pack(array):
        return lax.ppermute(array, "dp", [(d, d ^ 1) for d in range(packs)])

    def swap_both(array):
        return lax.ppermute(array, ("dp", "seq"), [(d * shards + s, (d ^ 1) * shards + (s ^ 1)) for d in range(packs) for s in range(shards)])

    message, keep_f, keep_g, decays, u, v, bc = kernel(
        first_body,
        (
            shape(2 * base + 4 * slot, state), shape(base, state), shape(base, state), shape(4 * slot, state),
            shape(length, width, bf16), shape(length, width, bf16), shape(length, 2 * state, bf16),
        ),
        normed, w_bc, values, cotangent, rate_index, starts,
        scratch=[
            pltpu.VMEM((8, slot, LANES), f32), pltpu.VMEM(hidden.shape, bf16), pltpu.VMEM(w_bc.shape, bf16),
            pltpu.VMEM(vals.shape, bf16), pltpu.VMEM(cots.shape, bf16), pltpu.VMEM(rate.shape, jnp.int32),
            pltpu.VMEM(starts.shape, jnp.int32),
        ] + [pltpu.SemaphoreType.DMA((count,)) for count in (2, 4, 4, 4, 4)],
        vmem=24, far=True,
    )
    recv = swap(message, 1)

    direct = packs == 2 and depth % (packs * shards * 16) == 0 and length == 3 * LANES // 2
    rows = depth // (packs * shards)
    part = depth // 4
    wide = part + part // 2
    pack_turned = None
    if direct:
        own_turned, core_turned, message = kernel(
            bind(turn_body, levels, rows), (shape(part, length, bf16), shape(wide, LANES), shape(2 * wide, LANES)),
            hidden, scratch=[pltpu.VMEM((depth, length), f32)], vmem=16,
        )
        pack_turned = swap_pack(message)

    bounds = [-(-eighth * i // CHUNKS) for i in range(CHUNKS + 1)]
    chunks = [(a, b - a) for a, b in zip(bounds, bounds[1:])]

    def parcel(size):
        return shape(2 * size * head + padded(size), state)

    def to_quad(arrays):
        return [swap(array, flip * 2) for flip, array in enumerate(arrays, 1)]

    quads = []
    for start, size in chunks:
        waits = quads[-1][1:2] if quads else ()
        own, *sends = kernel(bind(chip_body, start, size, head), (parcel(size),) * 4, keep_f, keep_g, decays, recv, behind=waits)
        quads.append([own] + to_quad(sends))

    totals, arrived = [], [[] for unused in chunks]
    for number, ((start, size), group) in enumerate(zip(chunks, quads)):
        last = 1 if bits == 2 else None
        out = parcel(size) if last is None else shape(size * head, state)
        totals.append(kernel(bind(quad_body, size, head, last), out, *group))
        arrived[number].append(swap(totals[number], 8))
    for bit in range(1, bits - 1):
        last = bit + 1 if bit == bits - 2 else None
        for number, (start, size) in enumerate(chunks):
            out = parcel(size) if last is None else shape(size * head, state)
            totals[number] = kernel(bind(join_body, size, head, bit, last), out, totals[number], arrived[number][-1])
            arrived[number].append(swap(totals[number], 8 << bit))
    grad_local, scale, dbc_local = kernel(
        local_body, (shape(length, width), shape(length, width), shape(length, 2 * state)),
        vals, cots, rate, starts, bc, vmem=24,
    )
    if direct:
        beside = swap(kernel(stack_body, shape(2 * wide, LANES), core_turned, pack_turned, vmem=8), 1)
    pieces = [array for group, steps in zip(quads, arrived) for array in group + steps]
    enter, *sends = kernel(
        bind(enter_body, chunks, head, bits), (shape(2 * eighth * head, state),) * 4, *pieces,
    )
    send, final = kernel(
        bind(core_body, 0, eighth, head), (shape(base * 2, state), shape(base * 2, state, bf16)),
        enter, *to_quad(sends), keep_f, keep_g, decays, recv, behind=[beside] if direct else [],
    )
    core_recv = swap(send, 1)
    dbc, after = kernel(
        bind(cross_body, ((0, eighth),), head), (shape(length, 2 * state), shape(width, state, bf16)),
        u, v, dbc_local, final, core_recv, scratch=[pltpu.VMEM((width, state), bf16)], vmem=16,
    )
    portion = 1.0 / (packs * shards * length)
    if direct:
        from_pack = swap_pack(dbc)
        from_core = swap(dbc, 1)
        from_both = swap(from_pack, 1)
    grad_values, unused_done = kernel(
        values_body, (shape(length, width, bf16), shape(8, LANES)), grad_local, scale, bc, after, vmem=16,
    )
    if not direct:
        product = lax.dot_general(hidden, dbc.astype(bf16), (((0,), (0,)), ((), ())), preferred_element_type=f32)
        return (grad_values[None], lax.psum_scatter(product * portion, ("dp", "seq"), scatter_dimension=0, tiled=True))
    turned = kernel(unpack_body, shape(part, 4 * length, bf16), own_turned, beside, pack_turned, vmem=8)
    keep, *sends = kernel(
        weight_body, (shape(part // 4, 2 * state),) * 4, turned, dbc, from_core, from_pack, from_both,
        scratch=[pltpu.VMEM((part, 2 * state), f32)], vmem=16,
    )
    terms = [keep] + to_quad(sends)
    size = part // 4
    for bit in range(1, bits):
        size //= 2
        send, keep = kernel(bind(halve_body, bit), (shape(size, 2 * state), shape(size, 2 * state)), *terms)
        terms = [keep, swap(send, 4 << bit)]
    grad_wbc = (terms[0] + terms[1]) * portion
    return (grad_values[None], grad_wbc)


def solution(mesh):
    placed = (
        P("dp", "seq", None),
        P("dp", "seq", None),
        P("dp", "seq", None),
        P(),
        P("dp", None, "seq"),
        P("dp", "seq"),
    )
    return jax.shard_map(
        local,
        mesh=mesh,
        in_specs=placed,
        out_specs=(P("dp", "seq", None), P(("dp", "seq"), None)),
        check_vma=False,
    )
```

```python
import math

import jax
import jax.numpy as jnp
from jax import lax
from jax.experimental import pallas as pl
from jax.experimental.pallas import tpu as pltpu
from jax.sharding import PartitionSpec as P

RATES = 16
CHUNKS = 2
LANES = 128
MIB = 1024 * 1024

f32 = jnp.float32
bf16 = jnp.bfloat16
highest = lax.Precision.HIGHEST


def log_rate(index):
    return -0.0001 * jnp.exp(index.astype(f32) * (math.log(500.0) / (RATES - 1)))


def dot(lhs, rhs, over=(1, 0), precision=None):
    dims = (((over[0],), (over[1],)), ((), ()))
    return lax.dot_general(lhs, rhs, dims, precision=precision, preferred_element_type=f32)


def padded(rows):
    return -(-rows // 8) * 8


def spread(small, heads, width):
    lane = lax.broadcasted_iota(jnp.int32, (heads, width), 1) // (width // heads)
    row = lax.broadcasted_iota(jnp.int32, (heads, width), 0)
    pattern = jnp.where(lane == row, 1.0, 0.0).astype(bf16)
    high = small.astype(bf16)
    low = (small - high.astype(f32)).astype(bf16)
    return dot(high, pattern) + dot(low, pattern)


def orders(length):
    return (lax.broadcasted_iota(jnp.int32, (length, length), 0), lax.broadcasted_iota(jnp.int32, (length, length), 1))


def decay_sums(logs):
    order, other = orders(logs.shape[1])
    lower = jnp.where(other <= order, 1.0, 0.0).astype(f32)
    return dot(lower, logs, (1, 1), highest)


def segments(flags):
    order, other = orders(flags.shape[1])
    column = jnp.sum(jnp.where(other <= order, flags, 0.0), axis=1, keepdims=True)
    return column, jnp.sum(flags, axis=1, keepdims=True)


def pieces_of(array, count):
    rows = array.shape[0] // count
    return [slice(i * rows, (i + 1) * rows) for i in range(count)]


def first_body(
    place, normed_far, w_far, vals_far, cots_far, rate_far, starts_far, message, keep_f, keep_g, decays, u_out, v_out, bc_out,
    groups, normed, w_bc, vals, cots, rate, starts, small, first, second, third, fourth,
):
    heads = rate.shape[0]
    width = vals.shape[1]
    state = w_bc.shape[1] // 2
    early = [pltpu.make_async_copy(rate_far.at[0], rate, small.at[0]), pltpu.make_async_copy(starts_far, starts, small.at[1])]
    waves = []
    for source, target, sems in (
        (normed_far.at[0], normed, first), (w_far, w_bc, second), (cots_far.at[0], cots, third), (vals_far.at[0], vals, fourth),
    ):
        waves.append([
            pltpu.make_async_copy(source.at[rows], target.at[rows], sems.at[i])
            for i, rows in enumerate(pieces_of(target, sems.shape[0]))
        ])
    for copies in [early] + waves:
        for copy in copies:
            copy.start()
    for copy in early:
        copy.wait()
    logs = log_rate(rate[...])
    flags = starts[...].astype(f32)
    sums = decay_sums(logs)
    segment, last_segment = segments(flags)
    total = jnp.where(last_segment == 0.0, jnp.exp(jnp.sum(logs, axis=1, keepdims=True)), 0.0)
    total = jnp.broadcast_to(total, (heads, LANES))
    eighth = heads // 8
    for group in range(8):
        groups[group, :eighth, :] = total[group * eighth:(group + 1) * eighth]
    up = jnp.where(segment == 0.0, jnp.exp(sums), 0.0)
    down = jnp.where(segment == last_segment, jnp.exp(sums[-1:, :] - sums), 0.0)
    up_wide = spread(up, heads, width)
    down_wide = spread(down, heads, width)
    for copy in waves[0] + waves[1]:
        copy.wait()
    bc = dot(normed[...], w_bc[...]).astype(bf16)
    bc_out[...] = bc
    for copy in waves[2]:
        copy.wait()
    u_out[...] = (up_wide * cots[...].astype(f32)).astype(bf16)
    for copy in waves[3]:
        copy.wait()
    v_out[...] = (down_wide * vals[...].astype(f32)).astype(bf16)
    bmat, cmat = bc[:, :state], bc[:, state:]
    slot = groups.shape[1]
    half, part = width // 2, width // 8
    quad = quad_of(place)
    for near_set in (1, 0):
        which = lax.rem(place[0] + near_set, 2)
        columns = pl.ds(pl.multiple_of(which * half, half), half)
        forward = dot(v_out[:, columns], bmat, (0, 0))
        backward = dot(u_out[:, columns], cmat, (0, 0))
        for group in range(4):
            flip = jnp.bitwise_xor(quad, group)
            rows = slice(group * part, (group + 1) * part)
            to = pl.ds(pl.multiple_of(flip * part, part), part)
            behind = pl.ds(pl.multiple_of(half + flip * part, part), part)
            factors = groups[which * 4 + group]
            if near_set == 0:
                keep_f[to, :] = forward[rows]
                keep_g[to, :] = backward[rows]
                decays[pl.ds(pl.multiple_of(flip * slot, slot), slot), :] = factors
            else:
                message[to, :] = forward[rows]
                message[behind, :] = backward[rows]
                message[pl.ds(pl.multiple_of(2 * half + flip * slot, slot), slot), :] = factors


def local_body(place, vals, cots, rate, starts, bc_ref, grad_out, scale_out, dbc_out):
    heads, length = rate.shape
    width = vals.shape[1]
    state = bc_ref.shape[1] // 2
    flags = starts[...].astype(f32)
    sums = decay_sums(log_rate(rate[...]))
    segment, last_segment = segments(flags)
    order, other = orders(length)
    later = jnp.where(other <= order, flags, 0.0)
    reach = dot(later.astype(bf16), jnp.where(order > other, 1.0, 0.0).astype(bf16))
    inside = jnp.logical_and(order >= other, reach == 0.0)
    scale = spread(jnp.exp(sums[-1:, :] - sums), heads, width)
    lifted = (spread(jnp.exp(sums - sums[-1:, :]), heads, width) * cots[...].astype(f32)).astype(bf16)
    weighted = (scale * vals[...].astype(f32)).astype(bf16)
    bmat, cmat = bc_ref[:, :state], bc_ref[:, state:]
    paired = jnp.where(inside, dot(lifted, weighted, (1, 1)), 0.0).astype(bf16)
    scores = jnp.where(inside, dot(cmat, bmat, (1, 1)), 0.0).astype(bf16)
    grad_out[...] = scale * dot(scores, lifted, (0, 0))
    scale_out[...] = jnp.where(segment == last_segment, scale, 0.0)
    dbc_out[:, :state] = dot(paired, cmat, (0, 0))
    dbc_out[:, state:] = dot(paired, bmat)


def pick(flag, first, second):
    return jnp.where(flag, first, second)


def quad_of(place):
    return lax.rem(place[2], 2) * 2 + place[1]


def chip_body(start, size, head, place, keep_f, keep_g, decays, recv, *outs):
    rows = size * head
    base = keep_f.shape[0]
    slot = decays.shape[0] // 4
    second = place[0] == 1
    for flip, out in enumerate(outs):
        for k in range(size):
            at = flip * (base // 4) + (start + k) * head
            spot = flip * slot + start + k
            mine = decays[spot:spot + 1, :]
            theirs = recv[2 * base + spot:2 * base + spot + 1, :]
            kf, rf = keep_f[at:at + head, :], recv[at:at + head, :]
            kg, rg = keep_g[at:at + head, :], recv[base + at:base + at + head, :]
            to = slice(k * head, (k + 1) * head)
            out[to, :] = pick(second, 1.0, theirs) * kf + pick(second, mine, 1.0) * rf
            to = slice(rows + k * head, rows + (k + 1) * head)
            out[to, :] = pick(second, theirs, 1.0) * kg + pick(second, 1.0, mine) * rg
            out[2 * rows + k:2 * rows + k + 1, :] = mine * theirs


def parts(ref, size, head, k):
    rows = size * head
    return ref[k * head:(k + 1) * head, :], ref[rows + k * head:rows + (k + 1) * head, :], ref[2 * rows + k:2 * rows + k + 1, :]


def joined(mine, theirs, second):
    forward = pick(second, 1.0, theirs[2]) * mine[0] + pick(second, mine[2], 1.0) * theirs[0]
    backward = pick(second, theirs[2], 1.0) * mine[1] + pick(second, 1.0, mine[2]) * theirs[1]
    return forward, backward, mine[2] * theirs[2]


def entering(mine, theirs, second, before, behind):
    my_before = pick(second, theirs[2], 1.0) * before + pick(second, 1.0, 0.0) * theirs[0]
    their_before = pick(second, 1.0, mine[2]) * before + pick(second, 0.0, 1.0) * mine[0]
    my_behind = pick(second, 1.0, theirs[2]) * behind + pick(second, 0.0, 1.0) * theirs[1]
    their_behind = pick(second, mine[2], 1.0) * behind + pick(second, 1.0, 0.0) * mine[1]
    return (my_before, my_behind), (their_before, their_behind)


def level_bit(place, bit):
    return lax.rem(place[2] // (1 << bit), 2) == 1


def store_total(out, total, size, head, k, upper):
    rows = size * head
    if upper is None:
        out[k * head:(k + 1) * head, :] = total[0]
        out[rows + k * head:rows + (k + 1) * head, :] = total[1]
        out[2 * rows + k:2 * rows + k + 1, :] = total[2]
    else:
        out[k * head:(k + 1) * head, :] = pick(upper, total[1], total[0])


def quad_body(size, head, last, place, own, one, two, three, out):
    second, later = place[1] == 1, level_bit(place, 0)
    upper = None if last is None else level_bit(place, last)
    for k in range(size):
        here, beside, along, across = (parts(ref, size, head, k) for ref in (own, one, two, three))
        total = joined(joined(here, beside, second), joined(along, across, second), later)
        store_total(out, total, size, head, k, upper)


def join_body(size, head, bit, last, place, total, recv, out):
    upper = None if last is None else level_bit(place, last)
    for k in range(size):
        mine, theirs = parts(total, size, head, k), parts(recv, size, head, k)
        store_total(out, joined(mine, theirs, level_bit(place, bit)), size, head, k, upper)


def enter_body(size, head, bits, place, own, one, two, three, *refs):
    levels, final, outs = refs[:bits - 2], refs[bits - 2], refs[bits - 1:]
    rows = size * head
    second, later = place[1] == 1, level_bit(place, 0)
    for k in range(size):
        before, behind, left, right = 0.0, 0.0, 1.0, 1.0
        for bit, recv in enumerate(levels):
            high = level_bit(place, bit + 1)
            forward, backward, decay = parts(recv, size, head, k)
            before = before + pick(high, left, 0.0) * forward
            behind = behind + pick(high, 0.0, right) * backward
            left = pick(high, left * decay, left)
            right = pick(high, right, right * decay)
        high = level_bit(place, bits - 1)
        at, after = slice(k * head, (k + 1) * head), slice(rows + k * head, rows + (k + 1) * head)
        last = final[at, :]
        before = before + pick(high, left, 0.0) * last
        behind = behind + pick(high, 0.0, right) * last
        here, beside, along, across = (parts(ref, size, head, k) for ref in (own, one, two, three))
        row, other = entering(joined(here, beside, second), joined(along, across, second), later, before, behind)
        states = entering(here, beside, second, *row) + entering(along, across, second, *other)
        for out, (state_before, state_behind) in zip(outs, states):
            out[at, :] = state_before
            out[after, :] = state_behind


def core_body(chunks, head, place, *refs):
    count = 4 * len(chunks)
    keep_f, keep_g, decays, recv, send, own = refs[count:]
    base = keep_f.shape[0]
    rows = base // 4
    slot = decays.shape[0] // 4
    second = place[0] == 1
    for number, (start, size) in enumerate(chunks):
        for flip, ref in enumerate(refs[number * 4:number * 4 + 4]):
            for k in range(size):
                at = flip * rows + (start + k) * head
                spot = flip * slot + start + k
                here = decays[spot:spot + 1, :]
                there = recv[2 * base + spot:2 * base + spot + 1, :]
                state = ref[k * head:(k + 1) * head, :]
                to, got = slice(at, at + head), recv[at:at + head, :]
                send[to, :] = pick(second, 1.0, here) * state + pick(second, 0.0, 1.0) * keep_f[to, :]
                own[to, :] = (pick(second, there, 1.0) * state + pick(second, 1.0, 0.0) * got).astype(bf16)
                state = ref[(size + k) * head:(size + k + 1) * head, :]
                to, got = slice(base + at, base + at + head), recv[base + at:base + at + head, :]
                send[to, :] = pick(second, here, 1.0) * state + pick(second, 1.0, 0.0) * keep_g[at:at + head, :]
                own[to, :] = (pick(second, 1.0, there) * state + pick(second, 0.0, 1.0) * got).astype(bf16)


def cross_body(chunks, head, place, u_ref, v_ref, local_ref, *refs):
    count = len(chunks)
    mine, theirs = refs[:count], refs[count:2 * count]
    out, after, before = refs[2 * count:]
    group = after.shape[0] // 8
    state = after.shape[1]
    quad = quad_of(place)
    for near_set, pieces in ((0, mine), (1, theirs)):
        for (start, size), piece in zip(chunks, pieces):
            rows = size * head
            for flip in range(4):
                which = lax.rem(place[0] + near_set, 2) * 4 + jnp.bitwise_xor(quad, flip)
                to = pl.ds(pl.multiple_of(which * group + start * head, head), rows)
                before[to, :] = piece[flip * rows:(flip + 1) * rows, :].astype(bf16)
                after[to, :] = piece[(4 + flip) * rows:(5 + flip) * rows, :].astype(bf16)
    out[:, :state] = (local_ref[:, :state] + dot(v_ref[...], after[...])).astype(bf16).astype(f32)
    out[:, state:] = (local_ref[:, state:] + dot(u_ref[...], before[...])).astype(bf16).astype(f32)


def values_body(place, grad_ref, scale_ref, bc_ref, after, grad_out, done):
    done[...] = jnp.zeros_like(done)
    bmat = bc_ref[:, : after.shape[1]]
    grad_out[...] = (grad_ref[...] + scale_ref[...] * dot(bmat, after[...], (1, 1))).astype(bf16)


def block_row(quarter, position, levels, rows):
    quad, rest = position // (levels // 2), position % (levels // 2)
    level = 0
    for bit in range(levels.bit_length() - 2):
        level = level * 2 + rest % 2
        rest //= 2
    index = (quarter // 2) * (4 * levels) + (level * 2 + quad // 2) * 4 + quad % 2 * 2 + lax.rem(quarter, 2)
    return pl.multiple_of(index * rows, rows)


def turn_body(levels, rows, place, normed, own, beside, beyond, turned):
    turned[...] = normed[...].T.astype(f32)
    count = 2 * levels
    quarter = place[3] * 2 + place[0]
    half = count // 2 * rows
    for flip in range(4):
        out, base = ((own, 0), (beside, 0), (beyond, 0), (beyond, 3 * half))[flip]
        for position in range(count):
            start = block_row(jnp.bitwise_xor(quarter, flip), position, levels, rows)
            block = turned[pl.ds(start, rows), :]
            at = position * rows
            if flip == 0:
                out[at:at + rows, :] = block.astype(bf16)
            else:
                out[base + at:base + at + rows, :] = block[:, :LANES]
                tail = base + 2 * half + at % half
                lanes = slice(0, LANES // 2) if position < count // 2 else slice(LANES // 2, LANES)
                out[tail:tail + rows, lanes] = block[:, LANES:]


def stack_body(place, beside, beyond, out):
    rows = beside.shape[0]
    out[:rows, :] = beside[...]
    out[rows:, :] = beyond[rows:, :]


def unpack_body(place, own, beside, beyond, out):
    length = own.shape[1]
    total = own.shape[0]
    half = total // 2
    wide = 3 * half
    out[:, :length] = own[...]
    for index, (ref, base) in enumerate(((beside, 0), (beyond, 0), (beside, wide)), 1):
        left = index * length
        out[:, left:left + LANES] = ref[base:base + total, :].astype(bf16)
        out[:half, left + LANES:left + length] = ref[base + total:base + wide, :LANES // 2].astype(bf16)
        out[half:, left + LANES:left + length] = ref[base + total:base + wide, LANES // 2:].astype(bf16)


def weight_body(place, turned, own, one, two, three, *refs):
    outs, product = refs[:4], refs[4]
    length = own.shape[0]
    total = None
    for index, ref in enumerate((own, one, two, three)):
        term = dot(turned[:, index * length:(index + 1) * length], ref[...].astype(bf16))
        total = term if total is None else total + term
    product[...] = total
    rows = outs[0].shape[0]
    for flip, out in enumerate(outs):
        block = jnp.bitwise_xor(quad_of(place), flip)
        out[...] = product[pl.ds(pl.multiple_of(block * rows, rows), rows), :]


def halve_body(bit, place, *refs):
    terms, send, keep = refs[:-2], refs[-2], refs[-1]
    rows = keep.shape[0]
    here = lax.rem(place[2] // (1 << bit), 2)
    for which, out in ((1 - here, send), (here, keep)):
        at = pl.ds(pl.multiple_of(which * rows, rows), rows)
        total = terms[0][at, :]
        for term in terms[1:]:
            total = total + term[at, :]
        out[...] = total


def local(normed, values, cotangent, w_bc, rate_index, starts):
    hidden, vals, cots = normed[0], values[0], cotangent[0]
    rate = rate_index[0]
    length, width = vals.shape
    depth = hidden.shape[1]
    heads = rate.shape[0]
    head = width // heads
    state = w_bc.shape[1] // 2
    shards = lax.axis_size("seq")
    packs = lax.axis_size("dp")
    levels = shards // 4
    bits = levels.bit_length() - 1
    eighth = heads // 8
    slot = padded(eighth)
    base = width // 2

    def shape(rows, columns, dtype=f32):
        return jax.ShapeDtypeStruct((rows, columns), dtype)

    token = []

    def kernel(body, outs, *args, scratch=(), vmem=4, far=False, behind=()):
        count = len(args)
        after = list(token) + list(behind)
        single = not isinstance(outs, tuple)

        def run(*refs):
            spot = lax.axis_index("seq")
            place = (spot & 1, (spot >> 1) & 1, spot >> 2, lax.axis_index("dp") & 1)
            body(place, *refs[:count], *refs[count + len(after):])

        here = pl.BlockSpec(memory_space=pltpu.VMEM)
        there = pl.BlockSpec(memory_space=pltpu.HBM) if far else here
        if far:
            args = [pltpu.with_memory_space_constraint(array, pltpu.HBM) for array in args]
        result = pl.pallas_call(
            run,
            in_specs=[there] * count + [pl.BlockSpec(memory_space=pl.ANY)] * len(after),
            out_specs=here if single else (here,) * len(outs),
            out_shape=outs,
            scratch_shapes=list(scratch),
            compiler_params=pltpu.CompilerParams(vmem_limit_bytes=vmem * MIB),
            cost_estimate=pl.CostEstimate(flops=1000, bytes_accessed=1000, transcendentals=0),
        )(*args, *after)
        token[:] = [result if single else min(result, key=lambda array: array.size)]
        return result

    def bind(body, *constants):
        return lambda *refs: body(*constants, *refs)

    def swap(array, mask):
        return lax.ppermute(array, "seq", [(s, s ^ mask) for s in range(shards)])

    def swap_pack(array):
        return lax.ppermute(array, "dp", [(d, d ^ 1) for d in range(packs)])

    def swap_both(array):
        return lax.ppermute(array, ("dp", "seq"), [(d * shards + s, (d ^ 1) * shards + (s ^ 1)) for d in range(packs) for s in range(shards)])

    message, keep_f, keep_g, decays, u, v, bc = kernel(
        first_body,
        (
            shape(2 * base + 4 * slot, state), shape(base, state), shape(base, state), shape(4 * slot, state),
            shape(length, width, bf16), shape(length, width, bf16), shape(length, 2 * state, bf16),
        ),
        normed, w_bc, values, cotangent, rate_index, starts,
        scratch=[
            pltpu.VMEM((8, slot, LANES), f32), pltpu.VMEM(hidden.shape, bf16), pltpu.VMEM(w_bc.shape, bf16),
            pltpu.VMEM(vals.shape, bf16), pltpu.VMEM(cots.shape, bf16), pltpu.VMEM(rate.shape, jnp.int32),
            pltpu.VMEM(starts.shape, jnp.int32),
        ] + [pltpu.SemaphoreType.DMA((count,)) for count in (2, 4, 4, 4, 4)],
        vmem=24, far=True,
    )
    recv = swap(message, 1)

    direct = packs == 2 and depth % (packs * shards * 16) == 0 and length == 3 * LANES // 2
    rows = depth // (packs * shards)
    part = depth // 4
    wide = part + part // 2
    pack_turned = None
    if direct:
        own_turned, core_turned, message = kernel(
            bind(turn_body, levels, rows), (shape(part, length, bf16), shape(wide, LANES), shape(2 * wide, LANES)),
            hidden, scratch=[pltpu.VMEM((depth, length), f32)], vmem=16,
        )
        pack_turned = swap_pack(message)

    bounds = [-(-eighth * i // CHUNKS) for i in range(CHUNKS + 1)]
    chunks = [(a, b - a) for a, b in zip(bounds, bounds[1:])]

    def parcel(size):
        return shape(2 * size * head + padded(size), state)

    def to_quad(arrays):
        return [swap(array, flip * 2) for flip, array in enumerate(arrays, 1)]

    quads = []
    for start, size in chunks:
        waits = quads[-1][1:2] if quads else ()
        own, *sends = kernel(bind(chip_body, start, size, head), (parcel(size),) * 4, keep_f, keep_g, decays, recv, behind=waits)
        quads.append([own] + to_quad(sends))

    totals, arrived = [], [[] for unused in chunks]
    for number, ((start, size), group) in enumerate(zip(chunks, quads)):
        last = 1 if bits == 2 else None
        out = parcel(size) if last is None else shape(size * head, state)
        totals.append(kernel(bind(quad_body, size, head, last), out, *group))
        arrived[number].append(swap(totals[number], 8))
    for bit in range(1, bits - 1):
        last = bit + 1 if bit == bits - 2 else None
        for number, (start, size) in enumerate(chunks):
            out = parcel(size) if last is None else shape(size * head, state)
            totals[number] = kernel(bind(join_body, size, head, bit, last), out, totals[number], arrived[number][-1])
            arrived[number].append(swap(totals[number], 8 << bit))
    grad_local, scale, dbc_local = kernel(
        local_body, (shape(length, width), shape(length, width), shape(length, 2 * state)),
        vals, cots, rate, starts, bc, vmem=24,
    )
    states = []
    for number, ((start, size), group, steps) in enumerate(zip(chunks, quads, arrived)):
        waits = states[1:2] if states else ([pack_turned] if direct else [])
        enter, *sends = kernel(
            bind(enter_body, size, head, bits), (shape(2 * size * head, state),) * 4, *group, *steps, behind=waits,
        )
        states += [enter] + to_quad(sends)
    send, final = kernel(
        bind(core_body, chunks, head), (shape(2 * base, state), shape(2 * base, state, bf16)), *states, keep_f, keep_g, decays, recv,
    )
    core_recv = swap(send, 1)
    dbc, after = kernel(
        bind(cross_body, ((0, eighth),), head), (shape(length, 2 * state), shape(width, state, bf16)),
        u, v, dbc_local, final, core_recv, scratch=[pltpu.VMEM((width, state), bf16)], vmem=16,
    )
    portion = 1.0 / (packs * shards * length)
    if direct:
        from_pack = swap_pack(dbc)
        from_core = swap(dbc, 1)
        from_both = swap(from_pack, 1)
        beside = swap(kernel(stack_body, shape(2 * wide, LANES), core_turned, pack_turned, vmem=8), 1)
    grad_values, unused_done = kernel(
        values_body, (shape(length, width, bf16), shape(8, LANES)), grad_local, scale, bc, after, vmem=16,
    )
    if not direct:
        product = lax.dot_general(hidden, dbc.astype(bf16), (((0,), (0,)), ((), ())), preferred_element_type=f32)
        return (grad_values[None], lax.psum_scatter(product * portion, ("dp", "seq"), scatter_dimension=0, tiled=True))
    turned = kernel(unpack_body, shape(part, 4 * length, bf16), own_turned, beside, pack_turned, vmem=8)
    keep, *sends = kernel(
        weight_body, (shape(part // 4, 2 * state),) * 4, turned, dbc, from_core, from_pack, from_both,
        scratch=[pltpu.VMEM((part, 2 * state), f32)], vmem=16,
    )
    terms = [keep] + to_quad(sends)
    size = part // 4
    for bit in range(1, bits):
        size //= 2
        send, keep = kernel(bind(halve_body, bit), (shape(size, 2 * state), shape(size, 2 * state)), *terms)
        terms = [keep, swap(send, 4 << bit)]
    grad_wbc = (terms[0] + terms[1]) * portion
    return (grad_values[None], grad_wbc)


def solution(mesh):
    placed = (
        P("dp", "seq", None),
        P("dp", "seq", None),
        P("dp", "seq", None),
        P(),
        P("dp", None, "seq"),
        P("dp", "seq"),
    )
    return jax.shard_map(
        local,
        mesh=mesh,
        in_specs=placed,
        out_specs=(P("dp", "seq", None), P(("dp", "seq"), None)),
        check_vma=False,
    )
```

```python
import math

import jax
import jax.numpy as jnp
from jax import lax
from jax.experimental import pallas as pl
from jax.experimental.pallas import tpu as pltpu
from jax.sharding import PartitionSpec as P

RATES = 16
CHUNKS = 2
LANES = 128
MIB = 1024 * 1024

f32 = jnp.float32
bf16 = jnp.bfloat16
highest = lax.Precision.HIGHEST


def log_rate(index):
    return -0.0001 * jnp.exp(index.astype(f32) * (math.log(500.0) / (RATES - 1)))


def dot(lhs, rhs, over=(1, 0), precision=None):
    dims = (((over[0],), (over[1],)), ((), ()))
    return lax.dot_general(lhs, rhs, dims, precision=precision, preferred_element_type=f32)


def padded(rows):
    return -(-rows // 8) * 8


def spread(small, heads, width):
    lane = lax.broadcasted_iota(jnp.int32, (heads, width), 1) // (width // heads)
    row = lax.broadcasted_iota(jnp.int32, (heads, width), 0)
    pattern = jnp.where(lane == row, 1.0, 0.0).astype(bf16)
    high = small.astype(bf16).astype(f32)
    halves = jnp.concatenate([high, small - high], axis=1).astype(bf16)
    return dot(halves, jnp.concatenate([pattern, pattern], axis=0))


def orders(length):
    return (lax.broadcasted_iota(jnp.int32, (length, length), 0), lax.broadcasted_iota(jnp.int32, (length, length), 1))


def decay_sums(logs):
    order, other = orders(logs.shape[1])
    lower = jnp.where(other <= order, 1.0, 0.0).astype(f32)
    return dot(lower, logs, (1, 1), highest)


def segments(flags):
    order, other = orders(flags.shape[1])
    column = jnp.sum(jnp.where(other <= order, flags, 0.0), axis=1, keepdims=True)
    return column, jnp.sum(flags, axis=1, keepdims=True)


def pieces_of(array, count):
    rows = array.shape[0] // count
    return [slice(i * rows, (i + 1) * rows) for i in range(count)]


def first_body(
    place, normed_far, w_far, vals_far, cots_far, rate_far, starts_far, message, factors_out, u_out, v_out, bc_out,
    groups, normed, w_bc, vals, cots, rate, starts, small, first, second, third, fourth,
):
    heads = rate.shape[0]
    width = vals.shape[1]
    state = w_bc.shape[1] // 2
    early = [pltpu.make_async_copy(rate_far.at[0], rate, small.at[0]), pltpu.make_async_copy(starts_far, starts, small.at[1])]
    waves = []
    for source, target, sems in (
        (normed_far.at[0], normed, first), (w_far, w_bc, second), (cots_far.at[0], cots, third), (vals_far.at[0], vals, fourth),
    ):
        waves.append([
            pltpu.make_async_copy(source.at[rows], target.at[rows], sems.at[i])
            for i, rows in enumerate(pieces_of(target, sems.shape[0]))
        ])
    for copies in [early] + waves:
        for copy in copies:
            copy.start()
    for copy in early:
        copy.wait()
    logs = log_rate(rate[...])
    flags = starts[...].astype(f32)
    sums = decay_sums(logs)
    segment, last_segment = segments(flags)
    total = jnp.where(last_segment == 0.0, jnp.exp(jnp.sum(logs, axis=1, keepdims=True)), 0.0)
    total = jnp.broadcast_to(total, (heads, LANES))
    eighth = heads // 8
    for group in range(8):
        groups[group, :eighth, :] = total[group * eighth:(group + 1) * eighth]
    up = jnp.where(segment == 0.0, jnp.exp(sums), 0.0)
    down = jnp.where(segment == last_segment, jnp.exp(sums[-1:, :] - sums), 0.0)
    up_wide = spread(up, heads, width)
    down_wide = spread(down, heads, width)
    for copy in waves[0] + waves[1] + waves[2] + waves[3]:
        copy.wait()
    bc = dot(normed[...], w_bc[...]).astype(bf16)
    bc_out[...] = bc
    u_out[...] = (up_wide * cots[...].astype(f32)).astype(bf16)
    v_out[...] = (down_wide * vals[...].astype(f32)).astype(bf16)
    factors_out[...] = groups[...]
    half = width // 2
    end_states(place, 1, u_out, v_out, bc_out, groups, message, message, message, (0, half, 2 * half))


def end_states(place, near_set, u_ref, v_ref, bc_ref, factors, into_f, into_g, into_decays, bases):
    state = bc_ref.shape[1] // 2
    half, part, slot = u_ref.shape[1] // 2, u_ref.shape[1] // 8, factors.shape[1]
    which = lax.rem(place[0] + near_set, 2)
    columns = pl.ds(pl.multiple_of(which * half, half), half)
    quad = quad_of(place)
    forward = dot(v_ref[:, columns], bc_ref[:, :state], (0, 0))
    backward = dot(u_ref[:, columns], bc_ref[:, state:], (0, 0))
    for group in range(4):
        flip = jnp.bitwise_xor(quad, group)
        rows = slice(group * part, (group + 1) * part)
        into_f[pl.ds(pl.multiple_of(bases[0] + flip * part, part), part), :] = forward[rows]
        into_g[pl.ds(pl.multiple_of(bases[1] + flip * part, part), part), :] = backward[rows]
        into_decays[pl.ds(pl.multiple_of(bases[2] + flip * slot, slot), slot), :] = factors[which * 4 + group]


def keep_body(place, u_ref, v_ref, bc_ref, factors, keep_f, keep_g, decays):
    end_states(place, 0, u_ref, v_ref, bc_ref, factors, keep_f, keep_g, decays, (0, 0, 0))


def local_body(place, vals, cots, rate, starts, bc_ref, grad_out, scale_out, dbc_out):
    heads, length = rate.shape
    width = vals.shape[1]
    state = bc_ref.shape[1] // 2
    flags = starts[...].astype(f32)
    sums = decay_sums(log_rate(rate[...]))
    segment, last_segment = segments(flags)
    order, other = orders(length)
    later = jnp.where(other <= order, flags, 0.0)
    reach = dot(later.astype(bf16), jnp.where(order > other, 1.0, 0.0).astype(bf16))
    inside = jnp.logical_and(order >= other, reach == 0.0)
    scale = spread(jnp.exp(sums[-1:, :] - sums), heads, width)
    lifted = (spread(jnp.exp(sums - sums[-1:, :]), heads, width) * cots[...].astype(f32)).astype(bf16)
    weighted = (scale * vals[...].astype(f32)).astype(bf16)
    bmat, cmat = bc_ref[:, :state], bc_ref[:, state:]
    paired = jnp.where(inside, dot(lifted, weighted, (1, 1)), 0.0).astype(bf16)
    scores = jnp.where(inside, dot(cmat, bmat, (1, 1)), 0.0).astype(bf16)
    grad_out[...] = scale * dot(scores, lifted, (0, 0))
    scale_out[...] = jnp.where(segment == last_segment, scale, 0.0)
    dbc_out[:, :state] = dot(paired, cmat, (0, 0))
    dbc_out[:, state:] = dot(paired, bmat)


def pick(flag, first, second):
    return jnp.where(flag, first, second)


def quad_of(place):
    return lax.rem(place[2], 2) * 2 + place[1]


def chip_body(start, size, head, place, keep_f, keep_g, decays, recv, *outs):
    rows = size * head
    base = keep_f.shape[0]
    slot = decays.shape[0] // 4
    second = place[0] == 1
    for flip, out in enumerate(outs):
        for k in range(size):
            at = flip * (base // 4) + (start + k) * head
            spot = flip * slot + start + k
            mine = decays[spot:spot + 1, :]
            theirs = recv[2 * base + spot:2 * base + spot + 1, :]
            kf, rf = keep_f[at:at + head, :], recv[at:at + head, :]
            kg, rg = keep_g[at:at + head, :], recv[base + at:base + at + head, :]
            to = slice(k * head, (k + 1) * head)
            out[to, :] = pick(second, 1.0, theirs) * kf + pick(second, mine, 1.0) * rf
            to = slice(rows + k * head, rows + (k + 1) * head)
            out[to, :] = pick(second, theirs, 1.0) * kg + pick(second, 1.0, mine) * rg
            out[2 * rows + k:2 * rows + k + 1, :] = mine * theirs


def parts(ref, size, head, k):
    rows = size * head
    return ref[k * head:(k + 1) * head, :], ref[rows + k * head:rows + (k + 1) * head, :], ref[2 * rows + k:2 * rows + k + 1, :]


def joined(mine, theirs, second):
    forward = pick(second, 1.0, theirs[2]) * mine[0] + pick(second, mine[2], 1.0) * theirs[0]
    backward = pick(second, theirs[2], 1.0) * mine[1] + pick(second, 1.0, mine[2]) * theirs[1]
    return forward, backward, mine[2] * theirs[2]


def entering(mine, theirs, second, before, behind):
    my_before = pick(second, theirs[2], 1.0) * before + pick(second, 1.0, 0.0) * theirs[0]
    their_before = pick(second, 1.0, mine[2]) * before + pick(second, 0.0, 1.0) * mine[0]
    my_behind = pick(second, 1.0, theirs[2]) * behind + pick(second, 0.0, 1.0) * theirs[1]
    their_behind = pick(second, mine[2], 1.0) * behind + pick(second, 1.0, 0.0) * mine[1]
    return (my_before, my_behind), (their_before, their_behind)


def level_bit(place, bit):
    return lax.rem(place[2] // (1 << bit), 2) == 1


def store_total(out, total, size, head, k, upper):
    rows = size * head
    if upper is None:
        out[k * head:(k + 1) * head, :] = total[0]
        out[rows + k * head:rows + (k + 1) * head, :] = total[1]
        out[2 * rows + k:2 * rows + k + 1, :] = total[2]
    else:
        out[k * head:(k + 1) * head, :] = pick(upper, total[1], total[0])


def quad_body(size, head, last, place, own, three, one, two, out):
    second, later = place[1] == 1, level_bit(place, 0)
    upper = None if last is None else level_bit(place, last)
    for k in range(size):
        here, beside, along, across = (parts(ref, size, head, k) for ref in (own, one, two, three))
        total = joined(joined(here, beside, second), joined(along, across, second), later)
        store_total(out, total, size, head, k, upper)


def join_body(size, head, bit, last, place, total, recv, out):
    upper = None if last is None else level_bit(place, last)
    for k in range(size):
        mine, theirs = parts(total, size, head, k), parts(recv, size, head, k)
        store_total(out, joined(mine, theirs, level_bit(place, bit)), size, head, k, upper)


def enter_body(size, head, bits, place, own, three, one, two, *refs):
    levels, final, outs = refs[:bits - 2], refs[bits - 2], refs[bits - 1:]
    rows = size * head
    second, later = place[1] == 1, level_bit(place, 0)
    for k in range(size):
        before, behind, left, right = 0.0, 0.0, 1.0, 1.0
        for bit, recv in enumerate(levels):
            high = level_bit(place, bit + 1)
            forward, backward, decay = parts(recv, size, head, k)
            before = before + pick(high, left, 0.0) * forward
            behind = behind + pick(high, 0.0, right) * backward
            left = pick(high, left * decay, left)
            right = pick(high, right, right * decay)
        high = level_bit(place, bits - 1)
        at, after = slice(k * head, (k + 1) * head), slice(rows + k * head, rows + (k + 1) * head)
        last = final[at, :]
        before = before + pick(high, left, 0.0) * last
        behind = behind + pick(high, 0.0, right) * last
        here, beside, along, across = (parts(ref, size, head, k) for ref in (own, one, two, three))
        row, other = entering(joined(here, beside, second), joined(along, across, second), later, before, behind)
        states = entering(here, beside, second, *row) + entering(along, across, second, *other)
        for out, (state_before, state_behind) in zip(outs, states):
            out[at, :] = state_before
            out[after, :] = state_behind


def core_body(chunks, flips, head, place, *refs):
    count = 4 * len(chunks)
    keep_f, keep_g, decays, recv, send, own = refs[count:]
    base = keep_f.shape[0]
    rows = base // 4
    slot = decays.shape[0] // 4
    second = place[0] == 1
    for number, (start, size) in enumerate(chunks):
        for flip, ref in zip((0,) + flips[number], refs[number * 4:number * 4 + 4]):
            for k in range(size):
                at = flip * rows + (start + k) * head
                spot = flip * slot + start + k
                here = decays[spot:spot + 1, :]
                there = recv[2 * base + spot:2 * base + spot + 1, :]
                state = ref[k * head:(k + 1) * head, :]
                to, got = slice(at, at + head), recv[at:at + head, :]
                send[to, :] = pick(second, 1.0, here) * state + pick(second, 0.0, 1.0) * keep_f[to, :]
                own[to, :] = (pick(second, there, 1.0) * state + pick(second, 1.0, 0.0) * got).astype(bf16)
                state = ref[(size + k) * head:(size + k + 1) * head, :]
                to, got = slice(base + at, base + at + head), recv[base + at:base + at + head, :]
                send[to, :] = pick(second, here, 1.0) * state + pick(second, 1.0, 0.0) * keep_g[at:at + head, :]
                own[to, :] = (pick(second, 1.0, there) * state + pick(second, 0.0, 1.0) * got).astype(bf16)


def cross_body(near_set, last, place, u_ref, v_ref, so_far, states, out, after, before):
    half = after.shape[0]
    group, width = half // 4, after.shape[1]
    quad = quad_of(place)
    for flip in range(4):
        to = pl.ds(pl.multiple_of(jnp.bitwise_xor(quad, flip) * group, group), group)
        before[to, :] = states[flip * group:(flip + 1) * group, :].astype(bf16)
        after[to, :] = states[half + flip * group:half + (flip + 1) * group, :].astype(bf16)
    columns = pl.ds(pl.multiple_of(lax.rem(place[0] + near_set, 2) * half, half), half)
    for ref, weights, lanes in ((after, v_ref, slice(0, width)), (before, u_ref, slice(width, 2 * width))):
        total = so_far[:, lanes] + dot(weights[:, columns], ref[...])
        out[:, lanes] = total.astype(bf16).astype(f32) if last else total


def values_body(place, grad_ref, scale_ref, bc_ref, mine, theirs, grad_out, done):
    done[...] = jnp.zeros_like(done)
    half = mine.shape[0]
    bmat = bc_ref[:, : mine.shape[1]]
    for near_set, after in ((0, mine), (1, theirs)):
        columns = pl.ds(pl.multiple_of(lax.rem(place[0] + near_set, 2) * half, half), half)
        grad_out[:, columns] = (grad_ref[:, columns] + scale_ref[:, columns] * dot(bmat, after[...], (1, 1))).astype(bf16)


def block_row(quarter, position, levels, rows):
    quad, rest = position // (levels // 2), position % (levels // 2)
    level = 0
    for bit in range(levels.bit_length() - 2):
        level = level * 2 + rest % 2
        rest //= 2
    index = (quarter // 2) * (4 * levels) + (level * 2 + quad // 2) * 4 + quad % 2 * 2 + lax.rem(quarter, 2)
    return pl.multiple_of(index * rows, rows)


def turn_body(levels, rows, place, normed, own, beside, beyond, turned):
    turned[...] = normed[...].T.astype(f32)
    count = 2 * levels
    quarter = place[3] * 2 + place[0]
    half = count // 2 * rows
    for flip in range(4):
        out, base = ((own, 0), (beside, 0), (beyond, 0), (beyond, 3 * half))[flip]
        for position in range(count):
            start = block_row(jnp.bitwise_xor(quarter, flip), position, levels, rows)
            block = turned[pl.ds(start, rows), :]
            at = position * rows
            if flip == 0:
                out[at:at + rows, :] = block.astype(bf16)
            else:
                out[base + at:base + at + rows, :] = block[:, :LANES]
                tail = base + 2 * half + at % half
                lanes = slice(0, LANES // 2) if position < count // 2 else slice(LANES // 2, LANES)
                out[tail:tail + rows, lanes] = block[:, LANES:]


def stack_body(place, beside, beyond, out):
    rows = beside.shape[0]
    out[:rows, :] = beside[...]
    out[rows:, :] = beyond[rows:, :]


def unpack_body(place, own, beside, beyond, out):
    length = own.shape[1]
    total = own.shape[0]
    half = total // 2
    wide = 3 * half
    out[:, :length] = own[...]
    for index, (ref, base) in enumerate(((beside, 0), (beyond, 0), (beside, wide)), 1):
        left = index * length
        out[:, left:left + LANES] = ref[base:base + total, :].astype(bf16)
        out[:half, left + LANES:left + length] = ref[base + total:base + wide, :LANES // 2].astype(bf16)
        out[half:, left + LANES:left + length] = ref[base + total:base + wide, LANES // 2:].astype(bf16)


def weight_body(place, turned, own, one, two, three, *refs):
    outs, product = refs[:4], refs[4]
    length = own.shape[0]
    total = None
    for index, ref in enumerate((own, one, two, three)):
        term = dot(turned[:, index * length:(index + 1) * length], ref[...].astype(bf16))
        total = term if total is None else total + term
    product[...] = total
    rows = outs[0].shape[0]
    for flip, out in enumerate(outs):
        block = jnp.bitwise_xor(quad_of(place), flip)
        out[...] = product[pl.ds(pl.multiple_of(block * rows, rows), rows), :]


def halve_body(bit, place, *refs):
    terms, send, keep = refs[:-2], refs[-2], refs[-1]
    rows = keep.shape[0]
    here = lax.rem(place[2] // (1 << bit), 2)
    for which, out in ((1 - here, send), (here, keep)):
        at = pl.ds(pl.multiple_of(which * rows, rows), rows)
        total = terms[0][at, :]
        for term in terms[1:]:
            total = total + term[at, :]
        out[...] = total


def local(normed, values, cotangent, w_bc, rate_index, starts):
    hidden, vals, cots = normed[0], values[0], cotangent[0]
    rate = rate_index[0]
    length, width = vals.shape
    depth = hidden.shape[1]
    heads = rate.shape[0]
    head = width // heads
    state = w_bc.shape[1] // 2
    shards = lax.axis_size("seq")
    packs = lax.axis_size("dp")
    levels = shards // 4
    bits = levels.bit_length() - 1
    eighth = heads // 8
    slot = padded(eighth)
    base = width // 2

    def shape(rows, columns, dtype=f32):
        return jax.ShapeDtypeStruct((rows, columns), dtype)

    token = []

    def kernel(body, outs, *args, scratch=(), vmem=4, far=False, behind=()):
        count = len(args)
        after = list(token) + list(behind)
        single = not isinstance(outs, tuple)

        def run(*refs):
            spot = lax.axis_index("seq")
            place = (spot & 1, (spot >> 1) & 1, spot >> 2, lax.axis_index("dp") & 1)
            body(place, *refs[:count], *refs[count + len(after):])

        here = pl.BlockSpec(memory_space=pltpu.VMEM)
        there = pl.BlockSpec(memory_space=pltpu.HBM) if far else here
        if far:
            args = [pltpu.with_memory_space_constraint(array, pltpu.HBM) for array in args]
        result = pl.pallas_call(
            run,
            in_specs=[there] * count + [pl.BlockSpec(memory_space=pl.ANY)] * len(after),
            out_specs=here if single else (here,) * len(outs),
            out_shape=outs,
            scratch_shapes=list(scratch),
            compiler_params=pltpu.CompilerParams(vmem_limit_bytes=vmem * MIB),
            cost_estimate=pl.CostEstimate(flops=1000, bytes_accessed=1000, transcendentals=0),
        )(*args, *after)
        token[:] = [result if single else min(result, key=lambda array: array.size)]
        return result

    def bind(body, *constants):
        return lambda *refs: body(*constants, *refs)

    def swap(array, mask):
        return lax.ppermute(array, "seq", [(s, s ^ mask) for s in range(shards)])

    def swap_pack(array):
        return lax.ppermute(array, "dp", [(d, d ^ 1) for d in range(packs)])

    def swap_both(array):
        return lax.ppermute(array, ("dp", "seq"), [(d * shards + s, (d ^ 1) * shards + (s ^ 1)) for d in range(packs) for s in range(shards)])

    message, factors, u, v, bc = kernel(
        first_body,
        (
            shape(2 * base + 4 * slot, state), jax.ShapeDtypeStruct((8, slot, LANES), f32),
            shape(length, width, bf16), shape(length, width, bf16), shape(length, 2 * state, bf16),
        ),
        normed, w_bc, values, cotangent, rate_index, starts,
        scratch=[
            pltpu.VMEM((8, slot, LANES), f32), pltpu.VMEM(hidden.shape, bf16), pltpu.VMEM(w_bc.shape, bf16),
            pltpu.VMEM(vals.shape, bf16), pltpu.VMEM(cots.shape, bf16), pltpu.VMEM(rate.shape, jnp.int32),
            pltpu.VMEM(starts.shape, jnp.int32),
        ] + [pltpu.SemaphoreType.DMA((count,)) for count in (2, 4, 4, 4, 4)],
        vmem=24, far=True,
    )
    recv = swap(message, 1)
    keep_f, keep_g, decays = kernel(
        keep_body, (shape(base, state), shape(base, state), shape(4 * slot, state)), u, v, bc, factors, vmem=16,
    )

    direct = packs == 2 and depth % (packs * shards * 16) == 0 and length == 3 * LANES // 2
    rows = depth // (packs * shards)
    part = depth // 4
    wide = part + part // 2
    pack_turned = None
    if direct:
        own_turned, core_turned, message = kernel(
            bind(turn_body, levels, rows), (shape(part, length, bf16), shape(wide, LANES), shape(2 * wide, LANES)),
            hidden, scratch=[pltpu.VMEM((depth, length), f32)], vmem=16,
        )
        pack_turned = swap_pack(message)

    bounds = [-(-eighth * i // CHUNKS) for i in range(CHUNKS + 1)]
    chunks = [(a, b - a) for a, b in zip(bounds, bounds[1:])]

    def parcel(size):
        return shape(2 * size * head + padded(size), state)

    def to_quad(arrays, flips=(3, 1, 2)):
        return [swap(arrays[flip - 1], flip * 2) for flip in flips]

    quads = []
    for start, size in chunks:
        waits = quads[-1][1:2] if quads else ()
        if quads:
            grad_local, scale, dbc_local = kernel(
                local_body, (shape(length, width), shape(length, width), shape(length, 2 * state)),
                vals, cots, rate, starts, bc, vmem=24,
            )
        own, *sends = kernel(bind(chip_body, start, size, head), (parcel(size),) * 4, keep_f, keep_g, decays, recv, behind=waits)
        quads.append([own] + to_quad(sends))

    totals, arrived = [], [[] for unused in chunks]
    for number, ((start, size), group) in enumerate(zip(chunks, quads)):
        last = 1 if bits == 2 else None
        out = parcel(size) if last is None else shape(size * head, state)
        totals.append(kernel(bind(quad_body, size, head, last), out, *group))
        arrived[number].append(swap(totals[number], 8))
    for bit in range(1, bits - 1):
        last = bit + 1 if bit == bits - 2 else None
        for number, (start, size) in enumerate(chunks):
            out = parcel(size) if last is None else shape(size * head, state)
            totals[number] = kernel(bind(join_body, size, head, bit, last), out, totals[number], arrived[number][-1])
            arrived[number].append(swap(totals[number], 8 << bit))
    states, orders_of = [], []
    for number, ((start, size), group, steps) in enumerate(zip(chunks, quads, arrived)):
        waits = states[1:2] + ([pack_turned] if direct else []) if states else []
        enter, *sends = kernel(
            bind(enter_body, size, head, bits), (shape(2 * size * head, state),) * 4, *group, *steps, behind=waits,
        )
        orders_of.append((1, 3, 2) if number == 0 else (3, 1, 2))
        states += [enter] + to_quad(sends, orders_of[-1])
    send, final = kernel(
        bind(core_body, chunks, orders_of, head), (shape(2 * base, state), shape(2 * base, state, bf16)), *states, keep_f, keep_g, decays, recv,
    )
    core_recv = swap(send, 1)
    dbc = dbc_local
    afters = []
    for near_set, pieces in ((0, final), (1, core_recv)):
        dbc, after = kernel(
            bind(cross_body, near_set, near_set == 1), (shape(length, 2 * state), shape(base, state, bf16)),
            u, v, dbc, pieces, scratch=[pltpu.VMEM((base, state), bf16)], vmem=16,
        )
        afters.append(after)
    portion = 1.0 / (packs * shards * length)
    if direct:
        from_pack = swap_pack(dbc)
        from_core = swap(dbc, 1)
        from_both = swap(from_pack, 1)
        beside = swap(kernel(stack_body, shape(2 * wide, LANES), core_turned, pack_turned, vmem=8), 1)
    grad_values, unused_done = kernel(
        values_body, (shape(length, width, bf16), shape(8, LANES)), grad_local, scale, bc, *afters, vmem=16,
    )
    if not direct:
        product = lax.dot_general(hidden, dbc.astype(bf16), (((0,), (0,)), ((), ())), preferred_element_type=f32)
        return (grad_values[None], lax.psum_scatter(product * portion, ("dp", "seq"), scatter_dimension=0, tiled=True))
    turned = kernel(unpack_body, shape(part, 4 * length, bf16), own_turned, beside, pack_turned, vmem=8)
    keep, *sends = kernel(
        weight_body, (shape(part // 4, 2 * state),) * 4, turned, dbc, from_core, from_pack, from_both,
        scratch=[pltpu.VMEM((part, 2 * state), f32)], vmem=16,
    )
    terms = [keep] + to_quad(sends)
    size = part // 4
    for bit in range(1, bits):
        size //= 2
        send, keep = kernel(bind(halve_body, bit), (shape(size, 2 * state), shape(size, 2 * state)), *terms)
        terms = [keep, swap(send, 4 << bit)]
    grad_wbc = (terms[0] + terms[1]) * portion
    return (grad_values[None], grad_wbc)


def solution(mesh):
    placed = (
        P("dp", "seq", None),
        P("dp", "seq", None),
        P("dp", "seq", None),
        P(),
        P("dp", None, "seq"),
        P("dp", "seq"),
    )
    return jax.shard_map(
        local,
        mesh=mesh,
        in_specs=placed,
        out_specs=(P("dp", "seq", None), P(("dp", "seq"), None)),
        check_vma=False,
    )
```

```python
import math

import jax
import jax.numpy as jnp
from jax import lax
from jax.experimental import pallas as pl
from jax.experimental.pallas import tpu as pltpu
from jax.sharding import PartitionSpec as P

RATES = 16
CHUNKS = 2
LANES = 128
MIB = 1024 * 1024

f32 = jnp.float32
bf16 = jnp.bfloat16
highest = lax.Precision.HIGHEST


def log_rate(index):
    return -0.0001 * jnp.exp(index.astype(f32) * (math.log(500.0) / (RATES - 1)))


def dot(lhs, rhs, over=(1, 0), precision=None):
    dims = (((over[0],), (over[1],)), ((), ()))
    return lax.dot_general(lhs, rhs, dims, precision=precision, preferred_element_type=f32)


def padded(rows):
    return -(-rows // 8) * 8


def halves_of(small):
    high = small.astype(bf16).astype(f32)
    return jnp.concatenate([high, small - high], axis=1).astype(bf16)


def spread(halves, first, count, head):
    heads = halves.shape[1] // 2
    lane = (lax.broadcasted_iota(jnp.int32, (heads, count), 1) + first) // head
    row = lax.broadcasted_iota(jnp.int32, (heads, count), 0)
    pattern = jnp.where(lane == row, 1.0, 0.0).astype(bf16)
    return dot(halves, jnp.concatenate([pattern, pattern], axis=0))


def orders(length):
    return (lax.broadcasted_iota(jnp.int32, (length, length), 0), lax.broadcasted_iota(jnp.int32, (length, length), 1))


def decay_sums(logs):
    order, other = orders(logs.shape[1])
    lower = jnp.where(other <= order, 1.0, 0.0).astype(bf16)
    high = logs.astype(bf16)
    rest = logs - high.astype(f32)
    middle = rest.astype(bf16)
    low = (rest - middle.astype(f32)).astype(bf16)
    return dot(lower, low, (1, 1)) + dot(lower, middle, (1, 1)) + dot(lower, high, (1, 1))


def segments(flags):
    order, other = orders(flags.shape[1])
    column = jnp.sum(jnp.where(other <= order, flags, 0.0), axis=1, keepdims=True)
    return column, jnp.sum(flags, axis=1, keepdims=True)


def pieces_of(array, count):
    rows = array.shape[0] // count
    return [slice(i * rows, (i + 1) * rows) for i in range(count)]


def first_body(
    place, normed_far, w_far, vals_far, cots_far, rate_far, starts_far, message, factors_out, u_out, v_out, bc_out, normed,
    groups, w_bc, vals, cots, rate, starts, small, first, second, third, fourth,
):
    heads = rate.shape[0]
    width = vals.shape[1]
    state = w_bc.shape[1] // 2
    early = [pltpu.make_async_copy(rate_far.at[0], rate, small.at[0]), pltpu.make_async_copy(starts_far, starts, small.at[1])]
    waves = []
    for source, target, sems in (
        (normed_far.at[0], normed, first), (w_far, w_bc, second), (cots_far.at[0], cots, third), (vals_far.at[0], vals, fourth),
    ):
        waves.append([
            pltpu.make_async_copy(source.at[rows], target.at[rows], sems.at[i])
            for i, rows in enumerate(pieces_of(target, sems.shape[0]))
        ])
    for copies in [early] + waves:
        for copy in copies:
            copy.start()
    for copy in early:
        copy.wait()
    logs = log_rate(rate[...])
    flags = starts[...].astype(f32)
    sums = decay_sums(logs)
    segment, last_segment = segments(flags)
    total = jnp.where(last_segment == 0.0, jnp.exp(jnp.sum(logs, axis=1, keepdims=True)), 0.0)
    total = jnp.broadcast_to(total, (heads, LANES))
    eighth = heads // 8
    for group in range(8):
        groups[group, :eighth, :] = total[group * eighth:(group + 1) * eighth]
    up = jnp.where(segment == 0.0, jnp.exp(sums), 0.0)
    down = jnp.where(segment == last_segment, jnp.exp(sums[-1:, :] - sums), 0.0)
    up, down = halves_of(up), halves_of(down)
    for copy in waves[0] + waves[1] + waves[2] + waves[3]:
        copy.wait()
    bc_out[...] = dot(normed[...], w_bc[...]).astype(bf16)
    tile = width // 5
    for first in range(0, width, tile):
        lanes = slice(first, first + tile)
        u_out[:, lanes] = (spread(up, first, tile, width // heads) * cots[:, lanes].astype(f32)).astype(bf16)
        v_out[:, lanes] = (spread(down, first, tile, width // heads) * vals[:, lanes].astype(f32)).astype(bf16)
    factors_out[...] = groups[...]
    half = width // 2
    end_states(place, 1, u_out, v_out, bc_out, groups, message, message, message, (0, half, 2 * half))


def end_states(place, near_set, u_ref, v_ref, bc_ref, factors, into_f, into_g, into_decays, bases):
    state = bc_ref.shape[1] // 2
    half, part, slot = u_ref.shape[1] // 2, u_ref.shape[1] // 8, factors.shape[1]
    which = lax.rem(place[0] + near_set, 2)
    columns = pl.ds(pl.multiple_of(which * half, half), half)
    quad = quad_of(place)
    forward = dot(v_ref[:, columns], bc_ref[:, :state], (0, 0))
    backward = dot(u_ref[:, columns], bc_ref[:, state:], (0, 0))
    for group in range(4):
        flip = jnp.bitwise_xor(quad, group)
        rows = slice(group * part, (group + 1) * part)
        into_f[pl.ds(pl.multiple_of(bases[0] + flip * part, part), part), :] = forward[rows]
        into_g[pl.ds(pl.multiple_of(bases[1] + flip * part, part), part), :] = backward[rows]
        into_decays[pl.ds(pl.multiple_of(bases[2] + flip * slot, slot), slot), :] = factors[which * 4 + group]


def keep_body(place, u_ref, v_ref, bc_ref, factors, keep_f, keep_g, decays):
    end_states(place, 0, u_ref, v_ref, bc_ref, factors, keep_f, keep_g, decays, (0, 0, 0))


def local_body(place, vals, cots, rate, starts, bc_ref, grad_out, scale_out, dbc_out):
    heads, length = rate.shape
    width = vals.shape[1]
    state = bc_ref.shape[1] // 2
    flags = starts[...].astype(f32)
    sums = decay_sums(log_rate(rate[...]))
    segment, last_segment = segments(flags)
    order, other = orders(length)
    later = jnp.where(other <= order, flags, 0.0)
    reach = dot(later.astype(bf16), jnp.where(order > other, 1.0, 0.0).astype(bf16))
    inside = jnp.logical_and(order >= other, reach == 0.0)
    head = width // heads
    scale = spread(halves_of(jnp.exp(sums[-1:, :] - sums)), 0, width, head)
    lifted = (spread(halves_of(jnp.exp(sums - sums[-1:, :])), 0, width, head) * cots[...].astype(f32)).astype(bf16)
    weighted = (scale * vals[...].astype(f32)).astype(bf16)
    bmat, cmat = bc_ref[:, :state], bc_ref[:, state:]
    paired = jnp.where(inside, dot(lifted, weighted, (1, 1)), 0.0).astype(bf16)
    scores = jnp.where(inside, dot(cmat, bmat, (1, 1)), 0.0).astype(bf16)
    grad_out[...] = scale * dot(scores, lifted, (0, 0))
    scale_out[...] = jnp.where(segment == last_segment, scale, 0.0)
    dbc_out[:, :state] = dot(paired, cmat, (0, 0))
    dbc_out[:, state:] = dot(paired, bmat)


def pick(flag, first, second):
    return jnp.where(flag, first, second)


def quad_of(place):
    return lax.rem(place[2], 2) * 2 + place[1]


def chip_body(start, size, head, place, keep_f, keep_g, decays, recv, *outs):
    rows = size * head
    base = keep_f.shape[0]
    slot = decays.shape[0] // 4
    second = place[0] == 1
    for flip, out in enumerate(outs):
        for k in range(size):
            at = flip * (base // 4) + (start + k) * head
            spot = flip * slot + start + k
            mine = decays[spot:spot + 1, :]
            theirs = recv[2 * base + spot:2 * base + spot + 1, :]
            kf, rf = keep_f[at:at + head, :], recv[at:at + head, :]
            kg, rg = keep_g[at:at + head, :], recv[base + at:base + at + head, :]
            to = slice(k * head, (k + 1) * head)
            out[to, :] = pick(second, 1.0, theirs) * kf + pick(second, mine, 1.0) * rf
            to = slice(rows + k * head, rows + (k + 1) * head)
            out[to, :] = pick(second, theirs, 1.0) * kg + pick(second, 1.0, mine) * rg
            out[2 * rows + k:2 * rows + k + 1, :] = mine * theirs


def parts(ref, size, head, k):
    rows = size * head
    return ref[k * head:(k + 1) * head, :], ref[rows + k * head:rows + (k + 1) * head, :], ref[2 * rows + k:2 * rows + k + 1, :]


def joined(mine, theirs, second):
    forward = pick(second, 1.0, theirs[2]) * mine[0] + pick(second, mine[2], 1.0) * theirs[0]
    backward = pick(second, theirs[2], 1.0) * mine[1] + pick(second, 1.0, mine[2]) * theirs[1]
    return forward, backward, mine[2] * theirs[2]


def entering(mine, theirs, second, before, behind):
    my_before = pick(second, theirs[2], 1.0) * before + pick(second, 1.0, 0.0) * theirs[0]
    their_before = pick(second, 1.0, mine[2]) * before + pick(second, 0.0, 1.0) * mine[0]
    my_behind = pick(second, 1.0, theirs[2]) * behind + pick(second, 0.0, 1.0) * theirs[1]
    their_behind = pick(second, mine[2], 1.0) * behind + pick(second, 1.0, 0.0) * mine[1]
    return (my_before, my_behind), (their_before, their_behind)


def level_bit(place, bit):
    return lax.rem(place[2] // (1 << bit), 2) == 1


def store_total(out, total, size, head, k, upper):
    rows = size * head
    if upper is None:
        out[k * head:(k + 1) * head, :] = total[0]
        out[rows + k * head:rows + (k + 1) * head, :] = total[1]
        out[2 * rows + k:2 * rows + k + 1, :] = total[2]
    else:
        out[k * head:(k + 1) * head, :] = pick(upper, total[1], total[0])


def quad_body(size, head, last, place, own, three, one, two, out):
    second, later = place[1] == 1, level_bit(place, 0)
    upper = None if last is None else level_bit(place, last)
    for k in range(size):
        here, beside, along, across = (parts(ref, size, head, k) for ref in (own, one, two, three))
        total = joined(joined(here, beside, second), joined(along, across, second), later)
        store_total(out, total, size, head, k, upper)


def join_body(size, head, bit, last, place, total, recv, out):
    upper = None if last is None else level_bit(place, last)
    for k in range(size):
        mine, theirs = parts(total, size, head, k), parts(recv, size, head, k)
        store_total(out, joined(mine, theirs, level_bit(place, bit)), size, head, k, upper)


def enter_body(size, head, bits, place, own, three, one, two, *refs):
    levels, final, outs = refs[:bits - 2], refs[bits - 2], refs[bits - 1:]
    rows = size * head
    second, later = place[1] == 1, level_bit(place, 0)
    for k in range(size):
        before, behind, left, right = 0.0, 0.0, 1.0, 1.0
        for bit, recv in enumerate(levels):
            high = level_bit(place, bit + 1)
            forward, backward, decay = parts(recv, size, head, k)
            before = before + pick(high, left, 0.0) * forward
            behind = behind + pick(high, 0.0, right) * backward
            left = pick(high, left * decay, left)
            right = pick(high, right, right * decay)
        high = level_bit(place, bits - 1)
        at, after = slice(k * head, (k + 1) * head), slice(rows + k * head, rows + (k + 1) * head)
        last = final[at, :]
        before = before + pick(high, left, 0.0) * last
        behind = behind + pick(high, 0.0, right) * last
        here, beside, along, across = (parts(ref, size, head, k) for ref in (own, one, two, three))
        row, other = entering(joined(here, beside, second), joined(along, across, second), later, before, behind)
        states = entering(here, beside, second, *row) + entering(along, across, second, *other)
        for out, (state_before, state_behind) in zip(outs, states):
            out[at, :] = state_before
            out[after, :] = state_behind


def core_body(chunks, head, place, *refs):
    count = 4 * len(chunks)
    keep_f, keep_g, decays, recv, send, own = refs[count:]
    base = keep_f.shape[0]
    rows = base // 4
    slot = decays.shape[0] // 4
    second = place[0] == 1
    for number, (start, size) in enumerate(chunks):
        for flip, ref in zip((0, 3, 1, 2), refs[number * 4:number * 4 + 4]):
            for k in range(size):
                at = flip * rows + (start + k) * head
                spot = flip * slot + start + k
                here = decays[spot:spot + 1, :]
                there = recv[2 * base + spot:2 * base + spot + 1, :]
                state = ref[k * head:(k + 1) * head, :]
                to, got = slice(at, at + head), recv[at:at + head, :]
                send[to, :] = pick(second, 1.0, here) * state + pick(second, 0.0, 1.0) * keep_f[to, :]
                own[to, :] = (pick(second, there, 1.0) * state + pick(second, 1.0, 0.0) * got).astype(bf16)
                state = ref[(size + k) * head:(size + k + 1) * head, :]
                to, got = slice(base + at, base + at + head), recv[base + at:base + at + head, :]
                send[to, :] = pick(second, here, 1.0) * state + pick(second, 1.0, 0.0) * keep_g[at:at + head, :]
                own[to, :] = (pick(second, 1.0, there) * state + pick(second, 0.0, 1.0) * got).astype(bf16)


def cross_body(near_set, last, place, u_ref, v_ref, so_far, states, out, after, before):
    half = after.shape[0]
    group, width = half // 4, after.shape[1]
    quad = quad_of(place)
    for flip in range(4):
        to = pl.ds(pl.multiple_of(jnp.bitwise_xor(quad, flip) * group, group), group)
        before[to, :] = states[flip * group:(flip + 1) * group, :].astype(bf16)
        after[to, :] = states[half + flip * group:half + (flip + 1) * group, :].astype(bf16)
    columns = pl.ds(pl.multiple_of(lax.rem(place[0] + near_set, 2) * half, half), half)
    for ref, weights, lanes in ((after, v_ref, slice(0, width)), (before, u_ref, slice(width, 2 * width))):
        total = so_far[:, lanes] + dot(weights[:, columns], ref[...])
        out[:, lanes] = total.astype(bf16).astype(f32) if last else total


def values_body(place, grad_ref, scale_ref, bc_ref, mine, theirs, grad_out, done):
    done[...] = jnp.zeros_like(done)
    half = mine.shape[0]
    bmat = bc_ref[:, : mine.shape[1]]
    for near_set, after in ((0, mine), (1, theirs)):
        columns = pl.ds(pl.multiple_of(lax.rem(place[0] + near_set, 2) * half, half), half)
        grad_out[:, columns] = (grad_ref[:, columns] + scale_ref[:, columns] * dot(bmat, after[...], (1, 1))).astype(bf16)


def block_row(quarter, position, levels, rows):
    quad, rest = position // (levels // 2), position % (levels // 2)
    level = 0
    for bit in range(levels.bit_length() - 2):
        level = level * 2 + rest % 2
        rest //= 2
    index = (quarter // 2) * (4 * levels) + (level * 2 + quad // 2) * 4 + quad % 2 * 2 + lax.rem(quarter, 2)
    return pl.multiple_of(index * rows, rows)


def turn_body(levels, rows, place, normed, own, beside, beyond, turned):
    turned[...] = normed[...].T.astype(f32)
    count = 2 * levels
    quarter = place[3] * 2 + place[0]
    half = count // 2 * rows
    for flip in range(4):
        out, base = ((own, 0), (beside, 0), (beyond, 0), (beyond, 3 * half))[flip]
        for position in range(count):
            start = block_row(jnp.bitwise_xor(quarter, flip), position, levels, rows)
            block = turned[pl.ds(start, rows), :]
            at = position * rows
            if flip == 0:
                out[at:at + rows, :] = block.astype(bf16)
            else:
                out[base + at:base + at + rows, :] = block[:, :LANES]
                tail = base + 2 * half + at % half
                lanes = slice(0, LANES // 2) if position < count // 2 else slice(LANES // 2, LANES)
                out[tail:tail + rows, lanes] = block[:, LANES:]


def stack_body(place, beside, beyond, out):
    rows = beside.shape[0]
    out[:rows, :] = beside[...]
    out[rows:, :] = beyond[rows:, :]


def unpack_body(place, own, beside, beyond, out):
    length = own.shape[1]
    total = own.shape[0]
    half = total // 2
    wide = 3 * half
    out[:, :length] = own[...]
    for index, (ref, base) in enumerate(((beside, 0), (beyond, 0), (beside, wide)), 1):
        left = index * length
        out[:, left:left + LANES] = ref[base:base + total, :].astype(bf16)
        out[:half, left + LANES:left + length] = ref[base + total:base + wide, :LANES // 2].astype(bf16)
        out[half:, left + LANES:left + length] = ref[base + total:base + wide, LANES // 2:].astype(bf16)


def weight_body(place, turned, own, one, two, three, *refs):
    outs, product = refs[:4], refs[4]
    length = own.shape[0]
    total = None
    for index, ref in enumerate((own, one, two, three)):
        term = dot(turned[:, index * length:(index + 1) * length], ref[...].astype(bf16))
        total = term if total is None else total + term
    product[...] = total
    rows = outs[0].shape[0]
    for flip, out in enumerate(outs):
        block = jnp.bitwise_xor(quad_of(place), flip)
        out[...] = product[pl.ds(pl.multiple_of(block * rows, rows), rows), :]


def halve_body(bit, place, *refs):
    terms, send, keep = refs[:-2], refs[-2], refs[-1]
    rows = keep.shape[0]
    here = lax.rem(place[2] // (1 << bit), 2)
    for which, out in ((1 - here, send), (here, keep)):
        at = pl.ds(pl.multiple_of(which * rows, rows), rows)
        total = terms[0][at, :]
        for term in terms[1:]:
            total = total + term[at, :]
        out[...] = total


def local(normed, values, cotangent, w_bc, rate_index, starts):
    hidden, vals, cots = normed[0], values[0], cotangent[0]
    rate = rate_index[0]
    length, width = vals.shape
    depth = hidden.shape[1]
    heads = rate.shape[0]
    head = width // heads
    state = w_bc.shape[1] // 2
    shards = lax.axis_size("seq")
    packs = lax.axis_size("dp")
    levels = shards // 4
    bits = levels.bit_length() - 1
    eighth = heads // 8
    slot = padded(eighth)
    base = width // 2

    def shape(rows, columns, dtype=f32):
        return jax.ShapeDtypeStruct((rows, columns), dtype)

    token = []

    def kernel(body, outs, *args, scratch=(), vmem=4, far=False, behind=()):
        count = len(args)
        after = list(token) + list(behind)
        single = not isinstance(outs, tuple)

        def run(*refs):
            spot = lax.axis_index("seq")
            place = (spot & 1, (spot >> 1) & 1, spot >> 2, lax.axis_index("dp") & 1)
            body(place, *refs[:count], *refs[count + len(after):])

        here = pl.BlockSpec(memory_space=pltpu.VMEM)
        there = pl.BlockSpec(memory_space=pltpu.HBM) if far else here
        if far:
            args = [pltpu.with_memory_space_constraint(array, pltpu.HBM) for array in args]
        result = pl.pallas_call(
            run,
            in_specs=[there] * count + [pl.BlockSpec(memory_space=pl.ANY)] * len(after),
            out_specs=here if single else (here,) * len(outs),
            out_shape=outs,
            scratch_shapes=list(scratch),
            compiler_params=pltpu.CompilerParams(vmem_limit_bytes=vmem * MIB),
            cost_estimate=pl.CostEstimate(flops=1000, bytes_accessed=1000, transcendentals=0),
        )(*args, *after)
        token[:] = [result if single else min(result, key=lambda array: array.size)]
        return result

    def bind(body, *constants):
        return lambda *refs: body(*constants, *refs)

    def swap(array, mask):
        return lax.ppermute(array, "seq", [(s, s ^ mask) for s in range(shards)])

    def swap_pack(array):
        return lax.ppermute(array, "dp", [(d, d ^ 1) for d in range(packs)])

    def swap_both(array):
        return lax.ppermute(array, ("dp", "seq"), [(d * shards + s, (d ^ 1) * shards + (s ^ 1)) for d in range(packs) for s in range(shards)])

    message, factors, u, v, bc, near_normed = kernel(
        first_body,
        (
            shape(2 * base + 4 * slot, state), jax.ShapeDtypeStruct((8, slot, LANES), f32),
            shape(length, width, bf16), shape(length, width, bf16), shape(length, 2 * state, bf16), shape(length, depth, bf16),
        ),
        normed, w_bc, values, cotangent, rate_index, starts,
        scratch=[
            pltpu.VMEM((8, slot, LANES), f32), pltpu.VMEM(w_bc.shape, bf16),
            pltpu.VMEM(vals.shape, bf16), pltpu.VMEM(cots.shape, bf16), pltpu.VMEM(rate.shape, jnp.int32),
            pltpu.VMEM(starts.shape, jnp.int32),
        ] + [pltpu.SemaphoreType.DMA((count,)) for count in (2, 4, 4, 4, 4)],
        vmem=24, far=True,
    )
    recv = swap(message, 1)
    keep_f, keep_g, decays = kernel(
        keep_body, (shape(base, state), shape(base, state), shape(4 * slot, state)), u, v, bc, factors, vmem=16,
    )

    direct = packs == 2 and depth % (packs * shards * 16) == 0 and length == 3 * LANES // 2
    rows = depth // (packs * shards)
    part = depth // 4
    wide = part + part // 2
    pack_turned = None
    if direct:
        own_turned, core_turned, message = kernel(
            bind(turn_body, levels, rows), (shape(part, length, bf16), shape(wide, LANES), shape(2 * wide, LANES)),
            near_normed, scratch=[pltpu.VMEM((depth, length), f32)], vmem=16,
        )
        pack_turned = swap_pack(message)

    bounds = [-(-eighth * i // CHUNKS) for i in range(CHUNKS + 1)]
    chunks = [(a, b - a) for a, b in zip(bounds, bounds[1:])]

    def parcel(size):
        return shape(2 * size * head + padded(size), state)

    def to_quad(arrays):
        across = swap(arrays[2], 6)
        return [across, swap(arrays[0], 2), swap(arrays[1], 4)]

    quads = []
    for start, size in chunks:
        waits = quads[-1][1:2] if quads else ()
        if quads:
            grad_local, scale, dbc_local = kernel(
                local_body, (shape(length, width), shape(length, width), shape(length, 2 * state)),
                vals, cots, rate, starts, bc, vmem=24,
            )
        own, *sends = kernel(bind(chip_body, start, size, head), (parcel(size),) * 4, keep_f, keep_g, decays, recv, behind=waits)
        quads.append([own] + to_quad(sends))

    totals, arrived = [], [[] for unused in chunks]
    for number, ((start, size), group) in enumerate(zip(chunks, quads)):
        last = 1 if bits == 2 else None
        out = parcel(size) if last is None else shape(size * head, state)
        totals.append(kernel(bind(quad_body, size, head, last), out, *group))
        arrived[number].append(swap(totals[number], 8))
    for bit in range(1, bits - 1):
        last = bit + 1 if bit == bits - 2 else None
        for number, (start, size) in enumerate(chunks):
            out = parcel(size) if last is None else shape(size * head, state)
            totals[number] = kernel(bind(join_body, size, head, bit, last), out, totals[number], arrived[number][-1])
            arrived[number].append(swap(totals[number], 8 << bit))
    states = []
    for number, ((start, size), group, steps) in enumerate(zip(chunks, quads, arrived)):
        waits = states[1:2] + ([pack_turned] if direct else []) if states else []
        enter, *sends = kernel(
            bind(enter_body, size, head, bits), (shape(2 * size * head, state),) * 4, *group, *steps, behind=waits,
        )
        states += [enter] + to_quad(sends)
    send, final = kernel(
        bind(core_body, chunks, head), (shape(2 * base, state), shape(2 * base, state, bf16)), *states, keep_f, keep_g, decays, recv,
    )
    core_recv = swap(send, 1)
    dbc = dbc_local
    afters = []
    for near_set, pieces in ((0, final), (1, core_recv)):
        dbc, after = kernel(
            bind(cross_body, near_set, near_set == 1), (shape(length, 2 * state), shape(base, state, bf16)),
            u, v, dbc, pieces, scratch=[pltpu.VMEM((base, state), bf16)], vmem=16,
        )
        afters.append(after)
    portion = 1.0 / (packs * shards * length)
    if direct:
        from_pack = swap_pack(dbc)
        from_core = swap(dbc, 1)
        from_both = swap(from_pack, 1)
        beside = swap(kernel(stack_body, shape(2 * wide, LANES), core_turned, pack_turned, vmem=8), 1)
    grad_values, unused_done = kernel(
        values_body, (shape(length, width, bf16), shape(8, LANES)), grad_local, scale, bc, *afters, vmem=16,
    )
    if not direct:
        product = lax.dot_general(hidden, dbc.astype(bf16), (((0,), (0,)), ((), ())), preferred_element_type=f32)
        return (grad_values[None], lax.psum_scatter(product * portion, ("dp", "seq"), scatter_dimension=0, tiled=True))
    turned = kernel(unpack_body, shape(part, 4 * length, bf16), own_turned, beside, pack_turned, vmem=8)
    keep, *sends = kernel(
        weight_body, (shape(part // 4, 2 * state),) * 4, turned, dbc, from_core, from_pack, from_both,
        scratch=[pltpu.VMEM((part, 2 * state), f32)], vmem=16,
    )
    terms = [keep] + to_quad(sends)
    size = part // 4
    for bit in range(1, bits):
        size //= 2
        send, keep = kernel(bind(halve_body, bit), (shape(size, 2 * state), shape(size, 2 * state)), *terms)
        terms = [keep, swap(send, 4 << bit)]
    grad_wbc = (terms[0] + terms[1]) * portion
    return (grad_values[None], grad_wbc)


def solution(mesh):
    placed = (
        P("dp", "seq", None),
        P("dp", "seq", None),
        P("dp", "seq", None),
        P(),
        P("dp", None, "seq"),
        P("dp", "seq"),
    )
    return jax.shard_map(
        local,
        mesh=mesh,
        in_specs=placed,
        out_specs=(P("dp", "seq", None), P(("dp", "seq"), None)),
        check_vma=False,
    )
```

```python
import math

import jax
import jax.numpy as jnp
from jax import lax
from jax.experimental import pallas as pl
from jax.experimental.pallas import tpu as pltpu
from jax.sharding import PartitionSpec as P

RATES = 16
CHUNKS = 2
LANES = 128
MIB = 1024 * 1024

f32 = jnp.float32
bf16 = jnp.bfloat16
highest = lax.Precision.HIGHEST


def log_rate(index):
    return -0.0001 * jnp.exp(index.astype(f32) * (math.log(500.0) / (RATES - 1)))


def dot(lhs, rhs, over=(1, 0), precision=None):
    dims = (((over[0],), (over[1],)), ((), ()))
    return lax.dot_general(lhs, rhs, dims, precision=precision, preferred_element_type=f32)


def padded(rows):
    return -(-rows // 8) * 8


def halves_of(small):
    high = small.astype(bf16).astype(f32)
    return jnp.concatenate([high, small - high], axis=1).astype(bf16)


def spread(halves, first, count, head):
    heads = halves.shape[1] // 2
    lane = (lax.broadcasted_iota(jnp.int32, (heads, count), 1) + first) // head
    row = lax.broadcasted_iota(jnp.int32, (heads, count), 0)
    pattern = jnp.where(lane == row, 1.0, 0.0).astype(bf16)
    return dot(halves, jnp.concatenate([pattern, pattern], axis=0))


def orders(length):
    return (lax.broadcasted_iota(jnp.int32, (length, length), 0), lax.broadcasted_iota(jnp.int32, (length, length), 1))


def decay_sums(logs):
    order, other = orders(logs.shape[1])
    lower = jnp.where(other <= order, 1.0, 0.0).astype(bf16)
    high = logs.astype(bf16)
    rest = logs - high.astype(f32)
    middle = rest.astype(bf16)
    low = (rest - middle.astype(f32)).astype(bf16)
    return dot(lower, low, (1, 1)) + dot(lower, middle, (1, 1)) + dot(lower, high, (1, 1))


def segments(flags):
    order, other = orders(flags.shape[1])
    column = jnp.sum(jnp.where(other <= order, flags, 0.0), axis=1, keepdims=True)
    return column, jnp.sum(flags, axis=1, keepdims=True)


def pieces_of(array, count):
    rows = array.shape[0] // count
    return [slice(i * rows, (i + 1) * rows) for i in range(count)]


def first_body(
    place, normed_far, w_far, vals_far, cots_far, rate_far, starts_far, message, factors_out, u_out, v_out, bc_out, normed,
    groups, w_bc, vals, cots, rate, starts, small, first, second, third, fourth,
):
    heads = rate.shape[0]
    width = vals.shape[1]
    state = w_bc.shape[1] // 2
    early = [pltpu.make_async_copy(rate_far.at[0], rate, small.at[0]), pltpu.make_async_copy(starts_far, starts, small.at[1])]
    waves = []
    for source, target, sems in (
        (cots_far.at[0], cots, first), (vals_far.at[0], vals, second), (normed_far.at[0], normed, third), (w_far, w_bc, fourth),
    ):
        waves.append([
            pltpu.make_async_copy(source.at[rows], target.at[rows], sems.at[i])
            for i, rows in enumerate(pieces_of(target, sems.shape[0]))
        ])
    for copies in [early] + waves:
        for copy in copies:
            copy.start()
    for copy in early:
        copy.wait()
    logs = log_rate(rate[...])
    flags = starts[...].astype(f32)
    sums = decay_sums(logs)
    segment, last_segment = segments(flags)
    total = jnp.where(last_segment == 0.0, jnp.exp(jnp.sum(logs, axis=1, keepdims=True)), 0.0)
    total = jnp.broadcast_to(total, (heads, LANES))
    eighth = heads // 8
    for group in range(8):
        groups[group, :eighth, :] = total[group * eighth:(group + 1) * eighth]
    up = jnp.where(segment == 0.0, jnp.exp(sums), 0.0)
    down = jnp.where(segment == last_segment, jnp.exp(sums[-1:, :] - sums), 0.0)
    up, down = halves_of(up), halves_of(down)
    for copy in waves[0] + waves[1]:
        copy.wait()
    tile = width // 5
    for first in range(0, width, tile):
        lanes = slice(first, first + tile)
        u_out[:, lanes] = (spread(up, first, tile, width // heads) * cots[:, lanes].astype(f32)).astype(bf16)
        v_out[:, lanes] = (spread(down, first, tile, width // heads) * vals[:, lanes].astype(f32)).astype(bf16)
    for copy in waves[2] + waves[3]:
        copy.wait()
    bc_out[...] = dot(normed[...], w_bc[...]).astype(bf16)
    factors_out[...] = groups[...]
    half = width // 2
    end_states(place, 1, u_out, v_out, bc_out, groups, message, message, message, (0, half, 2 * half))


def end_states(place, near_set, u_ref, v_ref, bc_ref, factors, into_f, into_g, into_decays, bases):
    state = bc_ref.shape[1] // 2
    half, part, slot = u_ref.shape[1] // 2, u_ref.shape[1] // 8, factors.shape[1]
    which = lax.rem(place[0] + near_set, 2)
    columns = pl.ds(pl.multiple_of(which * half, half), half)
    quad = quad_of(place)
    forward = dot(v_ref[:, columns], bc_ref[:, :state], (0, 0))
    backward = dot(u_ref[:, columns], bc_ref[:, state:], (0, 0))
    for group in range(4):
        flip = jnp.bitwise_xor(quad, group)
        rows = slice(group * part, (group + 1) * part)
        into_f[pl.ds(pl.multiple_of(bases[0] + flip * part, part), part), :] = forward[rows]
        into_g[pl.ds(pl.multiple_of(bases[1] + flip * part, part), part), :] = backward[rows]
        into_decays[pl.ds(pl.multiple_of(bases[2] + flip * slot, slot), slot), :] = factors[which * 4 + group]


def keep_body(place, u_ref, v_ref, bc_ref, factors, keep_f, keep_g, decays):
    end_states(place, 0, u_ref, v_ref, bc_ref, factors, keep_f, keep_g, decays, (0, 0, 0))


def local_body(place, vals, cots, rate, starts, bc_ref, grad_out, scale_out, dbc_out):
    heads, length = rate.shape
    width = vals.shape[1]
    state = bc_ref.shape[1] // 2
    flags = starts[...].astype(f32)
    sums = decay_sums(log_rate(rate[...]))
    segment, last_segment = segments(flags)
    order, other = orders(length)
    later = jnp.where(other <= order, flags, 0.0)
    reach = dot(later.astype(bf16), jnp.where(order > other, 1.0, 0.0).astype(bf16))
    inside = jnp.logical_and(order >= other, reach == 0.0)
    head = width // heads
    scale = spread(halves_of(jnp.exp(sums[-1:, :] - sums)), 0, width, head)
    lifted = (spread(halves_of(jnp.exp(sums - sums[-1:, :])), 0, width, head) * cots[...].astype(f32)).astype(bf16)
    weighted = (scale * vals[...].astype(f32)).astype(bf16)
    bmat, cmat = bc_ref[:, :state], bc_ref[:, state:]
    paired = jnp.where(inside, dot(lifted, weighted, (1, 1)), 0.0).astype(bf16)
    scores = jnp.where(inside, dot(cmat, bmat, (1, 1)), 0.0).astype(bf16)
    grad_out[...] = scale * dot(scores, lifted, (0, 0))
    scale_out[...] = jnp.where(segment == last_segment, scale, 0.0)
    dbc_out[:, :state] = dot(paired, cmat, (0, 0))
    dbc_out[:, state:] = dot(paired, bmat)


def pick(flag, first, second):
    return jnp.where(flag, first, second)


def quad_of(place):
    return lax.rem(place[2], 2) * 2 + place[1]


def chip_body(start, size, head, place, keep_f, keep_g, decays, recv, *outs):
    rows = size * head
    base = keep_f.shape[0]
    slot = decays.shape[0] // 4
    second = place[0] == 1
    for flip, out in enumerate(outs):
        for k in range(size):
            at = flip * (base // 4) + (start + k) * head
            spot = flip * slot + start + k
            mine = decays[spot:spot + 1, :]
            theirs = recv[2 * base + spot:2 * base + spot + 1, :]
            kf, rf = keep_f[at:at + head, :], recv[at:at + head, :]
            kg, rg = keep_g[at:at + head, :], recv[base + at:base + at + head, :]
            to = slice(k * head, (k + 1) * head)
            out[to, :] = pick(second, 1.0, theirs) * kf + pick(second, mine, 1.0) * rf
            to = slice(rows + k * head, rows + (k + 1) * head)
            out[to, :] = pick(second, theirs, 1.0) * kg + pick(second, 1.0, mine) * rg
            out[2 * rows + k:2 * rows + k + 1, :] = mine * theirs


def parts(ref, size, head, k):
    rows = size * head
    return ref[k * head:(k + 1) * head, :], ref[rows + k * head:rows + (k + 1) * head, :], ref[2 * rows + k:2 * rows + k + 1, :]


def joined(mine, theirs, second):
    forward = pick(second, 1.0, theirs[2]) * mine[0] + pick(second, mine[2], 1.0) * theirs[0]
    backward = pick(second, theirs[2], 1.0) * mine[1] + pick(second, 1.0, mine[2]) * theirs[1]
    return forward, backward, mine[2] * theirs[2]


def entering(mine, theirs, second, before, behind):
    my_before = pick(second, theirs[2], 1.0) * before + pick(second, 1.0, 0.0) * theirs[0]
    their_before = pick(second, 1.0, mine[2]) * before + pick(second, 0.0, 1.0) * mine[0]
    my_behind = pick(second, 1.0, theirs[2]) * behind + pick(second, 0.0, 1.0) * theirs[1]
    their_behind = pick(second, mine[2], 1.0) * behind + pick(second, 1.0, 0.0) * mine[1]
    return (my_before, my_behind), (their_before, their_behind)


def level_bit(place, bit):
    return lax.rem(place[2] // (1 << bit), 2) == 1


def store_total(out, total, size, head, k, upper):
    rows = size * head
    if upper is None:
        out[k * head:(k + 1) * head, :] = total[0]
        out[rows + k * head:rows + (k + 1) * head, :] = total[1]
        out[2 * rows + k:2 * rows + k + 1, :] = total[2]
    else:
        out[k * head:(k + 1) * head, :] = pick(upper, total[1], total[0])


def quad_body(size, head, last, place, own, three, one, two, out):
    second, later = place[1] == 1, level_bit(place, 0)
    upper = None if last is None else level_bit(place, last)
    for k in range(size):
        here, beside, along, across = (parts(ref, size, head, k) for ref in (own, one, two, three))
        total = joined(joined(here, beside, second), joined(along, across, second), later)
        store_total(out, total, size, head, k, upper)


def join_body(size, head, bit, last, place, total, recv, out):
    upper = None if last is None else level_bit(place, last)
    for k in range(size):
        mine, theirs = parts(total, size, head, k), parts(recv, size, head, k)
        store_total(out, joined(mine, theirs, level_bit(place, bit)), size, head, k, upper)


def enter_body(size, head, bits, place, own, three, one, two, *refs):
    levels, final, outs = refs[:bits - 2], refs[bits - 2], refs[bits - 1:]
    rows = size * head
    second, later = place[1] == 1, level_bit(place, 0)
    for k in range(size):
        before, behind, left, right = 0.0, 0.0, 1.0, 1.0
        for bit, recv in enumerate(levels):
            high = level_bit(place, bit + 1)
            forward, backward, decay = parts(recv, size, head, k)
            before = before + pick(high, left, 0.0) * forward
            behind = behind + pick(high, 0.0, right) * backward
            left = pick(high, left * decay, left)
            right = pick(high, right, right * decay)
        high = level_bit(place, bits - 1)
        at, after = slice(k * head, (k + 1) * head), slice(rows + k * head, rows + (k + 1) * head)
        last = final[at, :]
        before = before + pick(high, left, 0.0) * last
        behind = behind + pick(high, 0.0, right) * last
        here, beside, along, across = (parts(ref, size, head, k) for ref in (own, one, two, three))
        row, other = entering(joined(here, beside, second), joined(along, across, second), later, before, behind)
        states = entering(here, beside, second, *row) + entering(along, across, second, *other)
        for out, (state_before, state_behind) in zip(outs, states):
            out[at, :] = state_before
            out[after, :] = state_behind


def core_body(chunks, head, place, *refs):
    count = 4 * len(chunks)
    keep_f, keep_g, decays, recv, send, own = refs[count:]
    base = keep_f.shape[0]
    rows = base // 4
    slot = decays.shape[0] // 4
    second = place[0] == 1
    for number, (start, size) in enumerate(chunks):
        for flip, ref in zip((0, 3, 1, 2), refs[number * 4:number * 4 + 4]):
            for k in range(size):
                at = flip * rows + (start + k) * head
                spot = flip * slot + start + k
                here = decays[spot:spot + 1, :]
                there = recv[2 * base + spot:2 * base + spot + 1, :]
                state = ref[k * head:(k + 1) * head, :]
                to, got = slice(at, at + head), recv[at:at + head, :]
                send[to, :] = pick(second, 1.0, here) * state + pick(second, 0.0, 1.0) * keep_f[to, :]
                own[to, :] = (pick(second, there, 1.0) * state + pick(second, 1.0, 0.0) * got).astype(bf16)
                state = ref[(size + k) * head:(size + k + 1) * head, :]
                to, got = slice(base + at, base + at + head), recv[base + at:base + at + head, :]
                send[to, :] = pick(second, here, 1.0) * state + pick(second, 1.0, 0.0) * keep_g[at:at + head, :]
                own[to, :] = (pick(second, 1.0, there) * state + pick(second, 0.0, 1.0) * got).astype(bf16)


def cross_body(near_set, last, place, u_ref, v_ref, so_far, states, out, after, before):
    half = after.shape[0]
    group, width = half // 4, after.shape[1]
    quad = quad_of(place)
    for flip in range(4):
        to = pl.ds(pl.multiple_of(jnp.bitwise_xor(quad, flip) * group, group), group)
        before[to, :] = states[flip * group:(flip + 1) * group, :].astype(bf16)
        after[to, :] = states[half + flip * group:half + (flip + 1) * group, :].astype(bf16)
    columns = pl.ds(pl.multiple_of(lax.rem(place[0] + near_set, 2) * half, half), half)
    for ref, weights, lanes in ((after, v_ref, slice(0, width)), (before, u_ref, slice(width, 2 * width))):
        total = so_far[:, lanes] + dot(weights[:, columns], ref[...])
        out[:, lanes] = total.astype(bf16).astype(f32) if last else total


def values_body(place, grad_ref, scale_ref, bc_ref, mine, theirs, grad_out, done):
    done[...] = jnp.zeros_like(done)
    half = mine.shape[0]
    bmat = bc_ref[:, : mine.shape[1]]
    for near_set, after in ((0, mine), (1, theirs)):
        columns = pl.ds(pl.multiple_of(lax.rem(place[0] + near_set, 2) * half, half), half)
        grad_out[:, columns] = (grad_ref[:, columns] + scale_ref[:, columns] * dot(bmat, after[...], (1, 1))).astype(bf16)


def block_row(quarter, position, levels, rows):
    quad, rest = position // (levels // 2), position % (levels // 2)
    level = 0
    for bit in range(levels.bit_length() - 2):
        level = level * 2 + rest % 2
        rest //= 2
    index = (quarter // 2) * (4 * levels) + (level * 2 + quad // 2) * 4 + quad % 2 * 2 + lax.rem(quarter, 2)
    return pl.multiple_of(index * rows, rows)


def turn_body(levels, rows, place, normed, own, beside, beyond, turned):
    turned[...] = normed[...].T.astype(f32)
    count = 2 * levels
    quarter = place[3] * 2 + place[0]
    half = count // 2 * rows
    for flip in range(4):
        out, base = ((own, 0), (beside, 0), (beyond, 0), (beyond, 3 * half))[flip]
        for position in range(count):
            start = block_row(jnp.bitwise_xor(quarter, flip), position, levels, rows)
            block = turned[pl.ds(start, rows), :]
            at = position * rows
            if flip == 0:
                out[at:at + rows, :] = block.astype(bf16)
            else:
                out[base + at:base + at + rows, :] = block[:, :LANES]
                tail = base + 2 * half + at % half
                lanes = slice(0, LANES // 2) if position < count // 2 else slice(LANES // 2, LANES)
                out[tail:tail + rows, lanes] = block[:, LANES:]


def stack_body(place, beside, beyond, out):
    rows = beside.shape[0]
    out[:rows, :] = beside[...]
    out[rows:, :] = beyond[rows:, :]


def unpack_body(place, own, beside, beyond, out):
    length = own.shape[1]
    total = own.shape[0]
    half = total // 2
    wide = 3 * half
    out[:, :length] = own[...]
    for index, (ref, base) in enumerate(((beside, 0), (beyond, 0), (beside, wide)), 1):
        left = index * length
        out[:, left:left + LANES] = ref[base:base + total, :].astype(bf16)
        out[:half, left + LANES:left + length] = ref[base + total:base + wide, :LANES // 2].astype(bf16)
        out[half:, left + LANES:left + length] = ref[base + total:base + wide, LANES // 2:].astype(bf16)


def weight_body(place, turned, own, one, two, three, *refs):
    outs, product = refs[:4], refs[4]
    length = own.shape[0]
    total = None
    for index, ref in enumerate((own, one, two, three)):
        term = dot(turned[:, index * length:(index + 1) * length], ref[...].astype(bf16))
        total = term if total is None else total + term
    product[...] = total
    rows = outs[0].shape[0]
    for flip, out in enumerate(outs):
        block = jnp.bitwise_xor(quad_of(place), flip)
        out[...] = product[pl.ds(pl.multiple_of(block * rows, rows), rows), :]


def halve_body(bit, place, *refs):
    terms, send, keep = refs[:-2], refs[-2], refs[-1]
    rows = keep.shape[0]
    here = lax.rem(place[2] // (1 << bit), 2)
    for which, out in ((1 - here, send), (here, keep)):
        at = pl.ds(pl.multiple_of(which * rows, rows), rows)
        total = terms[0][at, :]
        for term in terms[1:]:
            total = total + term[at, :]
        out[...] = total


def local(normed, values, cotangent, w_bc, rate_index, starts):
    hidden, vals, cots = normed[0], values[0], cotangent[0]
    rate = rate_index[0]
    length, width = vals.shape
    depth = hidden.shape[1]
    heads = rate.shape[0]
    head = width // heads
    state = w_bc.shape[1] // 2
    shards = lax.axis_size("seq")
    packs = lax.axis_size("dp")
    levels = shards // 4
    bits = levels.bit_length() - 1
    eighth = heads // 8
    slot = padded(eighth)
    base = width // 2

    def shape(rows, columns, dtype=f32):
        return jax.ShapeDtypeStruct((rows, columns), dtype)

    token = []

    def kernel(body, outs, *args, scratch=(), vmem=4, far=False, behind=()):
        count = len(args)
        after = list(token) + list(behind)
        single = not isinstance(outs, tuple)

        def run(*refs):
            spot = lax.axis_index("seq")
            place = (spot & 1, (spot >> 1) & 1, spot >> 2, lax.axis_index("dp") & 1)
            body(place, *refs[:count], *refs[count + len(after):])

        here = pl.BlockSpec(memory_space=pltpu.VMEM)
        there = pl.BlockSpec(memory_space=pltpu.HBM) if far else here
        if far:
            args = [pltpu.with_memory_space_constraint(array, pltpu.HBM) for array in args]
        result = pl.pallas_call(
            run,
            in_specs=[there] * count + [pl.BlockSpec(memory_space=pl.ANY)] * len(after),
            out_specs=here if single else (here,) * len(outs),
            out_shape=outs,
            scratch_shapes=list(scratch),
            compiler_params=pltpu.CompilerParams(vmem_limit_bytes=vmem * MIB),
            cost_estimate=pl.CostEstimate(flops=1000, bytes_accessed=1000, transcendentals=0),
        )(*args, *after)
        token[:] = [result if single else min(result, key=lambda array: array.size)]
        return result

    def bind(body, *constants):
        return lambda *refs: body(*constants, *refs)

    def swap(array, mask):
        return lax.ppermute(array, "seq", [(s, s ^ mask) for s in range(shards)])

    def swap_pack(array):
        return lax.ppermute(array, "dp", [(d, d ^ 1) for d in range(packs)])

    def swap_both(array):
        return lax.ppermute(array, ("dp", "seq"), [(d * shards + s, (d ^ 1) * shards + (s ^ 1)) for d in range(packs) for s in range(shards)])

    message, factors, u, v, bc, near_normed = kernel(
        first_body,
        (
            shape(2 * base + 4 * slot, state), jax.ShapeDtypeStruct((8, slot, LANES), f32),
            shape(length, width, bf16), shape(length, width, bf16), shape(length, 2 * state, bf16), shape(length, depth, bf16),
        ),
        normed, w_bc, values, cotangent, rate_index, starts,
        scratch=[
            pltpu.VMEM((8, slot, LANES), f32), pltpu.VMEM(w_bc.shape, bf16),
            pltpu.VMEM(vals.shape, bf16), pltpu.VMEM(cots.shape, bf16), pltpu.VMEM(rate.shape, jnp.int32),
            pltpu.VMEM(starts.shape, jnp.int32),
        ] + [pltpu.SemaphoreType.DMA((count,)) for count in (2, 4, 4, 4, 4)],
        vmem=24, far=True,
    )
    recv = swap(message, 1)
    keep_f, keep_g, decays = kernel(
        keep_body, (shape(base, state), shape(base, state), shape(4 * slot, state)), u, v, bc, factors, vmem=16,
    )

    direct = packs == 2 and depth % (packs * shards * 16) == 0 and length == 3 * LANES // 2
    rows = depth // (packs * shards)
    part = depth // 4
    wide = part + part // 2
    pack_turned = None
    if direct:
        own_turned, core_turned, message = kernel(
            bind(turn_body, levels, rows), (shape(part, length, bf16), shape(wide, LANES), shape(2 * wide, LANES)),
            near_normed, scratch=[pltpu.VMEM((depth, length), f32)], vmem=16,
        )
        pack_turned = swap_pack(message)

    bounds = [-(-eighth * i // CHUNKS) for i in range(CHUNKS + 1)]
    chunks = [(a, b - a) for a, b in zip(bounds, bounds[1:])]

    def parcel(size):
        return shape(2 * size * head + padded(size), state)

    def to_quad(arrays):
        across = swap(arrays[2], 6)
        return [across, swap(arrays[0], 2), swap(arrays[1], 4)]

    quads = []
    for start, size in chunks:
        waits = quads[-1][1:2] if quads else ()
        if quads:
            grad_local, scale, dbc_local = kernel(
                local_body, (shape(length, width), shape(length, width), shape(length, 2 * state)),
                vals, cots, rate, starts, bc, vmem=24,
            )
        own, *sends = kernel(bind(chip_body, start, size, head), (parcel(size),) * 4, keep_f, keep_g, decays, recv, behind=waits)
        quads.append([own] + to_quad(sends))

    totals, arrived = [], [[] for unused in chunks]
    for number, ((start, size), group) in enumerate(zip(chunks, quads)):
        last = 1 if bits == 2 else None
        out = parcel(size) if last is None else shape(size * head, state)
        totals.append(kernel(bind(quad_body, size, head, last), out, *group))
        arrived[number].append(swap(totals[number], 8))
    for bit in range(1, bits - 1):
        last = bit + 1 if bit == bits - 2 else None
        for number, (start, size) in enumerate(chunks):
            out = parcel(size) if last is None else shape(size * head, state)
            totals[number] = kernel(bind(join_body, size, head, bit, last), out, totals[number], arrived[number][-1])
            arrived[number].append(swap(totals[number], 8 << bit))
    states = []
    for number, ((start, size), group, steps) in enumerate(zip(chunks, quads, arrived)):
        waits = states[1:2] + ([pack_turned] if direct else []) if states else []
        enter, *sends = kernel(
            bind(enter_body, size, head, bits), (shape(2 * size * head, state),) * 4, *group, *steps, behind=waits,
        )
        states += [enter] + to_quad(sends)
    send, final = kernel(
        bind(core_body, chunks, head), (shape(2 * base, state), shape(2 * base, state, bf16)), *states, keep_f, keep_g, decays, recv,
    )
    core_recv = swap(send, 1)
    dbc = dbc_local
    afters = []
    for near_set, pieces in ((0, final), (1, core_recv)):
        dbc, after = kernel(
            bind(cross_body, near_set, near_set == 1), (shape(length, 2 * state), shape(base, state, bf16)),
            u, v, dbc, pieces, scratch=[pltpu.VMEM((base, state), bf16)], vmem=16,
        )
        afters.append(after)
    portion = 1.0 / (packs * shards * length)
    if direct:
        from_pack = swap_pack(dbc)
        from_core = swap(dbc, 1)
        from_both = swap(from_pack, 1)
        beside = swap(kernel(stack_body, shape(2 * wide, LANES), core_turned, pack_turned, vmem=8), 1)
    grad_values, unused_done = kernel(
        values_body, (shape(length, width, bf16), shape(8, LANES)), grad_local, scale, bc, *afters, vmem=16,
    )
    if not direct:
        product = lax.dot_general(hidden, dbc.astype(bf16), (((0,), (0,)), ((), ())), preferred_element_type=f32)
        return (grad_values[None], lax.psum_scatter(product * portion, ("dp", "seq"), scatter_dimension=0, tiled=True))
    turned = kernel(unpack_body, shape(part, 4 * length, bf16), own_turned, beside, pack_turned, vmem=8)
    keep, *sends = kernel(
        weight_body, (shape(part // 4, 2 * state),) * 4, turned, dbc, from_core, from_pack, from_both,
        scratch=[pltpu.VMEM((part, 2 * state), f32)], vmem=16,
    )
    terms = [keep] + to_quad(sends)
    size = part // 4
    for bit in range(1, bits):
        size //= 2
        send, keep = kernel(bind(halve_body, bit), (shape(size, 2 * state), shape(size, 2 * state)), *terms)
        terms = [keep, swap(send, 4 << bit)]
    grad_wbc = (terms[0] + terms[1]) * portion
    return (grad_values[None], grad_wbc)


def solution(mesh):
    placed = (
        P("dp", "seq", None),
        P("dp", "seq", None),
        P("dp", "seq", None),
        P(),
        P("dp", None, "seq"),
        P("dp", "seq"),
    )
    return jax.shard_map(
        local,
        mesh=mesh,
        in_specs=placed,
        out_specs=(P("dp", "seq", None), P(("dp", "seq"), None)),
        check_vma=False,
    )
```

```python
import math

import jax
import jax.numpy as jnp
from jax import lax
from jax.experimental import pallas as pl
from jax.experimental.pallas import tpu as pltpu
from jax.sharding import PartitionSpec as P

RATES = 16
CHUNKS = 2
LANES = 128
MIB = 1024 * 1024

f32 = jnp.float32
bf16 = jnp.bfloat16
highest = lax.Precision.HIGHEST


def log_rate(index):
    return -0.0001 * jnp.exp(index.astype(f32) * (math.log(500.0) / (RATES - 1)))


def dot(lhs, rhs, over=(1, 0), precision=None):
    dims = (((over[0],), (over[1],)), ((), ()))
    return lax.dot_general(lhs, rhs, dims, precision=precision, preferred_element_type=f32)


def padded(rows):
    return -(-rows // 8) * 8


def halves_of(small):
    high = small.astype(bf16).astype(f32)
    return jnp.concatenate([high, small - high], axis=1).astype(bf16)


def spread(halves, first, count, head):
    heads = halves.shape[1] // 2
    lane = (lax.broadcasted_iota(jnp.int32, (heads, count), 1) + first) // head
    row = lax.broadcasted_iota(jnp.int32, (heads, count), 0)
    pattern = jnp.where(lane == row, 1.0, 0.0).astype(bf16)
    return dot(halves, jnp.concatenate([pattern, pattern], axis=0))


def orders(length):
    return (lax.broadcasted_iota(jnp.int32, (length, length), 0), lax.broadcasted_iota(jnp.int32, (length, length), 1))


def decay_sums(logs):
    order, other = orders(logs.shape[1])
    lower = jnp.where(other <= order, 1.0, 0.0).astype(bf16)
    high = logs.astype(bf16)
    rest = logs - high.astype(f32)
    middle = rest.astype(bf16)
    low = (rest - middle.astype(f32)).astype(bf16)
    return dot(lower, low, (1, 1)) + dot(lower, middle, (1, 1)) + dot(lower, high, (1, 1))


def segments(flags):
    order, other = orders(flags.shape[1])
    column = jnp.sum(jnp.where(other <= order, flags, 0.0), axis=1, keepdims=True)
    return column, jnp.sum(flags, axis=1, keepdims=True)


def pieces_of(array, count):
    rows = array.shape[0] // count
    return [slice(i * rows, (i + 1) * rows) for i in range(count)]


def first_body(
    place, normed_far, w_far, vals_far, cots_far, rate_far, starts_far, message, factors_out, u_out, v_out, bc_out, normed,
    groups, w_bc, vals, cots, rate, starts, small, first, second, third, fourth,
):
    heads = rate.shape[0]
    width = vals.shape[1]
    state = w_bc.shape[1] // 2
    early = [pltpu.make_async_copy(rate_far.at[0], rate, small.at[0]), pltpu.make_async_copy(starts_far, starts, small.at[1])]
    waves = []
    for source, target, sems in (
        (normed_far.at[0], normed, first), (w_far, w_bc, second), (cots_far.at[0], cots, third), (vals_far.at[0], vals, fourth),
    ):
        waves.append([
            pltpu.make_async_copy(source.at[rows], target.at[rows], sems.at[i])
            for i, rows in enumerate(pieces_of(target, sems.shape[0]))
        ])
    for copies in [early] + waves:
        for copy in copies:
            copy.start()
    for copy in early:
        copy.wait()
    logs = log_rate(rate[...])
    flags = starts[...].astype(f32)
    sums = decay_sums(logs)
    segment, last_segment = segments(flags)
    total = jnp.where(last_segment == 0.0, jnp.exp(jnp.sum(logs, axis=1, keepdims=True)), 0.0)
    total = jnp.broadcast_to(total, (heads, LANES))
    eighth = heads // 8
    for group in range(8):
        groups[group, :eighth, :] = total[group * eighth:(group + 1) * eighth]
    up = jnp.where(segment == 0.0, jnp.exp(sums), 0.0)
    down = jnp.where(segment == last_segment, jnp.exp(sums[-1:, :] - sums), 0.0)
    up, down = halves_of(up), halves_of(down)
    for copy in waves[0] + waves[1] + waves[2] + waves[3]:
        copy.wait()
    bc_out[...] = dot(normed[...], w_bc[...]).astype(bf16)
    tile = width // 10
    for first in range(0, width, tile):
        lanes = slice(first, first + tile)
        u_out[:, lanes] = (spread(up, first, tile, width // heads) * cots[:, lanes].astype(f32)).astype(bf16)
        v_out[:, lanes] = (spread(down, first, tile, width // heads) * vals[:, lanes].astype(f32)).astype(bf16)
    factors_out[...] = groups[...]
    half = width // 2
    end_states(place, 1, u_out, v_out, bc_out, groups, message, message, message, (0, half, 2 * half))


def end_states(place, near_set, u_ref, v_ref, bc_ref, factors, into_f, into_g, into_decays, bases):
    state = bc_ref.shape[1] // 2
    half, part, slot = u_ref.shape[1] // 2, u_ref.shape[1] // 8, factors.shape[1]
    which = lax.rem(place[0] + near_set, 2)
    columns = pl.ds(pl.multiple_of(which * half, half), half)
    quad = quad_of(place)
    forward = dot(v_ref[:, columns], bc_ref[:, :state], (0, 0))
    backward = dot(u_ref[:, columns], bc_ref[:, state:], (0, 0))
    for group in range(4):
        flip = jnp.bitwise_xor(quad, group)
        rows = slice(group * part, (group + 1) * part)
        into_f[pl.ds(pl.multiple_of(bases[0] + flip * part, part), part), :] = forward[rows]
        into_g[pl.ds(pl.multiple_of(bases[1] + flip * part, part), part), :] = backward[rows]
        into_decays[pl.ds(pl.multiple_of(bases[2] + flip * slot, slot), slot), :] = factors[which * 4 + group]


def keep_body(place, u_ref, v_ref, bc_ref, factors, keep_f, keep_g, decays):
    end_states(place, 0, u_ref, v_ref, bc_ref, factors, keep_f, keep_g, decays, (0, 0, 0))


def local_body(place, vals, cots, rate, starts, bc_ref, grad_out, scale_out, dbc_out):
    heads, length = rate.shape
    width = vals.shape[1]
    state = bc_ref.shape[1] // 2
    flags = starts[...].astype(f32)
    sums = decay_sums(log_rate(rate[...]))
    segment, last_segment = segments(flags)
    order, other = orders(length)
    later = jnp.where(other <= order, flags, 0.0)
    reach = dot(later.astype(bf16), jnp.where(order > other, 1.0, 0.0).astype(bf16))
    inside = jnp.logical_and(order >= other, reach == 0.0)
    head = width // heads
    scale = spread(halves_of(jnp.exp(sums[-1:, :] - sums)), 0, width, head)
    lifted = (spread(halves_of(jnp.exp(sums - sums[-1:, :])), 0, width, head) * cots[...].astype(f32)).astype(bf16)
    weighted = (scale * vals[...].astype(f32)).astype(bf16)
    bmat, cmat = bc_ref[:, :state], bc_ref[:, state:]
    paired = jnp.where(inside, dot(lifted, weighted, (1, 1)), 0.0).astype(bf16)
    scores = jnp.where(inside, dot(cmat, bmat, (1, 1)), 0.0).astype(bf16)
    grad_out[...] = scale * dot(scores, lifted, (0, 0))
    scale_out[...] = jnp.where(segment == last_segment, scale, 0.0)
    dbc_out[:, :state] = dot(paired, cmat, (0, 0))
    dbc_out[:, state:] = dot(paired, bmat)


def pick(flag, first, second):
    return jnp.where(flag, first, second)


def quad_of(place):
    return lax.rem(place[2], 2) * 2 + place[1]


def chip_body(start, size, head, place, keep_f, keep_g, decays, recv, *outs):
    rows = size * head
    base = keep_f.shape[0]
    slot = decays.shape[0] // 4
    second = place[0] == 1
    for flip, out in enumerate(outs):
        for k in range(size):
            at = flip * (base // 4) + (start + k) * head
            spot = flip * slot + start + k
            mine = decays[spot:spot + 1, :]
            theirs = recv[2 * base + spot:2 * base + spot + 1, :]
            kf, rf = keep_f[at:at + head, :], recv[at:at + head, :]
            kg, rg = keep_g[at:at + head, :], recv[base + at:base + at + head, :]
            to = slice(k * head, (k + 1) * head)
            out[to, :] = pick(second, 1.0, theirs) * kf + pick(second, mine, 1.0) * rf
            to = slice(rows + k * head, rows + (k + 1) * head)
            out[to, :] = pick(second, theirs, 1.0) * kg + pick(second, 1.0, mine) * rg
            out[2 * rows + k:2 * rows + k + 1, :] = mine * theirs


def parts(ref, size, head, k):
    rows = size * head
    return ref[k * head:(k + 1) * head, :], ref[rows + k * head:rows + (k + 1) * head, :], ref[2 * rows + k:2 * rows + k + 1, :]


def joined(mine, theirs, second):
    forward = pick(second, 1.0, theirs[2]) * mine[0] + pick(second, mine[2], 1.0) * theirs[0]
    backward = pick(second, theirs[2], 1.0) * mine[1] + pick(second, 1.0, mine[2]) * theirs[1]
    return forward, backward, mine[2] * theirs[2]


def entering(mine, theirs, second, before, behind):
    my_before = pick(second, theirs[2], 1.0) * before + pick(second, 1.0, 0.0) * theirs[0]
    their_before = pick(second, 1.0, mine[2]) * before + pick(second, 0.0, 1.0) * mine[0]
    my_behind = pick(second, 1.0, theirs[2]) * behind + pick(second, 0.0, 1.0) * theirs[1]
    their_behind = pick(second, mine[2], 1.0) * behind + pick(second, 1.0, 0.0) * mine[1]
    return (my_before, my_behind), (their_before, their_behind)


def level_bit(place, bit):
    return lax.rem(place[2] // (1 << bit), 2) == 1


def store_total(out, total, size, head, k, upper):
    rows = size * head
    if upper is None:
        out[k * head:(k + 1) * head, :] = total[0]
        out[rows + k * head:rows + (k + 1) * head, :] = total[1]
        out[2 * rows + k:2 * rows + k + 1, :] = total[2]
    else:
        out[k * head:(k + 1) * head, :] = pick(upper, total[1], total[0])


def quad_body(size, head, last, place, own, three, one, two, out):
    second, later = place[1] == 1, level_bit(place, 0)
    upper = None if last is None else level_bit(place, last)
    for k in range(size):
        here, beside, along, across = (parts(ref, size, head, k) for ref in (own, one, two, three))
        total = joined(joined(here, beside, second), joined(along, across, second), later)
        store_total(out, total, size, head, k, upper)


def join_body(size, head, bit, last, place, total, recv, out):
    upper = None if last is None else level_bit(place, last)
    for k in range(size):
        mine, theirs = parts(total, size, head, k), parts(recv, size, head, k)
        store_total(out, joined(mine, theirs, level_bit(place, bit)), size, head, k, upper)


def enter_body(size, head, bits, place, own, three, one, two, *refs):
    levels, final, outs = refs[:bits - 2], refs[bits - 2], refs[bits - 1:]
    rows = size * head
    second, later = place[1] == 1, level_bit(place, 0)
    for k in range(size):
        before, behind, left, right = 0.0, 0.0, 1.0, 1.0
        for bit, recv in enumerate(levels):
            high = level_bit(place, bit + 1)
            forward, backward, decay = parts(recv, size, head, k)
            before = before + pick(high, left, 0.0) * forward
            behind = behind + pick(high, 0.0, right) * backward
            left = pick(high, left * decay, left)
            right = pick(high, right, right * decay)
        high = level_bit(place, bits - 1)
        at, after = slice(k * head, (k + 1) * head), slice(rows + k * head, rows + (k + 1) * head)
        last = final[at, :]
        before = before + pick(high, left, 0.0) * last
        behind = behind + pick(high, 0.0, right) * last
        here, beside, along, across = (parts(ref, size, head, k) for ref in (own, one, two, three))
        row, other = entering(joined(here, beside, second), joined(along, across, second), later, before, behind)
        states = entering(here, beside, second, *row) + entering(along, across, second, *other)
        for out, (state_before, state_behind) in zip(outs, states):
            out[at, :] = state_before
            out[after, :] = state_behind


def core_body(chunks, head, place, *refs):
    count = 4 * len(chunks)
    keep_f, keep_g, decays, recv, send, own = refs[count:]
    base = keep_f.shape[0]
    rows = base // 4
    slot = decays.shape[0] // 4
    second = place[0] == 1
    for number, (start, size) in enumerate(chunks):
        for flip, ref in zip((0, 3, 1, 2), refs[number * 4:number * 4 + 4]):
            for k in range(size):
                at = flip * rows + (start + k) * head
                spot = flip * slot + start + k
                here = decays[spot:spot + 1, :]
                there = recv[2 * base + spot:2 * base + spot + 1, :]
                state = ref[k * head:(k + 1) * head, :]
                to, got = slice(at, at + head), recv[at:at + head, :]
                send[to, :] = pick(second, 1.0, here) * state + pick(second, 0.0, 1.0) * keep_f[to, :]
                own[to, :] = (pick(second, there, 1.0) * state + pick(second, 1.0, 0.0) * got).astype(bf16)
                state = ref[(size + k) * head:(size + k + 1) * head, :]
                to, got = slice(base + at, base + at + head), recv[base + at:base + at + head, :]
                send[to, :] = pick(second, here, 1.0) * state + pick(second, 1.0, 0.0) * keep_g[at:at + head, :]
                own[to, :] = (pick(second, 1.0, there) * state + pick(second, 0.0, 1.0) * got).astype(bf16)


def cross_body(near_set, last, place, u_ref, v_ref, so_far, states, out, after, before):
    half = after.shape[0]
    group, width = half // 4, after.shape[1]
    quad = quad_of(place)
    for flip in range(4):
        to = pl.ds(pl.multiple_of(jnp.bitwise_xor(quad, flip) * group, group), group)
        before[to, :] = states[flip * group:(flip + 1) * group, :].astype(bf16)
        after[to, :] = states[half + flip * group:half + (flip + 1) * group, :].astype(bf16)
    columns = pl.ds(pl.multiple_of(lax.rem(place[0] + near_set, 2) * half, half), half)
    for ref, weights, lanes in ((after, v_ref, slice(0, width)), (before, u_ref, slice(width, 2 * width))):
        total = so_far[:, lanes] + dot(weights[:, columns], ref[...])
        out[:, lanes] = total.astype(bf16).astype(f32) if last else total


def values_body(place, grad_ref, scale_ref, bc_ref, mine, theirs, grad_out, done):
    done[...] = jnp.zeros_like(done)
    half = mine.shape[0]
    bmat = bc_ref[:, : mine.shape[1]]
    for near_set, after in ((0, mine), (1, theirs)):
        columns = pl.ds(pl.multiple_of(lax.rem(place[0] + near_set, 2) * half, half), half)
        grad_out[:, columns] = (grad_ref[:, columns] + scale_ref[:, columns] * dot(bmat, after[...], (1, 1))).astype(bf16)


def block_row(quarter, position, levels, rows):
    quad, rest = position // (levels // 2), position % (levels // 2)
    level = 0
    for bit in range(levels.bit_length() - 2):
        level = level * 2 + rest % 2
        rest //= 2
    index = (quarter // 2) * (4 * levels) + (level * 2 + quad // 2) * 4 + quad % 2 * 2 + lax.rem(quarter, 2)
    return pl.multiple_of(index * rows, rows)


def turn_body(levels, rows, place, normed, own, beside, beyond, turned):
    turned[...] = normed[...].T.astype(f32)
    count = 2 * levels
    quarter = place[3] * 2 + place[0]
    half = count // 2 * rows
    for flip in range(4):
        out, base = ((own, 0), (beside, 0), (beyond, 0), (beyond, 3 * half))[flip]
        for position in range(count):
            start = block_row(jnp.bitwise_xor(quarter, flip), position, levels, rows)
            block = turned[pl.ds(start, rows), :]
            at = position * rows
            if flip == 0:
                out[at:at + rows, :] = block.astype(bf16)
            else:
                out[base + at:base + at + rows, :] = block[:, :LANES]
                tail = base + 2 * half + at % half
                lanes = slice(0, LANES // 2) if position < count // 2 else slice(LANES // 2, LANES)
                out[tail:tail + rows, lanes] = block[:, LANES:]


def stack_body(place, beside, beyond, out):
    rows = beside.shape[0]
    out[:rows, :] = beside[...]
    out[rows:, :] = beyond[rows:, :]


def unpack_body(place, own, beside, beyond, out):
    length = own.shape[1]
    total = own.shape[0]
    half = total // 2
    wide = 3 * half
    out[:, :length] = own[...]
    for index, (ref, base) in enumerate(((beside, 0), (beyond, 0), (beside, wide)), 1):
        left = index * length
        out[:, left:left + LANES] = ref[base:base + total, :].astype(bf16)
        out[:half, left + LANES:left + length] = ref[base + total:base + wide, :LANES // 2].astype(bf16)
        out[half:, left + LANES:left + length] = ref[base + total:base + wide, LANES // 2:].astype(bf16)


def weight_body(place, turned, own, one, two, three, *refs):
    outs, product = refs[:4], refs[4]
    length = own.shape[0]
    total = None
    for index, ref in enumerate((own, one, two, three)):
        term = dot(turned[:, index * length:(index + 1) * length], ref[...].astype(bf16))
        total = term if total is None else total + term
    product[...] = total
    rows = outs[0].shape[0]
    for flip, out in enumerate(outs):
        block = jnp.bitwise_xor(quad_of(place), flip)
        out[...] = product[pl.ds(pl.multiple_of(block * rows, rows), rows), :]


def halve_body(bit, place, *refs):
    terms, send, keep = refs[:-2], refs[-2], refs[-1]
    rows = keep.shape[0]
    here = lax.rem(place[2] // (1 << bit), 2)
    for which, out in ((1 - here, send), (here, keep)):
        at = pl.ds(pl.multiple_of(which * rows, rows), rows)
        total = terms[0][at, :]
        for term in terms[1:]:
            total = total + term[at, :]
        out[...] = total


def local(normed, values, cotangent, w_bc, rate_index, starts):
    hidden, vals, cots = normed[0], values[0], cotangent[0]
    rate = rate_index[0]
    length, width = vals.shape
    depth = hidden.shape[1]
    heads = rate.shape[0]
    head = width // heads
    state = w_bc.shape[1] // 2
    shards = lax.axis_size("seq")
    packs = lax.axis_size("dp")
    levels = shards // 4
    bits = levels.bit_length() - 1
    eighth = heads // 8
    slot = padded(eighth)
    base = width // 2

    def shape(rows, columns, dtype=f32):
        return jax.ShapeDtypeStruct((rows, columns), dtype)

    token = []

    def kernel(body, outs, *args, scratch=(), vmem=4, far=False, behind=()):
        count = len(args)
        after = list(token) + list(behind)
        single = not isinstance(outs, tuple)

        def run(*refs):
            spot = lax.axis_index("seq")
            place = (spot & 1, (spot >> 1) & 1, spot >> 2, lax.axis_index("dp") & 1)
            body(place, *refs[:count], *refs[count + len(after):])

        here = pl.BlockSpec(memory_space=pltpu.VMEM)
        there = pl.BlockSpec(memory_space=pltpu.HBM) if far else here
        if far:
            args = [pltpu.with_memory_space_constraint(array, pltpu.HBM) for array in args]
        result = pl.pallas_call(
            run,
            in_specs=[there] * count + [pl.BlockSpec(memory_space=pl.ANY)] * len(after),
            out_specs=here if single else (here,) * len(outs),
            out_shape=outs,
            scratch_shapes=list(scratch),
            compiler_params=pltpu.CompilerParams(vmem_limit_bytes=vmem * MIB),
            cost_estimate=pl.CostEstimate(flops=1000, bytes_accessed=1000, transcendentals=0),
        )(*args, *after)
        token[:] = [result if single else min(result, key=lambda array: array.size)]
        return result

    def bind(body, *constants):
        return lambda *refs: body(*constants, *refs)

    def swap(array, mask):
        return lax.ppermute(array, "seq", [(s, s ^ mask) for s in range(shards)])

    def swap_pack(array):
        return lax.ppermute(array, "dp", [(d, d ^ 1) for d in range(packs)])

    def swap_both(array):
        return lax.ppermute(array, ("dp", "seq"), [(d * shards + s, (d ^ 1) * shards + (s ^ 1)) for d in range(packs) for s in range(shards)])

    message, factors, u, v, bc, near_normed = kernel(
        first_body,
        (
            shape(2 * base + 4 * slot, state), jax.ShapeDtypeStruct((8, slot, LANES), f32),
            shape(length, width, bf16), shape(length, width, bf16), shape(length, 2 * state, bf16), shape(length, depth, bf16),
        ),
        normed, w_bc, values, cotangent, rate_index, starts,
        scratch=[
            pltpu.VMEM((8, slot, LANES), f32), pltpu.VMEM(w_bc.shape, bf16),
            pltpu.VMEM(vals.shape, bf16), pltpu.VMEM(cots.shape, bf16), pltpu.VMEM(rate.shape, jnp.int32),
            pltpu.VMEM(starts.shape, jnp.int32),
        ] + [pltpu.SemaphoreType.DMA((count,)) for count in (2, 6, 8, 6, 6)],
        vmem=24, far=True,
    )
    recv = swap(message, 1)
    keep_f, keep_g, decays = kernel(
        keep_body, (shape(base, state), shape(base, state), shape(4 * slot, state)), u, v, bc, factors, vmem=16,
    )

    direct = packs == 2 and depth % (packs * shards * 16) == 0 and length == 3 * LANES // 2
    rows = depth // (packs * shards)
    part = depth // 4
    wide = part + part // 2
    pack_turned = None
    if direct:
        own_turned, core_turned, message = kernel(
            bind(turn_body, levels, rows), (shape(part, length, bf16), shape(wide, LANES), shape(2 * wide, LANES)),
            near_normed, scratch=[pltpu.VMEM((depth, length), f32)], vmem=16,
        )
        pack_turned = swap_pack(message)

    bounds = [-(-eighth * i // CHUNKS) for i in range(CHUNKS + 1)]
    chunks = [(a, b - a) for a, b in zip(bounds, bounds[1:])]

    def parcel(size):
        return shape(2 * size * head + padded(size), state)

    def to_quad(arrays):
        across = swap(arrays[2], 6)
        return [across, swap(arrays[0], 2), swap(arrays[1], 4)]

    quads = []
    for start, size in chunks:
        waits = quads[-1][1:2] if quads else ()
        if quads:
            grad_local, scale, dbc_local = kernel(
                local_body, (shape(length, width), shape(length, width), shape(length, 2 * state)),
                vals, cots, rate, starts, bc, vmem=24,
            )
        own, *sends = kernel(bind(chip_body, start, size, head), (parcel(size),) * 4, keep_f, keep_g, decays, recv, behind=waits)
        quads.append([own] + to_quad(sends))

    totals, arrived = [], [[] for unused in chunks]
    for number, ((start, size), group) in enumerate(zip(chunks, quads)):
        last = 1 if bits == 2 else None
        out = parcel(size) if last is None else shape(size * head, state)
        totals.append(kernel(bind(quad_body, size, head, last), out, *group))
        arrived[number].append(swap(totals[number], 8))
    for bit in range(1, bits - 1):
        last = bit + 1 if bit == bits - 2 else None
        for number, (start, size) in enumerate(chunks):
            out = parcel(size) if last is None else shape(size * head, state)
            totals[number] = kernel(bind(join_body, size, head, bit, last), out, totals[number], arrived[number][-1])
            arrived[number].append(swap(totals[number], 8 << bit))
    states = []
    for number, ((start, size), group, steps) in enumerate(zip(chunks, quads, arrived)):
        waits = states[1:2] + ([pack_turned] if direct else []) if states else []
        enter, *sends = kernel(
            bind(enter_body, size, head, bits), (shape(2 * size * head, state),) * 4, *group, *steps, behind=waits,
        )
        states += [enter] + to_quad(sends)
    send, final = kernel(
        bind(core_body, chunks, head), (shape(2 * base, state), shape(2 * base, state, bf16)), *states, keep_f, keep_g, decays, recv,
    )
    core_recv = swap(send, 1)
    dbc = dbc_local
    afters = []
    for near_set, pieces in ((0, final), (1, core_recv)):
        dbc, after = kernel(
            bind(cross_body, near_set, near_set == 1), (shape(length, 2 * state), shape(base, state, bf16)),
            u, v, dbc, pieces, scratch=[pltpu.VMEM((base, state), bf16)], vmem=16,
        )
        afters.append(after)
    portion = 1.0 / (packs * shards * length)
    if direct:
        from_pack = swap_pack(dbc)
        from_core = swap(dbc, 1)
        from_both = swap(from_pack, 1)
        beside = swap(kernel(stack_body, shape(2 * wide, LANES), core_turned, pack_turned, vmem=8), 1)
    grad_values, unused_done = kernel(
        values_body, (shape(length, width, bf16), shape(8, LANES)), grad_local, scale, bc, *afters, vmem=16,
    )
    if not direct:
        product = lax.dot_general(hidden, dbc.astype(bf16), (((0,), (0,)), ((), ())), preferred_element_type=f32)
        return (grad_values[None], lax.psum_scatter(product * portion, ("dp", "seq"), scatter_dimension=0, tiled=True))
    turned = kernel(unpack_body, shape(part, 4 * length, bf16), own_turned, beside, pack_turned, vmem=8)
    keep, *sends = kernel(
        weight_body, (shape(part // 4, 2 * state),) * 4, turned, dbc, from_core, from_pack, from_both,
        scratch=[pltpu.VMEM((part, 2 * state), f32)], vmem=16,
    )
    terms = [keep] + to_quad(sends)
    size = part // 4
    for bit in range(1, bits):
        size //= 2
        send, keep = kernel(bind(halve_body, bit), (shape(size, 2 * state), shape(size, 2 * state)), *terms)
        terms = [keep, swap(send, 4 << bit)]
    grad_wbc = (terms[0] + terms[1]) * portion
    return (grad_values[None], grad_wbc)


def solution(mesh):
    placed = (
        P("dp", "seq", None),
        P("dp", "seq", None),
        P("dp", "seq", None),
        P(),
        P("dp", None, "seq"),
        P("dp", "seq"),
    )
    return jax.shard_map(
        local,
        mesh=mesh,
        in_specs=placed,
        out_specs=(P("dp", "seq", None), P(("dp", "seq"), None)),
        check_vma=False,
    )
```

```python
import math

import jax
import jax.numpy as jnp
from jax import lax
from jax.experimental import pallas as pl
from jax.experimental.pallas import tpu as pltpu
from jax.sharding import PartitionSpec as P

RATES = 16
CHUNKS = 2
LANES = 128
MIB = 1024 * 1024

f32 = jnp.float32
bf16 = jnp.bfloat16
highest = lax.Precision.HIGHEST


def log_rate(index):
    return -0.0001 * jnp.exp(index.astype(f32) * (math.log(500.0) / (RATES - 1)))


def dot(lhs, rhs, over=(1, 0), precision=None):
    dims = (((over[0],), (over[1],)), ((), ()))
    return lax.dot_general(lhs, rhs, dims, precision=precision, preferred_element_type=f32)


def padded(rows):
    return -(-rows // 8) * 8


def halves_of(small):
    high = small.astype(bf16).astype(f32)
    return jnp.concatenate([high, small - high], axis=1).astype(bf16)


def spread(halves, first, count, head):
    heads = halves.shape[1] // 2
    lane = (lax.broadcasted_iota(jnp.int32, (heads, count), 1) + first) // head
    row = lax.broadcasted_iota(jnp.int32, (heads, count), 0)
    pattern = jnp.where(lane == row, 1.0, 0.0).astype(bf16)
    return dot(halves, jnp.concatenate([pattern, pattern], axis=0))


def orders(length):
    return (lax.broadcasted_iota(jnp.int32, (length, length), 0), lax.broadcasted_iota(jnp.int32, (length, length), 1))


def decay_sums(logs):
    order, other = orders(logs.shape[1])
    lower = jnp.where(other <= order, 1.0, 0.0).astype(bf16)
    high = logs.astype(bf16)
    rest = logs - high.astype(f32)
    middle = rest.astype(bf16)
    low = (rest - middle.astype(f32)).astype(bf16)
    return dot(lower, low, (1, 1)) + dot(lower, middle, (1, 1)) + dot(lower, high, (1, 1))


def segments(flags):
    order, other = orders(flags.shape[1])
    column = jnp.sum(jnp.where(other <= order, flags, 0.0), axis=1, keepdims=True)
    return column, jnp.sum(flags, axis=1, keepdims=True)


def pieces_of(array, count):
    rows = array.shape[0] // count
    return [slice(i * rows, (i + 1) * rows) for i in range(count)]


def first_body(
    place, normed_far, w_far, vals_far, cots_far, rate_far, starts_far, message, factors_out, u_out, v_out, bc_out, normed,
    groups, w_bc, vals, cots, rate, starts, small, first, second, third, fourth,
):
    heads = rate.shape[0]
    width = vals.shape[1]
    state = w_bc.shape[1] // 2
    early = [pltpu.make_async_copy(rate_far.at[0], rate, small.at[0]), pltpu.make_async_copy(starts_far, starts, small.at[1])]
    waves = []
    for source, target, sems in (
        (normed_far.at[0], normed, first), (w_far, w_bc, second), (cots_far.at[0], cots, third), (vals_far.at[0], vals, fourth),
    ):
        waves.append([
            pltpu.make_async_copy(source.at[rows], target.at[rows], sems.at[i])
            for i, rows in enumerate(pieces_of(target, sems.shape[0]))
        ])
    for copies in [early] + waves:
        for copy in copies:
            copy.start()
    for copy in early:
        copy.wait()
    logs = log_rate(rate[...])
    flags = starts[...].astype(f32)
    sums = decay_sums(logs)
    segment, last_segment = segments(flags)
    total = jnp.where(last_segment == 0.0, jnp.exp(jnp.sum(logs, axis=1, keepdims=True)), 0.0)
    total = jnp.broadcast_to(total, (heads, LANES))
    eighth = heads // 8
    for group in range(8):
        groups[group, :eighth, :] = total[group * eighth:(group + 1) * eighth]
    up = jnp.where(segment == 0.0, jnp.exp(sums), 0.0)
    down = jnp.where(segment == last_segment, jnp.exp(sums[-1:, :] - sums), 0.0)
    up, down = halves_of(up), halves_of(down)
    for copy in waves[0] + waves[1] + waves[2] + waves[3]:
        copy.wait()
    bc_out[...] = dot(normed[...], w_bc[...]).astype(bf16)
    tile = width // 5
    for first in range(0, width, tile):
        lanes = slice(first, first + tile)
        u_out[:, lanes] = (spread(up, first, tile, width // heads) * cots[:, lanes].astype(f32)).astype(bf16)
        v_out[:, lanes] = (spread(down, first, tile, width // heads) * vals[:, lanes].astype(f32)).astype(bf16)
    factors_out[...] = groups[...]
    half = width // 2
    end_states(place, 1, u_out, v_out, bc_out, groups, message, message, message, (0, half, 2 * half))


def end_states(place, near_set, u_ref, v_ref, bc_ref, factors, into_f, into_g, into_decays, bases):
    state = bc_ref.shape[1] // 2
    half, part, slot = u_ref.shape[1] // 2, u_ref.shape[1] // 8, factors.shape[1]
    which = lax.rem(place[0] + near_set, 2)
    columns = pl.ds(pl.multiple_of(which * half, half), half)
    quad = quad_of(place)
    forward = dot(v_ref[:, columns], bc_ref[:, :state], (0, 0))
    backward = dot(u_ref[:, columns], bc_ref[:, state:], (0, 0))
    for group in range(4):
        flip = jnp.bitwise_xor(quad, group)
        rows = slice(group * part, (group + 1) * part)
        into_f[pl.ds(pl.multiple_of(bases[0] + flip * part, part), part), :] = forward[rows]
        into_g[pl.ds(pl.multiple_of(bases[1] + flip * part, part), part), :] = backward[rows]
        into_decays[pl.ds(pl.multiple_of(bases[2] + flip * slot, slot), slot), :] = factors[which * 4 + group]


def keep_body(place, u_ref, v_ref, bc_ref, factors, keep_f, keep_g, decays):
    end_states(place, 0, u_ref, v_ref, bc_ref, factors, keep_f, keep_g, decays, (0, 0, 0))


def local_body(place, vals, cots, rate, starts, bc_ref, grad_out, scale_out, dbc_out):
    heads, length = rate.shape
    width = vals.shape[1]
    state = bc_ref.shape[1] // 2
    flags = starts[...].astype(f32)
    sums = decay_sums(log_rate(rate[...]))
    segment, last_segment = segments(flags)
    order, other = orders(length)
    later = jnp.where(other <= order, flags, 0.0)
    reach = dot(later.astype(bf16), jnp.where(order > other, 1.0, 0.0).astype(bf16))
    inside = jnp.logical_and(order >= other, reach == 0.0)
    head = width // heads
    scale = spread(halves_of(jnp.exp(sums[-1:, :] - sums)), 0, width, head)
    lifted = (spread(halves_of(jnp.exp(sums - sums[-1:, :])), 0, width, head) * cots[...].astype(f32)).astype(bf16)
    weighted = (scale * vals[...].astype(f32)).astype(bf16)
    bmat, cmat = bc_ref[:, :state], bc_ref[:, state:]
    paired = jnp.where(inside, dot(lifted, weighted, (1, 1)), 0.0).astype(bf16)
    scores = jnp.where(inside, dot(cmat, bmat, (1, 1)), 0.0).astype(bf16)
    grad_out[...] = scale * dot(scores, lifted, (0, 0))
    scale_out[...] = jnp.where(segment == last_segment, scale, 0.0)
    dbc_out[:, :state] = dot(paired, cmat, (0, 0))
    dbc_out[:, state:] = dot(paired, bmat)


def pick(flag, first, second):
    return jnp.where(flag, first, second)


def quad_of(place):
    return lax.rem(place[2], 2) * 2 + place[1]


def chip_body(start, size, head, place, keep_f, keep_g, decays, recv, *outs):
    rows = size * head
    base = keep_f.shape[0]
    slot = decays.shape[0] // 4
    second = place[0] == 1
    for flip, out in enumerate(outs):
        for k in range(size):
            at = flip * (base // 4) + (start + k) * head
            spot = flip * slot + start + k
            mine = decays[spot:spot + 1, :]
            theirs = recv[2 * base + spot:2 * base + spot + 1, :]
            kf, rf = keep_f[at:at + head, :], recv[at:at + head, :]
            kg, rg = keep_g[at:at + head, :], recv[base + at:base + at + head, :]
            to = slice(k * head, (k + 1) * head)
            out[to, :] = pick(second, 1.0, theirs) * kf + pick(second, mine, 1.0) * rf
            to = slice(rows + k * head, rows + (k + 1) * head)
            out[to, :] = pick(second, theirs, 1.0) * kg + pick(second, 1.0, mine) * rg
            out[2 * rows + k:2 * rows + k + 1, :] = mine * theirs


def parts(ref, size, head, k):
    rows = size * head
    return ref[k * head:(k + 1) * head, :], ref[rows + k * head:rows + (k + 1) * head, :], ref[2 * rows + k:2 * rows + k + 1, :]


def joined(mine, theirs, second):
    forward = pick(second, 1.0, theirs[2]) * mine[0] + pick(second, mine[2], 1.0) * theirs[0]
    backward = pick(second, theirs[2], 1.0) * mine[1] + pick(second, 1.0, mine[2]) * theirs[1]
    return forward, backward, mine[2] * theirs[2]


def entering(mine, theirs, second, before, behind):
    my_before = pick(second, theirs[2], 1.0) * before + pick(second, 1.0, 0.0) * theirs[0]
    their_before = pick(second, 1.0, mine[2]) * before + pick(second, 0.0, 1.0) * mine[0]
    my_behind = pick(second, 1.0, theirs[2]) * behind + pick(second, 0.0, 1.0) * theirs[1]
    their_behind = pick(second, mine[2], 1.0) * behind + pick(second, 1.0, 0.0) * mine[1]
    return (my_before, my_behind), (their_before, their_behind)


def level_bit(place, bit):
    return lax.rem(place[2] // (1 << bit), 2) == 1


def store_total(out, total, size, head, k, upper):
    rows = size * head
    if upper is None:
        out[k * head:(k + 1) * head, :] = total[0]
        out[rows + k * head:rows + (k + 1) * head, :] = total[1]
        out[2 * rows + k:2 * rows + k + 1, :] = total[2]
    else:
        out[k * head:(k + 1) * head, :] = pick(upper, total[1], total[0])


def quad_body(size, head, last, place, own, three, one, two, out):
    second, later = place[1] == 1, level_bit(place, 0)
    upper = None if last is None else level_bit(place, last)
    for k in range(size):
        here, beside, along, across = (parts(ref, size, head, k) for ref in (own, one, two, three))
        total = joined(joined(here, beside, second), joined(along, across, second), later)
        store_total(out, total, size, head, k, upper)


def join_body(size, head, bit, last, place, total, recv, out):
    upper = None if last is None else level_bit(place, last)
    for k in range(size):
        mine, theirs = parts(total, size, head, k), parts(recv, size, head, k)
        store_total(out, joined(mine, theirs, level_bit(place, bit)), size, head, k, upper)


def enter_body(size, head, bits, place, own, three, one, two, *refs):
    levels, final, outs = refs[:bits - 2], refs[bits - 2], refs[bits - 1:]
    rows = size * head
    second, later = place[1] == 1, level_bit(place, 0)
    for k in range(size):
        before, behind, left, right = 0.0, 0.0, 1.0, 1.0
        for bit, recv in enumerate(levels):
            high = level_bit(place, bit + 1)
            forward, backward, decay = parts(recv, size, head, k)
            before = before + pick(high, left, 0.0) * forward
            behind = behind + pick(high, 0.0, right) * backward
            left = pick(high, left * decay, left)
            right = pick(high, right, right * decay)
        high = level_bit(place, bits - 1)
        at, after = slice(k * head, (k + 1) * head), slice(rows + k * head, rows + (k + 1) * head)
        last = final[at, :]
        before = before + pick(high, left, 0.0) * last
        behind = behind + pick(high, 0.0, right) * last
        here, beside, along, across = (parts(ref, size, head, k) for ref in (own, one, two, three))
        row, other = entering(joined(here, beside, second), joined(along, across, second), later, before, behind)
        states = entering(here, beside, second, *row) + entering(along, across, second, *other)
        for out, (state_before, state_behind) in zip(outs, states):
            out[at, :] = state_before
            out[after, :] = state_behind


def core_body(chunks, head, place, *refs):
    count = 4 * len(chunks)
    keep_f, keep_g, decays, recv, send, own = refs[count:]
    base = keep_f.shape[0]
    rows = base // 4
    slot = decays.shape[0] // 4
    second = place[0] == 1
    for number, (start, size) in enumerate(chunks):
        for flip, ref in zip((0, 3, 1, 2), refs[number * 4:number * 4 + 4]):
            for k in range(size):
                at = flip * rows + (start + k) * head
                spot = flip * slot + start + k
                here = decays[spot:spot + 1, :]
                there = recv[2 * base + spot:2 * base + spot + 1, :]
                state = ref[k * head:(k + 1) * head, :]
                to, got = slice(at, at + head), recv[at:at + head, :]
                send[to, :] = pick(second, 1.0, here) * state + pick(second, 0.0, 1.0) * keep_f[to, :]
                own[to, :] = (pick(second, there, 1.0) * state + pick(second, 1.0, 0.0) * got).astype(bf16)
                state = ref[(size + k) * head:(size + k + 1) * head, :]
                to, got = slice(base + at, base + at + head), recv[base + at:base + at + head, :]
                send[to, :] = pick(second, here, 1.0) * state + pick(second, 1.0, 0.0) * keep_g[at:at + head, :]
                own[to, :] = (pick(second, 1.0, there) * state + pick(second, 0.0, 1.0) * got).astype(bf16)


def cross_body(near_set, last, place, u_ref, v_ref, so_far, states, out, after, before):
    half = after.shape[0]
    group, width = half // 4, after.shape[1]
    quad = quad_of(place)
    for flip in range(4):
        to = pl.ds(pl.multiple_of(jnp.bitwise_xor(quad, flip) * group, group), group)
        before[to, :] = states[flip * group:(flip + 1) * group, :].astype(bf16)
        after[to, :] = states[half + flip * group:half + (flip + 1) * group, :].astype(bf16)
    columns = pl.ds(pl.multiple_of(lax.rem(place[0] + near_set, 2) * half, half), half)
    for ref, weights, lanes in ((after, v_ref, slice(0, width)), (before, u_ref, slice(width, 2 * width))):
        total = so_far[:, lanes] + dot(weights[:, columns], ref[...])
        out[:, lanes] = total.astype(bf16).astype(f32) if last else total


def values_body(place, grad_ref, scale_ref, bc_ref, mine, theirs, grad_out, done):
    done[...] = jnp.zeros_like(done)
    half = mine.shape[0]
    bmat = bc_ref[:, : mine.shape[1]]
    for near_set, after in ((0, mine), (1, theirs)):
        columns = pl.ds(pl.multiple_of(lax.rem(place[0] + near_set, 2) * half, half), half)
        grad_out[:, columns] = (grad_ref[:, columns] + scale_ref[:, columns] * dot(bmat, after[...], (1, 1))).astype(bf16)


def block_row(quarter, position, levels, rows):
    quad, rest = position // (levels // 2), position % (levels // 2)
    level = 0
    for bit in range(levels.bit_length() - 2):
        level = level * 2 + rest % 2
        rest //= 2
    index = (quarter // 2) * (4 * levels) + (level * 2 + quad // 2) * 4 + quad % 2 * 2 + lax.rem(quarter, 2)
    return pl.multiple_of(index * rows, rows)


def turn_body(levels, rows, place, normed, own, beside, beyond, turned):
    turned[...] = normed[...].T.astype(f32)
    count = 2 * levels
    quarter = place[3] * 2 + place[0]
    half = count // 2 * rows
    for flip in range(4):
        out, base = ((own, 0), (beside, 0), (beyond, 0), (beyond, 3 * half))[flip]
        for position in range(count):
            start = block_row(jnp.bitwise_xor(quarter, flip), position, levels, rows)
            block = turned[pl.ds(start, rows), :]
            at = position * rows
            if flip == 0:
                out[at:at + rows, :] = block.astype(bf16)
            else:
                out[base + at:base + at + rows, :] = block[:, :LANES]
                tail = base + 2 * half + at % half
                lanes = slice(0, LANES // 2) if position < count // 2 else slice(LANES // 2, LANES)
                out[tail:tail + rows, lanes] = block[:, LANES:]


def stack_body(place, beside, beyond, out):
    rows = beside.shape[0]
    out[:rows, :] = beside[...]
    out[rows:, :] = beyond[rows:, :]


def unpack_body(place, own, beside, beyond, out):
    length = own.shape[1]
    total = own.shape[0]
    half = total // 2
    wide = 3 * half
    out[:, :length] = own[...]
    for index, (ref, base) in enumerate(((beside, 0), (beyond, 0), (beside, wide)), 1):
        left = index * length
        out[:, left:left + LANES] = ref[base:base + total, :].astype(bf16)
        out[:half, left + LANES:left + length] = ref[base + total:base + wide, :LANES // 2].astype(bf16)
        out[half:, left + LANES:left + length] = ref[base + total:base + wide, LANES // 2:].astype(bf16)


def weight_body(place, turned, own, one, two, three, *refs):
    outs, product = refs[:4], refs[4]
    length = own.shape[0]
    total = None
    for index, ref in enumerate((own, one, two, three)):
        term = dot(turned[:, index * length:(index + 1) * length], ref[...].astype(bf16))
        total = term if total is None else total + term
    product[...] = total
    rows = outs[0].shape[0]
    for flip, out in enumerate(outs):
        block = jnp.bitwise_xor(quad_of(place), flip)
        out[...] = product[pl.ds(pl.multiple_of(block * rows, rows), rows), :]


def halve_body(bit, place, *refs):
    terms, send, keep = refs[:-2], refs[-2], refs[-1]
    rows = keep.shape[0]
    here = lax.rem(place[2] // (1 << bit), 2)
    for which, out in ((1 - here, send), (here, keep)):
        at = pl.ds(pl.multiple_of(which * rows, rows), rows)
        total = terms[0][at, :]
        for term in terms[1:]:
            total = total + term[at, :]
        out[...] = total


def local(normed, values, cotangent, w_bc, rate_index, starts):
    hidden, vals, cots = normed[0], values[0], cotangent[0]
    rate = rate_index[0]
    length, width = vals.shape
    depth = hidden.shape[1]
    heads = rate.shape[0]
    head = width // heads
    state = w_bc.shape[1] // 2
    shards = lax.axis_size("seq")
    packs = lax.axis_size("dp")
    levels = shards // 4
    bits = levels.bit_length() - 1
    eighth = heads // 8
    slot = padded(eighth)
    base = width // 2

    def shape(rows, columns, dtype=f32):
        return jax.ShapeDtypeStruct((rows, columns), dtype)

    token = []

    def kernel(body, outs, *args, scratch=(), vmem=4, far=False, behind=()):
        count = len(args)
        after = list(token) + list(behind)
        single = not isinstance(outs, tuple)

        def run(*refs):
            spot = lax.axis_index("seq")
            place = (spot & 1, (spot >> 1) & 1, spot >> 2, lax.axis_index("dp") & 1)
            body(place, *refs[:count], *refs[count + len(after):])

        here = pl.BlockSpec(memory_space=pltpu.VMEM)
        there = pl.BlockSpec(memory_space=pltpu.HBM) if far else here
        if far:
            args = [pltpu.with_memory_space_constraint(array, pltpu.HBM) for array in args]
        result = pl.pallas_call(
            run,
            in_specs=[there] * count + [pl.BlockSpec(memory_space=pl.ANY)] * len(after),
            out_specs=here if single else (here,) * len(outs),
            out_shape=outs,
            scratch_shapes=list(scratch),
            compiler_params=pltpu.CompilerParams(vmem_limit_bytes=vmem * MIB),
            cost_estimate=pl.CostEstimate(flops=1000, bytes_accessed=1000, transcendentals=0),
        )(*args, *after)
        token[:] = [result if single else min(result, key=lambda array: array.size)]
        return result

    def bind(body, *constants):
        return lambda *refs: body(*constants, *refs)

    def swap(array, mask):
        return lax.ppermute(array, "seq", [(s, s ^ mask) for s in range(shards)])

    def swap_pack(array):
        return lax.ppermute(array, "dp", [(d, d ^ 1) for d in range(packs)])

    def swap_both(array):
        return lax.ppermute(array, ("dp", "seq"), [(d * shards + s, (d ^ 1) * shards + (s ^ 1)) for d in range(packs) for s in range(shards)])

    message, factors, u, v, bc, near_normed = kernel(
        first_body,
        (
            shape(2 * base + 4 * slot, state), jax.ShapeDtypeStruct((8, slot, LANES), f32),
            shape(length, width, bf16), shape(length, width, bf16), shape(length, 2 * state, bf16), shape(length, depth, bf16),
        ),
        normed, w_bc, values, cotangent, rate_index, starts,
        scratch=[
            pltpu.VMEM((8, slot, LANES), f32), pltpu.VMEM(w_bc.shape, bf16),
            pltpu.VMEM(vals.shape, bf16), pltpu.VMEM(cots.shape, bf16), pltpu.VMEM(rate.shape, jnp.int32),
            pltpu.VMEM(starts.shape, jnp.int32),
        ] + [pltpu.SemaphoreType.DMA((count,)) for count in (2, 2, 2, 2, 2)],
        vmem=24, far=True,
    )
    recv = swap(message, 1)
    keep_f, keep_g, decays = kernel(
        keep_body, (shape(base, state), shape(base, state), shape(4 * slot, state)), u, v, bc, factors, vmem=16,
    )

    direct = packs == 2 and depth % (packs * shards * 16) == 0 and length == 3 * LANES // 2
    rows = depth // (packs * shards)
    part = depth // 4
    wide = part + part // 2
    pack_turned = None
    if direct:
        own_turned, core_turned, message = kernel(
            bind(turn_body, levels, rows), (shape(part, length, bf16), shape(wide, LANES), shape(2 * wide, LANES)),
            near_normed, scratch=[pltpu.VMEM((depth, length), f32)], vmem=16,
        )
        pack_turned = swap_pack(message)

    bounds = [-(-eighth * i // CHUNKS) for i in range(CHUNKS + 1)]
    chunks = [(a, b - a) for a, b in zip(bounds, bounds[1:])]

    def parcel(size):
        return shape(2 * size * head + padded(size), state)

    def to_quad(arrays):
        across = swap(arrays[2], 6)
        return [across, swap(arrays[0], 2), swap(arrays[1], 4)]

    quads = []
    for start, size in chunks:
        waits = quads[-1][1:2] if quads else ()
        if quads:
            grad_local, scale, dbc_local = kernel(
                local_body, (shape(length, width), shape(length, width), shape(length, 2 * state)),
                vals, cots, rate, starts, bc, vmem=24,
            )
        own, *sends = kernel(bind(chip_body, start, size, head), (parcel(size),) * 4, keep_f, keep_g, decays, recv, behind=waits)
        quads.append([own] + to_quad(sends))

    totals, arrived = [], [[] for unused in chunks]
    for number, ((start, size), group) in enumerate(zip(chunks, quads)):
        last = 1 if bits == 2 else None
        out = parcel(size) if last is None else shape(size * head, state)
        totals.append(kernel(bind(quad_body, size, head, last), out, *group))
        arrived[number].append(swap(totals[number], 8))
    for bit in range(1, bits - 1):
        last = bit + 1 if bit == bits - 2 else None
        for number, (start, size) in enumerate(chunks):
            out = parcel(size) if last is None else shape(size * head, state)
            totals[number] = kernel(bind(join_body, size, head, bit, last), out, totals[number], arrived[number][-1])
            arrived[number].append(swap(totals[number], 8 << bit))
    states = []
    for number, ((start, size), group, steps) in enumerate(zip(chunks, quads, arrived)):
        waits = states[1:2] + ([pack_turned] if direct else []) if states else []
        enter, *sends = kernel(
            bind(enter_body, size, head, bits), (shape(2 * size * head, state),) * 4, *group, *steps, behind=waits,
        )
        states += [enter] + to_quad(sends)
    send, final = kernel(
        bind(core_body, chunks, head), (shape(2 * base, state), shape(2 * base, state, bf16)), *states, keep_f, keep_g, decays, recv,
    )
    core_recv = swap(send, 1)
    dbc = dbc_local
    afters = []
    for near_set, pieces in ((0, final), (1, core_recv)):
        dbc, after = kernel(
            bind(cross_body, near_set, near_set == 1), (shape(length, 2 * state), shape(base, state, bf16)),
            u, v, dbc, pieces, scratch=[pltpu.VMEM((base, state), bf16)], vmem=16,
        )
        afters.append(after)
    portion = 1.0 / (packs * shards * length)
    if direct:
        from_pack = swap_pack(dbc)
        from_core = swap(dbc, 1)
        from_both = swap(from_pack, 1)
        beside = swap(kernel(stack_body, shape(2 * wide, LANES), core_turned, pack_turned, vmem=8), 1)
    grad_values, unused_done = kernel(
        values_body, (shape(length, width, bf16), shape(8, LANES)), grad_local, scale, bc, *afters, vmem=16,
    )
    if not direct:
        product = lax.dot_general(hidden, dbc.astype(bf16), (((0,), (0,)), ((), ())), preferred_element_type=f32)
        return (grad_values[None], lax.psum_scatter(product * portion, ("dp", "seq"), scatter_dimension=0, tiled=True))
    turned = kernel(unpack_body, shape(part, 4 * length, bf16), own_turned, beside, pack_turned, vmem=8)
    keep, *sends = kernel(
        weight_body, (shape(part // 4, 2 * state),) * 4, turned, dbc, from_core, from_pack, from_both,
        scratch=[pltpu.VMEM((part, 2 * state), f32)], vmem=16,
    )
    terms = [keep] + to_quad(sends)
    size = part // 4
    for bit in range(1, bits):
        size //= 2
        send, keep = kernel(bind(halve_body, bit), (shape(size, 2 * state), shape(size, 2 * state)), *terms)
        terms = [keep, swap(send, 4 << bit)]
    grad_wbc = (terms[0] + terms[1]) * portion
    return (grad_values[None], grad_wbc)


def solution(mesh):
    placed = (
        P("dp", "seq", None),
        P("dp", "seq", None),
        P("dp", "seq", None),
        P(),
        P("dp", None, "seq"),
        P("dp", "seq"),
    )
    return jax.shard_map(
        local,
        mesh=mesh,
        in_specs=placed,
        out_specs=(P("dp", "seq", None), P(("dp", "seq"), None)),
        check_vma=False,
    )
```

```python
import math

import jax
import jax.numpy as jnp
from jax import lax
from jax.experimental import pallas as pl
from jax.experimental.pallas import tpu as pltpu
from jax.sharding import PartitionSpec as P

RATES = 16
CHUNKS = 2
LANES = 128
MIB = 1024 * 1024

f32 = jnp.float32
bf16 = jnp.bfloat16
highest = lax.Precision.HIGHEST


def log_rate(index):
    return -0.0001 * jnp.exp(index.astype(f32) * (math.log(500.0) / (RATES - 1)))


def dot(lhs, rhs, over=(1, 0), precision=None):
    dims = (((over[0],), (over[1],)), ((), ()))
    return lax.dot_general(lhs, rhs, dims, precision=precision, preferred_element_type=f32)


def padded(rows):
    return -(-rows // 8) * 8


def halves_of(small):
    high = small.astype(bf16).astype(f32)
    return jnp.concatenate([high, small - high], axis=1).astype(bf16)


def spread(halves, first, count, head):
    heads = halves.shape[1] // 2
    lane = (lax.broadcasted_iota(jnp.int32, (heads, count), 1) + first) // head
    row = lax.broadcasted_iota(jnp.int32, (heads, count), 0)
    pattern = jnp.where(lane == row, 1.0, 0.0).astype(bf16)
    return dot(halves, jnp.concatenate([pattern, pattern], axis=0))


def orders(length):
    return (lax.broadcasted_iota(jnp.int32, (length, length), 0), lax.broadcasted_iota(jnp.int32, (length, length), 1))


def decay_sums(logs):
    order, other = orders(logs.shape[1])
    lower = jnp.where(other <= order, 1.0, 0.0).astype(bf16)
    high = logs.astype(bf16)
    rest = logs - high.astype(f32)
    middle = rest.astype(bf16)
    low = (rest - middle.astype(f32)).astype(bf16)
    return dot(lower, low, (1, 1)) + dot(lower, middle, (1, 1)) + dot(lower, high, (1, 1))


def segments(flags):
    order, other = orders(flags.shape[1])
    column = jnp.sum(jnp.where(other <= order, flags, 0.0), axis=1, keepdims=True)
    return column, jnp.sum(flags, axis=1, keepdims=True)


def pieces_of(array, count):
    rows = array.shape[0] // count
    return [slice(i * rows, (i + 1) * rows) for i in range(count)]


def first_body(
    place, normed_far, w_far, vals_far, cots_far, rate_far, starts_far, message, factors_out, u_out, v_out, bc_out, normed,
    groups, w_bc, vals, cots, rate, starts, small, first, second, third, fourth,
):
    heads = rate.shape[0]
    width = vals.shape[1]
    state = w_bc.shape[1] // 2
    early = [pltpu.make_async_copy(rate_far.at[0], rate, small.at[0]), pltpu.make_async_copy(starts_far, starts, small.at[1])]
    waves = []
    for source, target, sems in (
        (normed_far.at[0], normed, first), (w_far, w_bc, second), (cots_far.at[0], cots, third), (vals_far.at[0], vals, fourth),
    ):
        waves.append([
            pltpu.make_async_copy(source.at[rows], target.at[rows], sems.at[i])
            for i, rows in enumerate(pieces_of(target, sems.shape[0]))
        ])
    for copies in [early] + waves:
        for copy in copies:
            copy.start()
    for copy in early:
        copy.wait()
    logs = log_rate(rate[...])
    flags = starts[...].astype(f32)
    sums = decay_sums(logs)
    segment, last_segment = segments(flags)
    total = jnp.where(last_segment == 0.0, jnp.exp(jnp.sum(logs, axis=1, keepdims=True)), 0.0)
    total = jnp.broadcast_to(total, (heads, LANES))
    eighth = heads // 8
    for group in range(8):
        groups[group, :eighth, :] = total[group * eighth:(group + 1) * eighth]
    up = jnp.where(segment == 0.0, jnp.exp(sums), 0.0)
    down = jnp.where(segment == last_segment, jnp.exp(sums[-1:, :] - sums), 0.0)
    up, down = halves_of(up), halves_of(down)
    for copy in waves[0] + waves[1] + waves[2] + waves[3]:
        copy.wait()
    bc_out[...] = dot(normed[...], w_bc[...]).astype(bf16)
    tile = width // 5
    for first in range(0, width, tile):
        lanes = slice(first, first + tile)
        u_out[:, lanes] = (spread(up, first, tile, width // heads) * cots[:, lanes].astype(f32)).astype(bf16)
        v_out[:, lanes] = (spread(down, first, tile, width // heads) * vals[:, lanes].astype(f32)).astype(bf16)
    factors_out[...] = groups[...]
    half = width // 2
    end_states(place, 1, u_out, v_out, bc_out, groups, message, message, message, (0, half, 2 * half))


def end_states(place, near_set, u_ref, v_ref, bc_ref, factors, into_f, into_g, into_decays, bases):
    state = bc_ref.shape[1] // 2
    half, part, slot = u_ref.shape[1] // 2, u_ref.shape[1] // 8, factors.shape[1]
    which = lax.rem(place[0] + near_set, 2)
    columns = pl.ds(pl.multiple_of(which * half, half), half)
    quad = quad_of(place)
    forward = dot(v_ref[:, columns], bc_ref[:, :state], (0, 0))
    backward = dot(u_ref[:, columns], bc_ref[:, state:], (0, 0))
    for group in range(4):
        flip = jnp.bitwise_xor(quad, group)
        rows = slice(group * part, (group + 1) * part)
        into_f[pl.ds(pl.multiple_of(bases[0] + flip * part, part), part), :] = forward[rows]
        into_g[pl.ds(pl.multiple_of(bases[1] + flip * part, part), part), :] = backward[rows]
        into_decays[pl.ds(pl.multiple_of(bases[2] + flip * slot, slot), slot), :] = factors[which * 4 + group]


def keep_body(place, u_ref, v_ref, bc_ref, factors, keep_f, keep_g, decays):
    end_states(place, 0, u_ref, v_ref, bc_ref, factors, keep_f, keep_g, decays, (0, 0, 0))


def local_body(place, vals, cots, rate, starts, bc_ref, grad_out, scale_out, dbc_out):
    heads, length = rate.shape
    width = vals.shape[1]
    state = bc_ref.shape[1] // 2
    flags = starts[...].astype(f32)
    sums = decay_sums(log_rate(rate[...]))
    segment, last_segment = segments(flags)
    order, other = orders(length)
    later = jnp.where(other <= order, flags, 0.0)
    reach = dot(later.astype(bf16), jnp.where(order > other, 1.0, 0.0).astype(bf16))
    inside = jnp.logical_and(order >= other, reach == 0.0)
    head = width // heads
    scale = spread(halves_of(jnp.exp(sums[-1:, :] - sums)), 0, width, head)
    lifted = (spread(halves_of(jnp.exp(sums - sums[-1:, :])), 0, width, head) * cots[...].astype(f32)).astype(bf16)
    weighted = (scale * vals[...].astype(f32)).astype(bf16)
    bmat, cmat = bc_ref[:, :state], bc_ref[:, state:]
    paired = jnp.where(inside, dot(lifted, weighted, (1, 1)), 0.0).astype(bf16)
    scores = jnp.where(inside, dot(cmat, bmat, (1, 1)), 0.0).astype(bf16)
    grad_out[...] = scale * dot(scores, lifted, (0, 0))
    scale_out[...] = jnp.where(segment == last_segment, scale, 0.0)
    dbc_out[:, :state] = dot(paired, cmat, (0, 0))
    dbc_out[:, state:] = dot(paired, bmat)


def pick(flag, first, second):
    return jnp.where(flag, first, second)


def quad_of(place):
    return lax.rem(place[2], 2) * 2 + place[1]


def chip_body(start, size, head, place, keep_f, keep_g, decays, recv, *outs):
    rows = size * head
    base = keep_f.shape[0]
    slot = decays.shape[0] // 4
    second = place[0] == 1
    for flip, out in enumerate(outs):
        for k in range(size):
            at = flip * (base // 4) + (start + k) * head
            spot = flip * slot + start + k
            mine = decays[spot:spot + 1, :]
            theirs = recv[2 * base + spot:2 * base + spot + 1, :]
            kf, rf = keep_f[at:at + head, :], recv[at:at + head, :]
            kg, rg = keep_g[at:at + head, :], recv[base + at:base + at + head, :]
            to = slice(k * head, (k + 1) * head)
            out[to, :] = pick(second, 1.0, theirs) * kf + pick(second, mine, 1.0) * rf
            to = slice(rows + k * head, rows + (k + 1) * head)
            out[to, :] = pick(second, theirs, 1.0) * kg + pick(second, 1.0, mine) * rg
            out[2 * rows + k:2 * rows + k + 1, :] = mine * theirs


def parts(ref, size, head, k):
    rows = size * head
    return ref[k * head:(k + 1) * head, :], ref[rows + k * head:rows + (k + 1) * head, :], ref[2 * rows + k:2 * rows + k + 1, :]


def joined(mine, theirs, second):
    forward = pick(second, 1.0, theirs[2]) * mine[0] + pick(second, mine[2], 1.0) * theirs[0]
    backward = pick(second, theirs[2], 1.0) * mine[1] + pick(second, 1.0, mine[2]) * theirs[1]
    return forward, backward, mine[2] * theirs[2]


def entering(mine, theirs, second, before, behind):
    my_before = pick(second, theirs[2], 1.0) * before + pick(second, 1.0, 0.0) * theirs[0]
    their_before = pick(second, 1.0, mine[2]) * before + pick(second, 0.0, 1.0) * mine[0]
    my_behind = pick(second, 1.0, theirs[2]) * behind + pick(second, 0.0, 1.0) * theirs[1]
    their_behind = pick(second, mine[2], 1.0) * behind + pick(second, 1.0, 0.0) * mine[1]
    return (my_before, my_behind), (their_before, their_behind)


def level_bit(place, bit):
    return lax.rem(place[2] // (1 << bit), 2) == 1


def store_total(out, total, size, head, k, upper):
    rows = size * head
    if upper is None:
        out[k * head:(k + 1) * head, :] = total[0]
        out[rows + k * head:rows + (k + 1) * head, :] = total[1]
        out[2 * rows + k:2 * rows + k + 1, :] = total[2]
    else:
        out[k * head:(k + 1) * head, :] = pick(upper, total[1], total[0])


def quad_body(size, head, last, place, own, three, one, two, out):
    second, later = place[1] == 1, level_bit(place, 0)
    upper = None if last is None else level_bit(place, last)
    for k in range(size):
        here, beside, along, across = (parts(ref, size, head, k) for ref in (own, one, two, three))
        total = joined(joined(here, beside, second), joined(along, across, second), later)
        store_total(out, total, size, head, k, upper)


def join_body(size, head, bit, last, place, total, recv, out):
    upper = None if last is None else level_bit(place, last)
    for k in range(size):
        mine, theirs = parts(total, size, head, k), parts(recv, size, head, k)
        store_total(out, joined(mine, theirs, level_bit(place, bit)), size, head, k, upper)


def enter_body(size, head, bits, place, own, three, one, two, *refs):
    levels, final, outs = refs[:bits - 2], refs[bits - 2], refs[bits - 1:]
    rows = size * head
    second, later = place[1] == 1, level_bit(place, 0)
    for k in range(size):
        before, behind, left, right = 0.0, 0.0, 1.0, 1.0
        for bit, recv in enumerate(levels):
            high = level_bit(place, bit + 1)
            forward, backward, decay = parts(recv, size, head, k)
            before = before + pick(high, left, 0.0) * forward
            behind = behind + pick(high, 0.0, right) * backward
            left = pick(high, left * decay, left)
            right = pick(high, right, right * decay)
        high = level_bit(place, bits - 1)
        at, after = slice(k * head, (k + 1) * head), slice(rows + k * head, rows + (k + 1) * head)
        last = final[at, :]
        before = before + pick(high, left, 0.0) * last
        behind = behind + pick(high, 0.0, right) * last
        here, beside, along, across = (parts(ref, size, head, k) for ref in (own, one, two, three))
        row, other = entering(joined(here, beside, second), joined(along, across, second), later, before, behind)
        states = entering(here, beside, second, *row) + entering(along, across, second, *other)
        for out, (state_before, state_behind) in zip(outs, states):
            out[at, :] = state_before
            out[after, :] = state_behind


def core_body(chunks, head, place, *refs):
    count = 4 * len(chunks)
    keep_f, keep_g, decays, recv, send, own = refs[count:]
    base = keep_f.shape[0]
    rows = base // 4
    slot = decays.shape[0] // 4
    second = place[0] == 1
    for number, (start, size) in enumerate(chunks):
        for flip, ref in zip((0, 3, 1, 2), refs[number * 4:number * 4 + 4]):
            for k in range(size):
                at = flip * rows + (start + k) * head
                spot = flip * slot + start + k
                here = decays[spot:spot + 1, :]
                there = recv[2 * base + spot:2 * base + spot + 1, :]
                state = ref[k * head:(k + 1) * head, :]
                to, got = slice(at, at + head), recv[at:at + head, :]
                send[to, :] = pick(second, 1.0, here) * state + pick(second, 0.0, 1.0) * keep_f[to, :]
                own[to, :] = (pick(second, there, 1.0) * state + pick(second, 1.0, 0.0) * got).astype(bf16)
                state = ref[(size + k) * head:(size + k + 1) * head, :]
                to, got = slice(base + at, base + at + head), recv[base + at:base + at + head, :]
                send[to, :] = pick(second, here, 1.0) * state + pick(second, 1.0, 0.0) * keep_g[at:at + head, :]
                own[to, :] = (pick(second, 1.0, there) * state + pick(second, 0.0, 1.0) * got).astype(bf16)


def cross_body(near_set, last, place, u_ref, v_ref, so_far, states, out, after, before):
    half = after.shape[0]
    group, width = half // 4, after.shape[1]
    quad = quad_of(place)
    for flip in range(4):
        to = pl.ds(pl.multiple_of(jnp.bitwise_xor(quad, flip) * group, group), group)
        before[to, :] = states[flip * group:(flip + 1) * group, :].astype(bf16)
        after[to, :] = states[half + flip * group:half + (flip + 1) * group, :].astype(bf16)
    columns = pl.ds(pl.multiple_of(lax.rem(place[0] + near_set, 2) * half, half), half)
    for ref, weights, lanes in ((after, v_ref, slice(0, width)), (before, u_ref, slice(width, 2 * width))):
        total = so_far[:, lanes] + dot(weights[:, columns], ref[...])
        out[:, lanes] = total.astype(bf16).astype(f32) if last else total


def values_body(place, grad_ref, scale_ref, bc_ref, mine, theirs, grad_out, done):
    done[...] = jnp.zeros_like(done)
    half = mine.shape[0]
    bmat = bc_ref[:, : mine.shape[1]]
    for near_set, after in ((0, mine), (1, theirs)):
        columns = pl.ds(pl.multiple_of(lax.rem(place[0] + near_set, 2) * half, half), half)
        grad_out[:, columns] = (grad_ref[:, columns] + scale_ref[:, columns] * dot(bmat, after[...], (1, 1))).astype(bf16)


def block_row(quarter, position, levels, rows):
    quad, rest = position // (levels // 2), position % (levels // 2)
    level = 0
    for bit in range(levels.bit_length() - 2):
        level = level * 2 + rest % 2
        rest //= 2
    index = (quarter // 2) * (4 * levels) + (level * 2 + quad // 2) * 4 + quad % 2 * 2 + lax.rem(quarter, 2)
    return pl.multiple_of(index * rows, rows)


def turn_body(levels, rows, place, normed, own, beside, beyond, turned):
    turned[...] = normed[...].T.astype(f32)
    count = 2 * levels
    quarter = place[3] * 2 + place[0]
    half = count // 2 * rows
    for flip in range(4):
        out, base = ((own, 0), (beside, 0), (beyond, 0), (beyond, 3 * half))[flip]
        for position in range(count):
            start = block_row(jnp.bitwise_xor(quarter, flip), position, levels, rows)
            block = turned[pl.ds(start, rows), :]
            at = position * rows
            if flip == 0:
                out[at:at + rows, :] = block.astype(bf16)
            else:
                out[base + at:base + at + rows, :] = block[:, :LANES]
                tail = base + 2 * half + at % half
                lanes = slice(0, LANES // 2) if position < count // 2 else slice(LANES // 2, LANES)
                out[tail:tail + rows, lanes] = block[:, LANES:]


def stack_body(place, beside, beyond, out):
    rows = beside.shape[0]
    out[:rows, :] = beside[...]
    out[rows:, :] = beyond[rows:, :]


def unpack_body(place, own, beside, beyond, out):
    length = own.shape[1]
    total = own.shape[0]
    half = total // 2
    wide = 3 * half
    out[:, :length] = own[...]
    for index, (ref, base) in enumerate(((beside, 0), (beyond, 0), (beside, wide)), 1):
        left = index * length
        out[:, left:left + LANES] = ref[base:base + total, :].astype(bf16)
        out[:half, left + LANES:left + length] = ref[base + total:base + wide, :LANES // 2].astype(bf16)
        out[half:, left + LANES:left + length] = ref[base + total:base + wide, LANES // 2:].astype(bf16)


def weight_body(place, turned, own, one, two, three, *refs):
    outs, product = refs[:4], refs[4]
    length = own.shape[0]
    total = None
    for index, ref in enumerate((own, one, two, three)):
        term = dot(turned[:, index * length:(index + 1) * length], ref[...].astype(bf16))
        total = term if total is None else total + term
    product[...] = total
    rows = outs[0].shape[0]
    for flip, out in enumerate(outs):
        block = jnp.bitwise_xor(quad_of(place), flip)
        out[...] = product[pl.ds(pl.multiple_of(block * rows, rows), rows), :]


def halve_body(bit, place, *refs):
    terms, send, keep = refs[:-2], refs[-2], refs[-1]
    rows = keep.shape[0]
    here = lax.rem(place[2] // (1 << bit), 2)
    for which, out in ((1 - here, send), (here, keep)):
        at = pl.ds(pl.multiple_of(which * rows, rows), rows)
        total = terms[0][at, :]
        for term in terms[1:]:
            total = total + term[at, :]
        out[...] = total


def local(normed, values, cotangent, w_bc, rate_index, starts):
    hidden, vals, cots = normed[0], values[0], cotangent[0]
    rate = rate_index[0]
    length, width = vals.shape
    depth = hidden.shape[1]
    heads = rate.shape[0]
    head = width // heads
    state = w_bc.shape[1] // 2
    shards = lax.axis_size("seq")
    packs = lax.axis_size("dp")
    levels = shards // 4
    bits = levels.bit_length() - 1
    eighth = heads // 8
    slot = padded(eighth)
    base = width // 2

    def shape(rows, columns, dtype=f32):
        return jax.ShapeDtypeStruct((rows, columns), dtype)

    token = []

    def kernel(body, outs, *args, scratch=(), vmem=4, far=False, behind=()):
        count = len(args)
        after = list(token) + list(behind)
        single = not isinstance(outs, tuple)

        def run(*refs):
            spot = lax.axis_index("seq")
            place = (spot & 1, (spot >> 1) & 1, spot >> 2, lax.axis_index("dp") & 1)
            body(place, *refs[:count], *refs[count + len(after):])

        here = pl.BlockSpec(memory_space=pltpu.VMEM)
        there = pl.BlockSpec(memory_space=pltpu.HBM) if far else here
        if far:
            args = [pltpu.with_memory_space_constraint(array, pltpu.HBM) for array in args]
        result = pl.pallas_call(
            run,
            in_specs=[there] * count + [pl.BlockSpec(memory_space=pl.ANY)] * len(after),
            out_specs=here if single else (here,) * len(outs),
            out_shape=outs,
            scratch_shapes=list(scratch),
            compiler_params=pltpu.CompilerParams(vmem_limit_bytes=vmem * MIB),
            cost_estimate=pl.CostEstimate(flops=1000, bytes_accessed=1000, transcendentals=0),
        )(*args, *after)
        token[:] = [result if single else min(result, key=lambda array: array.size)]
        return result

    def bind(body, *constants):
        return lambda *refs: body(*constants, *refs)

    def swap(array, mask):
        return lax.ppermute(array, "seq", [(s, s ^ mask) for s in range(shards)])

    def swap_pack(array):
        return lax.ppermute(array, "dp", [(d, d ^ 1) for d in range(packs)])

    def swap_both(array):
        return lax.ppermute(array, ("dp", "seq"), [(d * shards + s, (d ^ 1) * shards + (s ^ 1)) for d in range(packs) for s in range(shards)])

    message, factors, u, v, bc, near_normed = kernel(
        first_body,
        (
            shape(2 * base + 4 * slot, state), jax.ShapeDtypeStruct((8, slot, LANES), f32),
            shape(length, width, bf16), shape(length, width, bf16), shape(length, 2 * state, bf16), shape(length, depth, bf16),
        ),
        normed, w_bc, values, cotangent, rate_index, starts,
        scratch=[
            pltpu.VMEM((8, slot, LANES), f32), pltpu.VMEM(w_bc.shape, bf16),
            pltpu.VMEM(vals.shape, bf16), pltpu.VMEM(cots.shape, bf16), pltpu.VMEM(rate.shape, jnp.int32),
            pltpu.VMEM(starts.shape, jnp.int32),
        ] + [pltpu.SemaphoreType.DMA((count,)) for count in (2, 2, 2, 2, 2)],
        vmem=24, far=True,
    )
    recv = swap(message, 1)
    keep_f, keep_g, decays = kernel(
        keep_body, (shape(base, state), shape(base, state), shape(4 * slot, state)), u, v, bc, factors, vmem=16,
    )

    direct = packs == 2 and depth % (packs * shards * 16) == 0 and length == 3 * LANES // 2
    rows = depth // (packs * shards)
    part = depth // 4
    wide = part + part // 2
    pack_turned = None
    if direct:
        own_turned, core_turned, message = kernel(
            bind(turn_body, levels, rows), (shape(part, length, bf16), shape(wide, LANES), shape(2 * wide, LANES)),
            near_normed, scratch=[pltpu.VMEM((depth, length), f32)], vmem=16,
        )
        pack_turned = swap_pack(message)

    bounds = [-(-eighth * i // CHUNKS) for i in range(CHUNKS + 1)]
    chunks = [(a, b - a) for a, b in zip(bounds, bounds[1:])]

    def parcel(size):
        return shape(2 * size * head + padded(size), state)

    def to_quad(arrays):
        across = swap(arrays[2], 6)
        return [across, swap(arrays[0], 2), swap(arrays[1], 4)]

    quads = []
    for start, size in chunks:
        waits = quads[-1][1:3] if quads else ()
        if quads:
            grad_local, scale, dbc_local = kernel(
                local_body, (shape(length, width), shape(length, width), shape(length, 2 * state)),
                vals, cots, rate, starts, bc, vmem=24,
            )
        own, *sends = kernel(bind(chip_body, start, size, head), (parcel(size),) * 4, keep_f, keep_g, decays, recv, behind=waits)
        quads.append([own] + to_quad(sends))

    totals, arrived = [], [[] for unused in chunks]
    for number, ((start, size), group) in enumerate(zip(chunks, quads)):
        last = 1 if bits == 2 else None
        out = parcel(size) if last is None else shape(size * head, state)
        totals.append(kernel(bind(quad_body, size, head, last), out, *group))
        arrived[number].append(swap(totals[number], 8))
    for bit in range(1, bits - 1):
        last = bit + 1 if bit == bits - 2 else None
        for number, (start, size) in enumerate(chunks):
            out = parcel(size) if last is None else shape(size * head, state)
            totals[number] = kernel(bind(join_body, size, head, bit, last), out, totals[number], arrived[number][-1])
            arrived[number].append(swap(totals[number], 8 << bit))
    states = []
    for number, ((start, size), group, steps) in enumerate(zip(chunks, quads, arrived)):
        waits = states[1:2] + ([pack_turned] if direct else []) if states else []
        enter, *sends = kernel(
            bind(enter_body, size, head, bits), (shape(2 * size * head, state),) * 4, *group, *steps, behind=waits,
        )
        states += [enter] + to_quad(sends)
    send, final = kernel(
        bind(core_body, chunks, head), (shape(2 * base, state), shape(2 * base, state, bf16)), *states, keep_f, keep_g, decays, recv,
    )
    core_recv = swap(send, 1)
    dbc = dbc_local
    afters = []
    for near_set, pieces in ((0, final), (1, core_recv)):
        dbc, after = kernel(
            bind(cross_body, near_set, near_set == 1), (shape(length, 2 * state), shape(base, state, bf16)),
            u, v, dbc, pieces, scratch=[pltpu.VMEM((base, state), bf16)], vmem=16,
        )
        afters.append(after)
    portion = 1.0 / (packs * shards * length)
    if direct:
        from_pack = swap_pack(dbc)
        from_core = swap(dbc, 1)
        from_both = swap(from_pack, 1)
        beside = swap(kernel(stack_body, shape(2 * wide, LANES), core_turned, pack_turned, vmem=8), 1)
    grad_values, unused_done = kernel(
        values_body, (shape(length, width, bf16), shape(8, LANES)), grad_local, scale, bc, *afters, vmem=16,
    )
    if not direct:
        product = lax.dot_general(hidden, dbc.astype(bf16), (((0,), (0,)), ((), ())), preferred_element_type=f32)
        return (grad_values[None], lax.psum_scatter(product * portion, ("dp", "seq"), scatter_dimension=0, tiled=True))
    turned = kernel(unpack_body, shape(part, 4 * length, bf16), own_turned, beside, pack_turned, vmem=8)
    keep, *sends = kernel(
        weight_body, (shape(part // 4, 2 * state),) * 4, turned, dbc, from_core, from_pack, from_both,
        scratch=[pltpu.VMEM((part, 2 * state), f32)], vmem=16,
    )
    terms = [keep] + to_quad(sends)
    size = part // 4
    for bit in range(1, bits):
        size //= 2
        send, keep = kernel(bind(halve_body, bit), (shape(size, 2 * state), shape(size, 2 * state)), *terms)
        terms = [keep, swap(send, 4 << bit)]
    grad_wbc = (terms[0] + terms[1]) * portion
    return (grad_values[None], grad_wbc)


def solution(mesh):
    placed = (
        P("dp", "seq", None),
        P("dp", "seq", None),
        P("dp", "seq", None),
        P(),
        P("dp", None, "seq"),
        P("dp", "seq"),
    )
    return jax.shard_map(
        local,
        mesh=mesh,
        in_specs=placed,
        out_specs=(P("dp", "seq", None), P(("dp", "seq"), None)),
        check_vma=False,
    )
```
